512 devices in a mesh: member: 16 (over y, x_hi), tile: 32 (over x_lo, z, core).
Axes of the slice: x: 4 (x_hi: 2, x_lo: 2; x = x_hi * 2 + x_lo), y: 8, z: 8, core: 2. Of those that a mesh axis runs over, the one named last changes fastest.
Arguments:
- predictor_inputs: bfloat16 [16, 64, 32, 4096], P('member', None, None, 'tile'), may hold values from -6 to 6
- target: float32 [16, 32, 4096], P(None, None, 'tile'), may hold values from -6 to 6
- depth_one: float32 [64, 9], replicated, may hold values from -2 to 2
- point_one: bfloat16 [64, 64], replicated, may hold values from -0.75 to 0.75
- bias_one: float32 [64], replicated, may hold values from -3 to 3
- depth_two: float32 [64, 9], replicated, may hold values from -2 to 2
- point_two: bfloat16 [16, 64], replicated, may hold values from -0.75 to 0.75
- bias_two: float32 [16], replicated, may hold values from -3 to 3
Outputs:
- corrected_realizations: bfloat16 [16, 16, 32, 4096], P('member', None, None, 'tile')
- grad_depth_one: float32 [64, 9], replicated
- grad_point_one: float32 [64, 64], replicated
- grad_bias_one: float32 [64], replicated
- grad_depth_two: float32 [64, 9], replicated
- grad_point_two: float32 [16, 64], replicated
- grad_bias_two: float32 [16], replicated
The draws below stay inside these ranges and needn't reach their ends.
All inputs are finite; a program needn't handle non-finite values.
Results may differ from the reference program's by a relative error of at most 0.0042.
The reference program's roundings to bfloat16 on the way count: a program that leaves them out, or rounds other values in their place, can miss the bound.
Values may be sent and summed in bfloat16 or wider, within the bound.
No kernel may reach another device: no remote copies, remote signals or barrier semaphores. Data moves between devices by JAX's collectives and lax.ppermute only.
A program may use at most 64 MiB of HBM per device.

```python
import jax
import jax.numpy as jnp
from jax import lax

CIN = 64
HID = 64
COUT = 16
LAT = 32
LON = 4096
MEMBERS = 16


def draw_predictor_inputs(key, part):
    key = jax.random.fold_in(key, 11)
    key_common = jax.random.fold_in(key, 1)
    key_offset = jax.random.fold_in(key, 2)
    key_noise = jax.random.fold_in(key, 3)
    common = jax.random.normal(key_common, (1, CIN, LAT, LON), jnp.float32)
    offset = 0.35 * jax.random.normal(key_offset, (MEMBERS, CIN, 1, 1), jnp.float32)
    noise = 0.1 * jax.random.normal(key_noise, (MEMBERS, CIN, LAT, LON), jnp.float32)
    return jnp.clip(common + offset + noise, -6.0, 6.0).astype(jnp.bfloat16)


def steps_of(key, shape, split, least, largest):
    gain = 1.0
    for position, blocks in split:
        steps = jax.random.uniform(jax.random.fold_in(jax.random.fold_in(key, 6), position), (blocks,), jnp.float32, least / len(split), largest / len(split))
        gain = gain * jnp.repeat(jnp.exp(steps), shape[position] // blocks).reshape((-1,) + (1,) * (len(shape) - 1 - position))
    return gain


def centred(own_key, extent, deviation, bound, shards=(), held_as=jnp.bfloat16):
    factor_of = steps_of(own_key, extent, shards, -0.22, 0.18) if shards else 1.0
    array = jax.random.normal(own_key, extent, jnp.float32) * deviation * factor_of
    return jnp.minimum(jnp.maximum(array, -bound), bound).astype(held_as)


def setup_inputs(seed: int = 0) -> dict:
    key_of = jax.random.split(jax.random.key(seed), 9)
    predictor_inputs = draw_predictor_inputs(jax.random.fold_in(key_of[8], 71), 0)
    target = centred(key_of[1], (COUT, LAT, LON), 1.0, 6.0, ((2, 32),), jnp.float32)
    depth_one = centred(key_of[2], (CIN, 9), 9 ** -0.5, 2.0, (), jnp.float32)
    point_one = centred(key_of[3], (HID, CIN), CIN ** -0.5, 0.75)
    bias_one = centred(key_of[4], (HID,), 0.5, 3.0, (), jnp.float32)
    depth_two = centred(key_of[5], (HID, 9), 9 ** -0.5, 2.0, (), jnp.float32)
    point_two = centred(key_of[6], (COUT, HID), HID ** -0.5, 0.75)
    bias_two = centred(key_of[7], (COUT,), 0.5, 3.0, (), jnp.float32)
    return dict(predictor_inputs=predictor_inputs, target=target, depth_one=depth_one, point_one=point_one, bias_one=bias_one, depth_two=depth_two, point_two=point_two, bias_two=bias_two)


smooth_width = 0.25
pair_weight = 0.95

def pad_poles(field):
    return jnp.pad(field, ((0, 0), (1, 1), (0, 0)))

def wrap_lon(field):
    return jnp.concatenate([field[:, :, -1:], field, field[:, :, :1]], axis=2)

def depthwise(padded, kernel, rows, cols):
    total = jnp.zeros((padded.shape[0], rows, cols), jnp.float32)
    for row_off in range(3):
        for col_off in range(3):
            tap = kernel[:, 3 * row_off + col_off].astype(jnp.float32)[:, None, None]
            total = total + tap * padded[:, row_off:row_off + rows, col_off:col_off + cols].astype(jnp.float32)
    return total

def depthwise_back(padded, kernel, rows, cols):
    total = jnp.zeros((padded.shape[0], rows, cols), jnp.float32)
    for row_off in range(3):
        for col_off in range(3):
            tap = kernel[:, 3 * row_off + col_off].astype(jnp.float32)[:, None, None]
            total = total + tap * padded[:, 2 - row_off:2 - row_off + rows, 2 - col_off:2 - col_off + cols].astype(jnp.float32)
    return total

def kernel_grad(cotan, padded, rows, cols):
    cotan_f = cotan.astype(jnp.float32)
    columns = []
    for row_off in range(3):
        for col_off in range(3):
            window = padded[:, row_off:row_off + rows, col_off:col_off + cols].astype(jnp.float32)
            columns.append(lax.optimization_barrier(jnp.sum(cotan_f * window, axis=(1, 2))))
    return jnp.stack(columns, axis=1)

def logistic_derivative(diff):
    return diff / jnp.sqrt(diff * diff + smooth_width * smooth_width)

def contract(left, right, dims):
    return lax.dot_general(left, right, ((dims[0], dims[1]), ((), ())), preferred_element_type=jnp.float32)

def reference(predictor_inputs, target, depth_one, point_one, bias_one, depth_two, point_two, bias_two):

    def evaluate_postprocessor(activation_field):
        padded_in = pad_poles(wrap_lon(activation_field))
        first_bf = depthwise(padded_in, depth_one, LAT, LON).astype(jnp.bfloat16)
        pre_act = (jnp.dot(point_one, first_bf.reshape(CIN, -1), preferred_element_type=jnp.float32) + bias_one[:, None]).reshape(HID, LAT, LON)
        hidden_bf = jax.nn.silu(pre_act).astype(jnp.bfloat16)
        hidden_pad = pad_poles(wrap_lon(hidden_bf))
        second_bf = depthwise(hidden_pad, depth_two, LAT, LON).astype(jnp.bfloat16)
        second_flat = second_bf.reshape(HID, -1)
        out = (jnp.dot(point_two, second_flat, preferred_element_type=jnp.float32) + bias_two[:, None]).astype(jnp.bfloat16).reshape(COUT, LAT, LON)
        return (padded_in, first_bf, pre_act, hidden_pad, second_flat, out)
    predicted_realizations = lax.map(lambda activation_field: evaluate_postprocessor(activation_field)[5], predictor_inputs)

    def result_cotangent_vector(own_bf):
        current_realization = own_bf.astype(jnp.float32)

        def step(realization_number, accumulated_amount):
            return accumulated_amount + logistic_derivative(current_realization - predicted_realizations[realization_number].astype(jnp.float32))
        pair_sum = lax.fori_loop(0, MEMBERS, step, jnp.zeros(current_realization.shape, jnp.float32))
        value = (logistic_derivative(current_realization - target) - pair_weight / (MEMBERS - 1) * pair_sum) / (LAT * LON)
        return value.astype(jnp.bfloat16)
    realization_derivatives = lax.map(result_cotangent_vector, predicted_realizations)

    def backward(pair):
        activation_field, cotan = pair
        padded_in, first_bf, pre_act, hidden_pad, second_flat, out = evaluate_postprocessor(activation_field)
        cot_flat = cotan.reshape(COUT, -1)
        g_point_two = contract(cot_flat, second_flat, ((1,), (1,)))
        g_bias_two = lax.optimization_barrier(jnp.sum(cot_flat.astype(jnp.float32), axis=1))
        back_two = contract(point_two, cot_flat, ((0,), (0,))).astype(jnp.bfloat16).reshape(HID, LAT, LON)
        g_depth_two = kernel_grad(back_two, hidden_pad, LAT, LON)
        back_hidden = depthwise_back(pad_poles(wrap_lon(back_two)), depth_two, LAT, LON)
        gate = jax.nn.sigmoid(pre_act)
        back_pre = (back_hidden * gate * (1.0 + pre_act * (1.0 - gate))).astype(jnp.bfloat16)
        pre_flat = back_pre.reshape(HID, -1)
        g_point_one = contract(pre_flat, first_bf.reshape(CIN, -1), ((1,), (1,)))
        g_bias_one = lax.optimization_barrier(jnp.sum(pre_flat.astype(jnp.float32), axis=1))
        back_first = contract(point_one, pre_flat, ((0,), (0,))).reshape(CIN, LAT, LON)
        g_depth_one = kernel_grad(back_first, padded_in, LAT, LON)
        return (g_depth_one, g_point_one, g_bias_one, g_depth_two, g_point_two, g_bias_two)
    grads = lax.map(backward, (predictor_inputs, realization_derivatives))
    cumulative_accumulations = [lax.optimization_barrier(jnp.sum(item, axis=0)) for item in grads]
    return (predicted_realizations, cumulative_accumulations[0], cumulative_accumulations[1], cumulative_accumulations[2], cumulative_accumulations[3], cumulative_accumulations[4], cumulative_accumulations[5])
```

```python
import functools

import jax
import jax.numpy as jnp
from jax import lax
from jax.experimental import pallas as pl
from jax.experimental.pallas import tpu as pltpu
from jax.sharding import PartitionSpec as P

smooth_width = 0.25
pair_weight = 0.95

slabs = 16
pitch = 160
own = 16
wide = 144
chunk = 48
edge_rows = 56

f32 = jnp.float32
bf16 = jnp.bfloat16


def lanes_of(shape):
    return lax.broadcasted_iota(jnp.int32, shape, len(shape) - 1)


def dot(left, right, left_dim, right_dim):
    return lax.dot_general(
        left, right, (((left_dim,), (right_dim,)), ((), ())), preferred_element_type=f32
    )


def rounded(value):
    return value.astype(bf16).astype(f32)


def wrap_slabs(ref):
    last = pltpu.roll(ref[slabs], 64, 1)
    ref[0] = jnp.where(lanes_of(last.shape) >= 64, last, 0.0)
    first = pltpu.roll(ref[1], 64, 1)
    ref[slabs + 1] = jnp.where(lanes_of(first.shape) < 64, first, 0.0)


def both_halves(row):
    return jnp.concatenate([row, row], axis=1)


def edge_kernel(x_ref, target_ref, xt_ref, first_ref, last_ref, rows_scr):
    rows_scr[...] = x_ref[...].reshape(64 * 32, 128).astype(f32)

    def body(p, _):
        here = jnp.concatenate(
            [rows_scr[pl.ds(p, 64, stride=32), :], rows_scr[pl.ds(p + 16, 64, stride=32), :]],
            axis=0,
        )
        turned = here.T
        xt_ref[p] = turned
        for j in range(3):
            first_ref[pl.ds(16 * j + p, 1), :] = turned[j : j + 1]
            last_ref[pl.ds(16 * j + p, 1), :] = turned[125 + j : 126 + j]
        return 0

    lax.fori_loop(0, slabs, body, 0)
    for k in range(4):
        turned = target_ref[4 * k : 4 * k + 4].reshape(128, 128).T
        first_ref[48 + k : 49 + k, :] = turned[0:1]
        last_ref[48 + k : 49 + k, :] = turned[127:128]
    first_ref[52:56, :] = jnp.zeros((4, 128), f32)
    last_ref[52:56, :] = jnp.zeros((4, 128), f32)


def forward_kernel(
    xt_ref, left_ref, right_ref, depth_one_ref, point_one_ref, bias_one_ref,
    depth_two_ref, point_two_ref, bias_two_ref,
    out_ref, send_ref, xs_ref, first_ref, gate_ref, hidden_ref, second_ref,
    one_ref, two_ref, taps_two_ref,
    hs_ref, y_ref, edge_ref, taps_one_ref, turn_ref, bias_ref,
):
    turn_ref[...] = jnp.zeros((128, 128), f32)
    turn_ref[0:64, 0:9] = depth_one_ref[...]
    taps = turn_ref[...].T[0:16]
    taps_one_ref[...] = taps + pltpu.roll(taps, 64, 1)
    turn_ref[0:64, 0:9] = depth_two_ref[...]
    taps = turn_ref[...].T[0:16]
    taps_two_ref[...] = taps + pltpu.roll(taps, 64, 1)
    turn_ref[...] = jnp.zeros((128, 128), f32)
    turn_ref[0:1, 0:16] = bias_two_ref[...]
    column = jnp.broadcast_to(turn_ref[...].T[0:16, 0:1], (16, 128))
    bias_ref[0:16] = column
    bias_ref[16:32] = column
    turn_ref[...] = jnp.zeros((128, 128), f32)
    weight = point_one_ref[...].astype(f32)
    turn_ref[0:64, 0:64] = weight
    turn_ref[64:128, 64:128] = weight
    one_ref[...] = turn_ref[...].astype(bf16)
    one_turned = turn_ref[...].T.astype(bf16)
    weight = point_two_ref[...].astype(f32)
    zero = jnp.zeros((16, 64), f32)
    two = jnp.concatenate(
        [jnp.concatenate([weight, zero], axis=1), jnp.concatenate([zero, weight], axis=1)], axis=0
    ).astype(bf16)
    two_ref[...] = two
    bias_one = both_halves(bias_one_ref[...])

    for k in range(slabs + 2):
        xs_ref[k, 0:16, :] = jnp.zeros((16, 128), f32)
        xs_ref[k, 144:160, :] = jnp.zeros((16, 128), f32)
    for p in range(slabs):
        xs_ref[p + 1, own : own + 128, :] = xt_ref[p]
        for j in range(3):
            xs_ref[p + 1, 13 + j : 14 + j, :] = left_ref[16 * j + p : 16 * j + p + 1, :]
            xs_ref[p + 1, 144 + j : 145 + j, :] = right_ref[16 * j + p : 16 * j + p + 1, :]
    wrap_slabs(xs_ref)

    def first_body(p, _):
        total = jnp.zeros((wide, 128), f32)
        for a in range(3):
            for b in range(3):
                tap = taps_one_ref[3 * a + b : 3 * a + b + 1, :]
                total = total + tap * xs_ref[p + a, 7 + b : 7 + b + wide, :]
        first_ref[p] = total[8:136].astype(bf16)
        pre = dot(total.astype(bf16), one_turned, 1, 0) + bias_one
        gate = 1.0 / (1.0 + jnp.exp(-pre))
        hidden = rounded(pre * gate)
        hs_ref[p + 1, 8 : 8 + wide, :] = hidden
        hidden_ref[p] = hidden[8:136].astype(bf16)
        gate_ref[p] = (gate * (1.0 + pre * (1.0 - gate)))[8:136]
        return 0

    for k in range(slabs + 2):
        hs_ref[k, 0:8, :] = jnp.zeros((8, 128), f32)
        hs_ref[k, 152:160, :] = jnp.zeros((8, 128), f32)
    lax.fori_loop(0, slabs, first_body, 0)
    wrap_slabs(hs_ref)
    y_ref[...] = jnp.zeros(y_ref.shape, f32)
    edge_ref[...] = jnp.zeros(edge_ref.shape, f32)

    def second_body(p, _):
        total = jnp.zeros((wide, 128), f32)
        for a in range(3):
            for b in range(3):
                tap = taps_two_ref[3 * a + b : 3 * a + b + 1, :]
                total = total + tap * hs_ref[p + a, 7 + b : 7 + b + wide, :]
        second = total[8:136].astype(bf16)
        second_ref[p] = second
        edge_ref[pl.ds(p, 1), :] = total[7:8]
        edge_ref[pl.ds(16 + p, 1), :] = total[136:137]
        y = dot(two, second, 1, 1) + bias_ref[...]
        y_ref[pl.ds(p, 16, stride=chunk), :] = y[0:16]
        y_ref[pl.ds(16 + p, 16, stride=chunk), :] = y[16:32]
        return 0

    lax.fori_loop(0, slabs, second_body, 0)
    y = dot(two, edge_ref[...].astype(bf16), 1, 1) + bias_ref[...]
    lane = lanes_of((16, 128))
    y = jnp.where(lane < 32, y[0:16], jnp.where(lane < 64, pltpu.roll(y[16:32], 32, 1), 0.0))
    y_ref[pl.ds(32, 16, stride=chunk), :] = y
    send = y_ref[...].astype(bf16).reshape(16, chunk, 128)
    send_ref[...] = send
    out_ref[0] = send[:, 0:32]


def slope(diff):
    return diff * lax.rsqrt(diff * diff + smooth_width * smooth_width)


def crps_kernel(cells_all, x_ref, target_ref, left_ref, right_ref, out_ref):
    members = x_ref.shape[0]
    me = lax.axis_index("member")
    turn = lax.rem(4 - lax.rem(me, 4), 4) * 32
    left = left_ref[pl.ds(48 + me // 4, 1), :]
    right = right_ref[pl.ds(48 + me // 4, 1), :]
    left = pltpu.roll(jnp.broadcast_to(left, (16, 128)), turn, 1)
    right = pltpu.roll(jnp.broadcast_to(right, (16, 128)), turn, 1)
    lane = lanes_of((16, 128))
    halo = jnp.where(
        lane < 16,
        left,
        jnp.where(
            lane < 32,
            pltpu.roll(right, 16, 1),
            jnp.where(lane < 48, pltpu.roll(left, 16, 1), pltpu.roll(right, 32, 1)),
        ),
    )
    for part in range(3):
        rows = slice(16 * part, 16 * part + 16)
        x = [x_ref[i, rows, :].astype(f32) for i in range(members)]
        total = [None] * members
        for i in range(members):
            for j in range(i + 1, members):
                s = slope(x[i] - x[j])
                total[i] = s if total[i] is None else total[i] + s
                total[j] = -s if total[j] is None else total[j] - s
        aim = halo if part == 2 else target_ref[me, rows, :]
        for i in range(members):
            value = slope(x[i] - aim) - pair_weight / (members - 1) * total[i]
            out_ref[i, rows, :] = (value / cells_all).astype(bf16)


def tap_sum(value):
    return jnp.sum(value.reshape(16, 8, 128), axis=0)


def backward_kernel(
    cot_ref, xs_ref, first_ref, gate_ref, hidden_ref, second_ref, one_ref, two_ref, taps_two_ref,
    out_ref,
    cf_ref, bs_ref, sums_ref, cot_sum_ref, point_two_ref, point_one_ref, other_ref,
):
    cf_ref[...] = cot_ref[...].reshape(16 * chunk, 128).astype(f32)
    two = two_ref[...]
    one = one_ref[...]
    sums_ref[...] = jnp.zeros(sums_ref.shape, f32)
    cot_sum_ref[...] = jnp.zeros(cot_sum_ref.shape, f32)
    point_two_ref[...] = jnp.zeros(point_two_ref.shape, f32)
    point_one_ref[...] = jnp.zeros(point_one_ref.shape, f32)
    other_ref[...] = jnp.zeros(other_ref.shape, f32)

    def cot_body(p, _):
        cot = jnp.concatenate(
            [cf_ref[pl.ds(p, 16, stride=chunk), :], cf_ref[pl.ds(16 + p, 16, stride=chunk), :]], axis=0
        )
        cot_sum_ref[...] += cot
        cot = cot.astype(bf16)
        bs_ref[p + 1, own : own + 128, :] = rounded(dot(cot, two, 0, 0))
        point_two_ref[...] += dot(cot, second_ref[p], 1, 0)
        return 0

    lax.fori_loop(0, slabs, cot_body, 0)
    halo = cf_ref[pl.ds(32, 16, stride=chunk), :]
    halo = jnp.concatenate([halo, pltpu.roll(halo, 96, 1)], axis=0).astype(bf16)
    halo = rounded(dot(halo, two, 0, 0))
    for p in range(slabs):
        bs_ref[p + 1, 15:16, :] = halo[p : p + 1]
        bs_ref[p + 1, 144:145, :] = halo[16 + p : 17 + p]
    wrap_slabs(bs_ref)

    def body(p, _):
        total = jnp.zeros((128, 128), f32)
        hidden = hidden_ref[p].astype(f32)
        for a in range(3):
            for b in range(3):
                t = 3 * a + b
                back = bs_ref[p + 2 - a, 17 - b : 145 - b, :]
                total = total + taps_two_ref[t : t + 1, :] * back
                sums_ref[9 + t] += tap_sum(back * hidden)
        back_pre = (total * gate_ref[p]).astype(bf16)
        sums_ref[18] += tap_sum(back_pre.astype(f32))
        point_one_ref[...] += dot(back_pre, first_ref[p], 0, 0)
        back_first = dot(back_pre, one, 1, 0)
        for a in range(3):
            for b in range(3):
                sums_ref[3 * a + b] += tap_sum(back_first * xs_ref[p + a, 15 + b : 143 + b, :])
        return 0

    lax.fori_loop(0, slabs, body, 0)
    for t in range(19):
        total = jnp.sum(sums_ref[t], axis=0, keepdims=True)
        other_ref[t : t + 1, :] = total + pltpu.roll(total, 64, 1)
    other_ref[24:40, :] = pltpu.roll(point_two_ref[0:16], 64, 1) + point_two_ref[16:32]
    bias_two = jnp.sum(cot_sum_ref[0:16] + cot_sum_ref[16:32], axis=1, keepdims=True)
    other_ref[40:56, :] = jnp.broadcast_to(bias_two, (16, 128))
    point_one = point_one_ref[0:64] + pltpu.roll(point_one_ref[64:128], 64, 1)
    packed = jnp.where(lanes_of((64, 128)) < 64, point_one, other_ref[...])
    out_ref[...] = packed.reshape(out_ref.shape)


def call(kernel, out_shape, scratch, flops):
    return pl.pallas_call(
        kernel,
        out_shape=out_shape,
        scratch_shapes=scratch,
        compiler_params=pltpu.CompilerParams(vmem_limit_bytes=24 * 1024 * 1024),
        cost_estimate=pl.CostEstimate(flops=flops, bytes_accessed=4 << 20, transcendentals=0),
    )


def shape(dims, dtype):
    return jax.ShapeDtypeStruct(dims, dtype)


def local(predictor_inputs, target, depth_one, point_one, bias_one, depth_two, point_two, bias_two):
    members = lax.axis_size("member")
    tiles = lax.axis_size("tile")
    _, chans, rows, cols = predictor_inputs.shape
    slab = (slabs, cols, 128)
    xt, first_cols, last_cols = call(
        edge_kernel,
        (shape(slab, f32), shape((edge_rows, 128), f32), shape((edge_rows, 128), f32)),
        [pltpu.VMEM((chans * rows, 128), f32)],
        1 << 20,
    )(predictor_inputs[0], target)
    up = [(i, (i + 1) % tiles) for i in range(tiles)]
    left = lax.ppermute(last_cols, "tile", up)
    right = lax.ppermute(first_cols, "tile", [(j, i) for i, j in up])
    out, send, xs, first, gate, hidden, second, one, two, taps_two = call(
        forward_kernel,
        (
            shape((1, 16, rows, cols), bf16),
            shape((16, chunk, 128), bf16),
            shape((slabs + 2, pitch, 128), f32),
            shape(slab, bf16),
            shape(slab, f32),
            shape(slab, bf16),
            shape(slab, bf16),
            shape((128, 128), bf16),
            shape((32, 128), bf16),
            shape((16, 128), f32),
        ),
        [
            pltpu.VMEM((slabs + 2, pitch, 128), f32),
            pltpu.VMEM((16 * chunk, 128), f32),
            pltpu.VMEM((128, 128), f32),
            pltpu.VMEM((16, 128), f32),
            pltpu.VMEM((128, 128), f32),
            pltpu.VMEM((32, 128), f32),
        ],
        1 << 28,
    )(xt, left, right, depth_one, point_one, bias_one[None], depth_two, point_two, bias_two[None])
    seen = lax.all_to_all(send, "member", 0, 0, tiled=True)
    cot = call(
        functools.partial(crps_kernel, rows * cols * tiles),
        shape((members, chunk, 128), bf16),
        [],
        1 << 24,
    )(seen, target, left, right)
    cot = lax.all_to_all(cot, "member", 0, 0, tiled=True)
    packed = call(
        backward_kernel,
        shape((members, 64 // members, 128), f32),
        [
            pltpu.VMEM((16 * chunk, 128), f32),
            pltpu.VMEM((slabs + 2, pitch, 128), f32),
            pltpu.VMEM((19, 8, 128), f32),
            pltpu.VMEM((32, 128), f32),
            pltpu.VMEM((32, 128), f32),
            pltpu.VMEM((128, 128), f32),
            pltpu.VMEM((64, 128), f32),
        ],
        1 << 28,
    )(cot, xs, first, gate, hidden, second, one, two, taps_two)
    part = jnp.sum(lax.all_to_all(packed, "member", 0, 0, tiled=True), axis=0)
    part = jnp.broadcast_to(part[None], (tiles,) + part.shape)
    part = jnp.sum(lax.all_to_all(part, "tile", 0, 0, tiled=True), axis=0)
    part = jnp.broadcast_to(part[None], (members,) + part.shape)
    total = lax.all_to_all(part, "member", 0, 0, tiled=True).reshape(64, 128)
    other = total[:, 64:]
    return (
        out,
        other[0:9].T,
        total[:, :64],
        other[18],
        other[9:18].T,
        other[24:40],
        other[40:56, 0],
    )


def solution(mesh):
    return jax.shard_map(
        local,
        mesh=mesh,
        in_specs=(
            P("member", None, None, "tile"),
            P(None, None, "tile"),
            P(),
            P(),
            P(),
            P(),
            P(),
            P(),
        ),
        out_specs=(P("member", None, None, "tile"), P(), P(), P(), P(), P(), P()),
        check_vma=False,
    )
```

```python
import functools

import jax
import jax.numpy as jnp
from jax import lax
from jax.experimental import pallas as pl
from jax.experimental.pallas import tpu as pltpu
from jax.sharding import PartitionSpec as P

smooth_width = 0.25
pair_weight = 0.95

slabs = 16
pitch = 160
own = 16
wide = 144
chunk = 48
edge_rows = 56

f32 = jnp.float32
bf16 = jnp.bfloat16


def lanes_of(shape):
    return lax.broadcasted_iota(jnp.int32, shape, len(shape) - 1)


def dot(left, right, left_dim, right_dim):
    return lax.dot_general(
        left, right, (((left_dim,), (right_dim,)), ((), ())), preferred_element_type=f32
    )


def rounded(value):
    return value.astype(bf16).astype(f32)


def wrap_slabs(ref):
    last = pltpu.roll(ref[slabs], 64, 1)
    ref[0] = jnp.where(lanes_of(last.shape) >= 64, last, 0.0)
    first = pltpu.roll(ref[1], 64, 1)
    ref[slabs + 1] = jnp.where(lanes_of(first.shape) < 64, first, 0.0)


def both_halves(row):
    return jnp.concatenate([row, row], axis=1)


def each_slab(body):
    def step(p, carry):
        body(p)
        return carry

    lax.fori_loop(0, slabs, step, 0, unroll=True)


def fetch(sources, places, sems):
    copies = [
        pltpu.make_async_copy(source, place, sems.at[k])
        for k, (source, place) in enumerate(zip(sources, places))
    ]
    for copy in copies:
        copy.start()
    return copies


def edge_kernel(x_hbm, target_hbm, xt_ref, first_ref, last_ref, x_ref, target_ref, rows_scr, sems):
    x_copy, target_copy = fetch((x_hbm.at[0], target_hbm), (x_ref, target_ref), sems)
    x_copy.wait()
    rows_scr[...] = x_ref[...].reshape(64 * 32, 128).astype(f32)

    def body(p):
        here = jnp.concatenate(
            [rows_scr[pl.ds(p, 64, stride=32), :], rows_scr[pl.ds(p + 16, 64, stride=32), :]],
            axis=0,
        )
        turned = here.T
        xt_ref[p] = turned
        for j in range(3):
            first_ref[pl.ds(16 * j + p, 1), :] = turned[j : j + 1]
            last_ref[pl.ds(16 * j + p, 1), :] = turned[125 + j : 126 + j]

    each_slab(body)
    target_copy.wait()
    for k in range(4):
        turned = target_ref[4 * k : 4 * k + 4].reshape(128, 128).T
        first_ref[48 + k : 49 + k, :] = turned[0:1]
        last_ref[48 + k : 49 + k, :] = turned[127:128]
    first_ref[52:56, :] = jnp.zeros((4, 128), f32)
    last_ref[52:56, :] = jnp.zeros((4, 128), f32)


def weight_kernel(
    depth_one_hbm, point_one_hbm, bias_one_hbm, depth_two_hbm, point_two_hbm, bias_two_hbm,
    taps_one_ref, one_ref, one_turned_ref, bias_one_ref, taps_two_ref, two_ref, bias_two_ref,
    d1_ref, p1_ref, b1_ref, d2_ref, p2_ref, b2_ref, turn_ref, sems,
):
    places = (d1_ref, p1_ref, b1_ref, d2_ref, p2_ref, b2_ref)
    sources = (
        depth_one_hbm, point_one_hbm, bias_one_hbm, depth_two_hbm, point_two_hbm, bias_two_hbm
    )
    copies = fetch(sources, places, sems)
    turn_ref[...] = jnp.zeros((128, 128), f32)
    for copy in copies:
        copy.wait()
    zero = jnp.zeros((7, 128), f32)
    taps_one_ref[...] = jnp.concatenate([both_halves(d1_ref[...]), zero], axis=0)
    taps_two_ref[...] = jnp.concatenate([both_halves(d2_ref[...]), zero], axis=0)
    bias_one_ref[...] = jnp.broadcast_to(both_halves(b1_ref[...]), (8, 128))
    turn_ref[0:1, 0:16] = b2_ref[...]
    column = jnp.broadcast_to(turn_ref[...].T[0:16, 0:1], (16, 128))
    bias_two_ref[0:16] = column
    bias_two_ref[16:32] = column
    turn_ref[0:1, :] = jnp.zeros((1, 128), f32)
    weight = p1_ref[...].astype(f32)
    turn_ref[0:64, 0:64] = weight
    turn_ref[64:128, 64:128] = weight
    one_ref[...] = turn_ref[...].astype(bf16)
    one_turned_ref[...] = turn_ref[...].T.astype(bf16)
    weight = p2_ref[...].astype(f32)
    zero = jnp.zeros((16, 64), f32)
    two_ref[...] = jnp.concatenate(
        [jnp.concatenate([weight, zero], axis=1), jnp.concatenate([zero, weight], axis=1)], axis=0
    ).astype(bf16)


def forward_kernel(
    xt_ref, left_ref, right_ref,
    taps_one_ref, one_turned_ref, bias_one_ref, taps_two_ref, two_ref, bias_ref,
    out_ref, send_ref, xs_ref, first_ref, gate_ref, hidden_ref, second_ref,
    hs_ref, y_ref, edge_ref,
):
    one_turned = one_turned_ref[...]
    two = two_ref[...]
    bias_one = bias_one_ref[0:1]

    for k in range(slabs + 2):
        xs_ref[k, 0:16, :] = jnp.zeros((16, 128), f32)
        xs_ref[k, 144:160, :] = jnp.zeros((16, 128), f32)
    for p in range(slabs):
        xs_ref[p + 1, own : own + 128, :] = xt_ref[p]
        for j in range(3):
            xs_ref[p + 1, 13 + j : 14 + j, :] = left_ref[16 * j + p : 16 * j + p + 1, :]
            xs_ref[p + 1, 144 + j : 145 + j, :] = right_ref[16 * j + p : 16 * j + p + 1, :]
    wrap_slabs(xs_ref)

    def first_body(p):
        total = jnp.zeros((wide, 128), f32)
        for a in range(3):
            for b in range(3):
                tap = taps_one_ref[3 * a + b : 3 * a + b + 1, :]
                total = total + tap * xs_ref[p + a, 7 + b : 7 + b + wide, :]
        first_ref[p] = total[8:136].astype(bf16)
        pre = dot(total.astype(bf16), one_turned, 1, 0) + bias_one
        gate = 1.0 / (1.0 + jnp.exp(-pre))
        hidden = rounded(pre * gate)
        hs_ref[p + 1, 8 : 8 + wide, :] = hidden
        hidden_ref[p] = hidden[8:136].astype(bf16)
        gate_ref[p] = (gate * (1.0 + pre * (1.0 - gate)))[8:136]

    for k in range(slabs + 2):
        hs_ref[k, 0:8, :] = jnp.zeros((8, 128), f32)
        hs_ref[k, 152:160, :] = jnp.zeros((8, 128), f32)
    each_slab(first_body)
    wrap_slabs(hs_ref)
    y_ref[...] = jnp.zeros(y_ref.shape, f32)
    edge_ref[...] = jnp.zeros(edge_ref.shape, f32)

    def second_body(p):
        total = jnp.zeros((wide, 128), f32)
        for a in range(3):
            for b in range(3):
                tap = taps_two_ref[3 * a + b : 3 * a + b + 1, :]
                total = total + tap * hs_ref[p + a, 7 + b : 7 + b + wide, :]
        second = total[8:136].astype(bf16)
        second_ref[p] = second
        edge_ref[pl.ds(p, 1), :] = total[7:8]
        edge_ref[pl.ds(16 + p, 1), :] = total[136:137]
        y = dot(two, second, 1, 1) + bias_ref[...]
        y_ref[pl.ds(p, 16, stride=chunk), :] = y[0:16]
        y_ref[pl.ds(16 + p, 16, stride=chunk), :] = y[16:32]

    each_slab(second_body)
    y = dot(two, edge_ref[...].astype(bf16), 1, 1) + bias_ref[...]
    lane = lanes_of((16, 128))
    y = jnp.where(lane < 32, y[0:16], jnp.where(lane < 64, pltpu.roll(y[16:32], 32, 1), 0.0))
    y_ref[pl.ds(32, 16, stride=chunk), :] = y
    send = y_ref[...].astype(bf16).reshape(16, chunk, 128)
    send_ref[...] = send
    out_ref[0] = send[:, 0:32]


def slope(diff):
    return diff * lax.rsqrt(diff * diff + smooth_width * smooth_width)


def crps_kernel(cells_all, x_ref, target_ref, left_ref, right_ref, out_ref):
    members = x_ref.shape[0]
    me = lax.axis_index("member")
    turn = lax.rem(4 - lax.rem(me, 4), 4) * 32
    left = left_ref[pl.ds(48 + me // 4, 1), :]
    right = right_ref[pl.ds(48 + me // 4, 1), :]
    left = pltpu.roll(jnp.broadcast_to(left, (16, 128)), turn, 1)
    right = pltpu.roll(jnp.broadcast_to(right, (16, 128)), turn, 1)
    lane = lanes_of((16, 128))
    halo = jnp.where(
        lane < 16,
        left,
        jnp.where(
            lane < 32,
            pltpu.roll(right, 16, 1),
            jnp.where(lane < 48, pltpu.roll(left, 16, 1), pltpu.roll(right, 32, 1)),
        ),
    )
    for part in range(3):
        rows = slice(16 * part, 16 * part + 16)
        x = [x_ref[i, rows, :].astype(f32) for i in range(members)]
        total = [None] * members
        for i in range(members):
            for j in range(i + 1, members):
                s = slope(x[i] - x[j])
                total[i] = s if total[i] is None else total[i] + s
                total[j] = -s if total[j] is None else total[j] - s
        aim = halo if part == 2 else target_ref[me, rows, :]
        for i in range(members):
            value = slope(x[i] - aim) - pair_weight / (members - 1) * total[i]
            out_ref[i, rows, :] = (value / cells_all).astype(bf16)


def tap_sum(value):
    return jnp.sum(value.reshape(16, 8, 128), axis=0)


def backward_kernel(
    cot_ref, xs_ref, first_ref, gate_ref, hidden_ref, second_ref, one_ref, two_ref, taps_two_ref,
    out_ref,
    cf_ref, bs_ref, sums_ref, cot_sum_ref, point_two_ref, point_one_ref, other_ref,
):
    cf_ref[...] = cot_ref[...].reshape(16 * chunk, 128).astype(f32)
    two = two_ref[...]
    one = one_ref[...]
    sums_ref[...] = jnp.zeros(sums_ref.shape, f32)
    cot_sum_ref[...] = jnp.zeros(cot_sum_ref.shape, f32)
    point_two_ref[...] = jnp.zeros(point_two_ref.shape, f32)
    point_one_ref[...] = jnp.zeros(point_one_ref.shape, f32)
    other_ref[...] = jnp.zeros(other_ref.shape, f32)

    def cot_body(p):
        cot = jnp.concatenate(
            [cf_ref[pl.ds(p, 16, stride=chunk), :], cf_ref[pl.ds(16 + p, 16, stride=chunk), :]], axis=0
        )
        cot_sum_ref[0:32] += cot
        cot = cot.astype(bf16)
        bs_ref[p + 1, own : own + 128, :] = rounded(dot(cot, two, 0, 0))
        point_two_ref[...] += dot(cot, second_ref[p], 1, 0)

    each_slab(cot_body)
    halo = cf_ref[pl.ds(32, 16, stride=chunk), :]
    halo = jnp.concatenate([halo, pltpu.roll(halo, 96, 1)], axis=0).astype(bf16)
    halo = rounded(dot(halo, two, 0, 0))
    for p in range(slabs):
        bs_ref[p + 1, 15:16, :] = halo[p : p + 1]
        bs_ref[p + 1, 144:145, :] = halo[16 + p : 17 + p]
    wrap_slabs(bs_ref)

    def body(p):
        total = jnp.zeros((128, 128), f32)
        hidden = hidden_ref[p].astype(f32)
        for a in range(3):
            for b in range(3):
                t = 3 * a + b
                back = bs_ref[p + 2 - a, 17 - b : 145 - b, :]
                total = total + taps_two_ref[t : t + 1, :] * back
                sums_ref[9 + t] += tap_sum(back * hidden)
        back_pre = (total * gate_ref[p]).astype(bf16)
        sums_ref[18] += tap_sum(back_pre.astype(f32))
        point_one_ref[...] += dot(back_pre, first_ref[p], 0, 0)
        back_first = dot(back_pre, one, 1, 0)
        for a in range(3):
            for b in range(3):
                sums_ref[3 * a + b] += tap_sum(back_first * xs_ref[p + a, 15 + b : 143 + b, :])

    each_slab(body)
    for t in range(19):
        total = jnp.sum(sums_ref[t], axis=0, keepdims=True)
        other_ref[t : t + 1, :] = total + pltpu.roll(total, 64, 1)
    other_ref[24:40, :] = pltpu.roll(point_two_ref[0:16], 64, 1) + point_two_ref[16:32]
    bias_two = jnp.sum(cot_sum_ref[...].T, axis=0, keepdims=True)
    bias_two = bias_two + pltpu.roll(bias_two, 112, 1)
    other_ref[19:20, :] = pltpu.roll(bias_two, 64, 1)
    point_one = point_one_ref[0:64] + pltpu.roll(point_one_ref[64:128], 64, 1)
    packed = jnp.where(lanes_of((64, 128)) < 64, point_one, other_ref[...])
    out_ref[...] = packed.reshape(out_ref.shape)


def output_kernel(total_ref, depth_one_ref, point_one_ref, bias_one_ref, depth_two_ref, point_two_ref, bias_two_ref, rows_ref):
    rows_ref[...] = total_ref[...].reshape(64, 128)
    point_one_ref[...] = rows_ref[:, 0:64]
    depth_one_ref[...] = rows_ref[0:9, 64:128]
    depth_two_ref[...] = rows_ref[9:18, 64:128]
    bias_one_ref[...] = rows_ref[18:19, 64:128]
    bias_two_ref[...] = rows_ref[19:20, 64:80]
    point_two_ref[...] = rows_ref[24:40, 64:128]


def call(kernel, out_shape, scratch, flops, fetched=0, passed=0):
    hbm = pl.BlockSpec(memory_space=pltpu.HBM)
    vmem = pl.BlockSpec(memory_space=pltpu.VMEM)
    return pl.pallas_call(
        kernel,
        out_shape=out_shape,
        in_specs=[hbm] * fetched + [vmem] * passed,
        scratch_shapes=scratch,
        compiler_params=pltpu.CompilerParams(vmem_limit_bytes=24 * 1024 * 1024),
        cost_estimate=pl.CostEstimate(flops=flops, bytes_accessed=4 << 20, transcendentals=0),
    )


def in_hbm(*arrays):
    return [pltpu.with_memory_space_constraint(array, pltpu.HBM) for array in arrays]


def shape(dims, dtype):
    return jax.ShapeDtypeStruct(dims, dtype)


def local(predictor_inputs, target, depth_one, point_one, bias_one, depth_two, point_two, bias_two):
    members = lax.axis_size("member")
    tiles = lax.axis_size("tile")
    _, chans, rows, cols = predictor_inputs.shape
    slab = (slabs, cols, 128)
    xt, first_cols, last_cols = call(
        edge_kernel,
        (shape(slab, f32), shape((edge_rows, 128), f32), shape((edge_rows, 128), f32)),
        [
            pltpu.VMEM((chans, rows, cols), bf16),
            pltpu.VMEM((16, rows, cols), f32),
            pltpu.VMEM((chans * rows, 128), f32),
            pltpu.SemaphoreType.DMA((2,)),
        ],
        1 << 20,
        fetched=2,
    )(*in_hbm(predictor_inputs, target))
    up = [(i, (i + 1) % tiles) for i in range(tiles)]
    left = lax.ppermute(last_cols, "tile", up)
    right = lax.ppermute(first_cols, "tile", [(j, i) for i, j in up])
    taps_one, one, one_turned, bias_one, taps_two, two, bias_two = call(
        weight_kernel,
        (
            shape((16, 128), f32),
            shape((128, 128), bf16),
            shape((128, 128), bf16),
            shape((8, 128), f32),
            shape((16, 128), f32),
            shape((32, 128), bf16),
            shape((32, 128), f32),
        ),
        [
            pltpu.VMEM((9, 64), f32),
            pltpu.VMEM((64, 64), bf16),
            pltpu.VMEM((1, 64), f32),
            pltpu.VMEM((9, 64), f32),
            pltpu.VMEM((16, 64), bf16),
            pltpu.VMEM((1, 16), f32),
            pltpu.VMEM((128, 128), f32),
            pltpu.SemaphoreType.DMA((6,)),
        ],
        1 << 20,
        fetched=6,
    )(
        *in_hbm(
            depth_one.T, point_one, bias_one[None], depth_two.T, point_two, bias_two[None]
        )
    )
    out, send, xs, first, gate, hidden, second = call(
        forward_kernel,
        (
            shape((1, 16, rows, cols), bf16),
            shape((16, chunk, 128), bf16),
            shape((slabs + 2, pitch, 128), f32),
            shape(slab, bf16),
            shape(slab, f32),
            shape(slab, bf16),
            shape(slab, bf16),
        ),
        [
            pltpu.VMEM((slabs + 2, pitch, 128), f32),
            pltpu.VMEM((16 * chunk, 128), f32),
            pltpu.VMEM((128, 128), f32),
        ],
        1 << 28,
        passed=9,
    )(xt, left, right, taps_one, one_turned, bias_one, taps_two, two, bias_two)
    seen = lax.all_to_all(send, "member", 0, 0, tiled=True)
    cot = call(
        functools.partial(crps_kernel, rows * cols * tiles),
        shape((members, chunk, 128), bf16),
        [],
        1 << 24,
        passed=4,
    )(seen, target, left, right)
    cot = lax.all_to_all(cot, "member", 0, 0, tiled=True)
    packed = call(
        backward_kernel,
        shape((16, 4, 128), f32),
        [
            pltpu.VMEM((16 * chunk, 128), f32),
            pltpu.VMEM((slabs + 2, pitch, 128), f32),
            pltpu.VMEM((19, 8, 128), f32),
            pltpu.VMEM((128, 128), f32),
            pltpu.VMEM((32, 128), f32),
            pltpu.VMEM((128, 128), f32),
            pltpu.VMEM((64, 128), f32),
        ],
        1 << 28,
        passed=9,
    )(cot, xs, first, gate, hidden, second, one, two, taps_two)
    axes = ("member", "tile")
    near = [[16 * g + k for k in range(16)] for g in range(members * tiles // 16)]
    far = [list(group) for group in zip(*near)]
    part = lax.all_to_all(packed, axes, 0, 0, tiled=True, axis_index_groups=near)
    part = jnp.sum(part, axis=0)
    part = jnp.broadcast_to(part[None], (len(near),) + part.shape)
    part = lax.all_to_all(part, axes, 0, 0, tiled=True, axis_index_groups=far)
    part = jnp.sum(part, axis=0)
    part = jnp.broadcast_to(part[None], (len(far),) + part.shape)
    total = lax.all_to_all(part, axes, 0, 0, tiled=True, axis_index_groups=near)
    g_depth_one, g_point_one, g_bias_one, g_depth_two, g_point_two, g_bias_two = call(
        output_kernel,
        (
            shape((9, 64), f32),
            shape((64, 64), f32),
            shape((1, 64), f32),
            shape((9, 64), f32),
            shape((16, 64), f32),
            shape((1, 16), f32),
        ),
        [pltpu.VMEM((64, 128), f32)],
        1 << 20,
        passed=1,
    )(total)
    return (
        out,
        g_depth_one.T,
        g_point_one,
        g_bias_one[0],
        g_depth_two.T,
        g_point_two,
        g_bias_two[0],
    )


def solution(mesh):
    return jax.shard_map(
        local,
        mesh=mesh,
        in_specs=(
            P("member", None, None, "tile"),
            P(None, None, "tile"),
            P(),
            P(),
            P(),
            P(),
            P(),
            P(),
        ),
        out_specs=(P("member", None, None, "tile"), P(), P(), P(), P(), P(), P()),
        check_vma=False,
    )
```

```python
import functools

import jax
import jax.numpy as jnp
from jax import lax
from jax.experimental import pallas as pl
from jax.experimental.pallas import tpu as pltpu
from jax.sharding import PartitionSpec as P

smooth_width = 0.25
pair_weight = 0.95

slabs = 16
pitch = 160
own = 16
wide = 144
chunk = 48
edge_rows = 56

f32 = jnp.float32
bf16 = jnp.bfloat16


def lanes_of(shape):
    return lax.broadcasted_iota(jnp.int32, shape, len(shape) - 1)


def dot(left, right, left_dim, right_dim):
    return lax.dot_general(
        left, right, (((left_dim,), (right_dim,)), ((), ())), preferred_element_type=f32
    )


def rounded(value):
    return value.astype(bf16).astype(f32)


def wrap_slabs(ref):
    last = pltpu.roll(ref[slabs], 64, 1)
    ref[0] = jnp.where(lanes_of(last.shape) >= 64, last, 0.0)
    first = pltpu.roll(ref[1], 64, 1)
    ref[slabs + 1] = jnp.where(lanes_of(first.shape) < 64, first, 0.0)


def both_halves(row):
    return jnp.concatenate([row, row], axis=1)


def each_slab(body):
    def step(p, carry):
        body(p)
        return carry

    lax.fori_loop(0, slabs, step, 0, unroll=True)


def fetch(sources, places, sems):
    copies = [
        pltpu.make_async_copy(source, place, sems.at[k])
        for k, (source, place) in enumerate(zip(sources, places))
    ]
    for copy in copies:
        copy.start()
    return copies


def edge_kernel(x_hbm, target_hbm, xt_ref, first_ref, last_ref, x_ref, target_ref, rows_scr, sems):
    x_copy, target_copy = fetch((x_hbm.at[0], target_hbm), (x_ref, target_ref), sems)
    x_copy.wait()
    rows_scr[...] = x_ref[...].reshape(64 * 32, 128).astype(f32)

    def body(p):
        here = jnp.concatenate(
            [rows_scr[pl.ds(p, 64, stride=32), :], rows_scr[pl.ds(p + 16, 64, stride=32), :]],
            axis=0,
        )
        turned = here.T
        xt_ref[p] = turned
        for j in range(3):
            first_ref[pl.ds(16 * j + p, 1), :] = turned[j : j + 1]
            last_ref[pl.ds(16 * j + p, 1), :] = turned[125 + j : 126 + j]

    each_slab(body)
    target_copy.wait()
    for k in range(4):
        turned = target_ref[4 * k : 4 * k + 4].reshape(128, 128).T
        first_ref[48 + k : 49 + k, :] = turned[0:1]
        last_ref[48 + k : 49 + k, :] = turned[127:128]
    first_ref[52:56, :] = jnp.zeros((4, 128), f32)
    last_ref[52:56, :] = jnp.zeros((4, 128), f32)


def main_kernel(
    depth_one_hbm, point_one_hbm, bias_one_hbm, depth_two_hbm, point_two_hbm, bias_two_hbm, xt_ref,
    taps_one_ref, one_ref, one_turned_ref, bias_one_ref, taps_two_ref, two_ref, bias_two_ref,
    first_ref, gate_ref, hidden_ref, second_ref,
    d1_ref, p1_ref, b1_ref, d2_ref, p2_ref, b2_ref, turn_ref, xs_ref, hs_ref, sems,
):
    places = (d1_ref, p1_ref, b1_ref, d2_ref, p2_ref, b2_ref)
    sources = (
        depth_one_hbm, point_one_hbm, bias_one_hbm, depth_two_hbm, point_two_hbm, bias_two_hbm
    )
    copies = fetch(sources, places, sems)
    turn_ref[...] = jnp.zeros((128, 128), f32)
    for ref in (xs_ref, hs_ref):
        for k in range(slabs + 2):
            ref[k, 0:8, :] = jnp.zeros((8, 128), f32)
            ref[k, 136:144, :] = jnp.zeros((8, 128), f32)
    for p in range(slabs):
        xs_ref[p + 1, 8:136, :] = xt_ref[p]
    wrap_slabs(xs_ref)
    for copy in copies:
        copy.wait()
    zero = jnp.zeros((7, 128), f32)
    taps_one_ref[...] = jnp.concatenate([both_halves(d1_ref[...]), zero], axis=0)
    taps_two_ref[...] = jnp.concatenate([both_halves(d2_ref[...]), zero], axis=0)
    bias_one_ref[...] = jnp.broadcast_to(both_halves(b1_ref[...]), (8, 128))
    turn_ref[0:1, 0:16] = b2_ref[...]
    column = jnp.broadcast_to(turn_ref[...].T[0:16, 0:1], (16, 128))
    bias_two_ref[0:16] = column
    bias_two_ref[16:32] = column
    turn_ref[0:1, :] = jnp.zeros((1, 128), f32)
    weight = p1_ref[...].astype(f32)
    turn_ref[0:64, 0:64] = weight
    turn_ref[64:128, 64:128] = weight
    one_ref[...] = turn_ref[...].astype(bf16)
    one_turned = turn_ref[...].T.astype(bf16)
    one_turned_ref[...] = one_turned
    weight = p2_ref[...].astype(f32)
    zero = jnp.zeros((16, 64), f32)
    two_ref[...] = jnp.concatenate(
        [jnp.concatenate([weight, zero], axis=1), jnp.concatenate([zero, weight], axis=1)], axis=0
    ).astype(bf16)

    def first_body(p):
        first = rounded(depthwise(taps_one_ref, xs_ref, p, 7, 128))
        first_ref[p] = first
        hidden, gate = activation(first, one_turned, bias_one_ref)
        hidden_ref[p] = hidden
        hs_ref[p + 1, 8:136, :] = hidden
        gate_ref[p] = gate

    def second_body(p):
        second_ref[p] = depthwise(taps_two_ref, hs_ref, p, 7, 128)

    each_slab(first_body)
    wrap_slabs(hs_ref)
    each_slab(second_body)


def depthwise(taps_ref, ref, p, row, count):
    total = jnp.zeros((count, 128), f32)
    for a in range(3):
        for b in range(3):
            tap = taps_ref[3 * a + b : 3 * a + b + 1, :]
            total = total + tap * ref[p + a, row + b : row + b + count, :]
    return total


def activation(first, one_turned, bias_ref):
    pre = dot(first.astype(bf16), one_turned, 1, 0) + bias_ref[0:1]
    gate = 1.0 / (1.0 + jnp.exp(-pre))
    return rounded(pre * gate), gate * (1.0 + pre * (1.0 - gate))


def with_edges(main, edge):
    return jnp.concatenate([edge[0:8], main[8:120], edge[8:16]], axis=0)


def halo_kernel(
    xt_ref, left_ref, right_ref, hidden_ref, main_second_ref,
    taps_one_ref, one_turned_ref, bias_one_ref, taps_two_ref, two_ref, bias_ref,
    out_ref, send_ref, xs_ref, first_ref, gate_ref, edge_hidden_ref, second_ref,
    hs_ref, first_scr, y_ref, edge_ref,
):
    two = two_ref[...]

    for k in range(slabs + 2):
        xs_ref[k, 0:16, :] = jnp.zeros((16, 128), f32)
        xs_ref[k, 144:160, :] = jnp.zeros((16, 128), f32)
    for p in range(slabs):
        xs_ref[p + 1, own : own + 128, :] = xt_ref[p]
        for j in range(3):
            xs_ref[p + 1, 13 + j : 14 + j, :] = left_ref[16 * j + p : 16 * j + p + 1, :]
            xs_ref[p + 1, 144 + j : 145 + j, :] = right_ref[16 * j + p : 16 * j + p + 1, :]
    wrap_slabs(xs_ref)

    def first_body(p):
        first = jnp.concatenate(
            [depthwise(taps_one_ref, xs_ref, p, 7, 16), depthwise(taps_one_ref, xs_ref, p, 135, 16)],
            axis=0,
        )
        first_scr[pl.ds(32 * p, 32), :] = rounded(first)

    each_slab(first_body)
    first = first_scr[...]
    hidden, gate = activation(first, one_turned_ref[...], bias_one_ref)
    for p in range(slabs):
        rows = slice(32 * p + 8, 32 * p + 24)
        first_ref[p] = first[rows]
        gate_ref[p] = gate[rows]
        edge_hidden_ref[p] = hidden[rows]
        hs_ref[p + 1, 0:8, :] = jnp.zeros((8, 128), f32)
        hs_ref[p + 1, 8:24, :] = hidden[32 * p : 32 * p + 16]
        hs_ref[p + 1, 24:32, :] = hidden_ref[p, 8:16, :]
        hs_ref[p + 1, 32:40, :] = hidden_ref[p, 112:120, :]
        hs_ref[p + 1, 40:56, :] = hidden[32 * p + 16 : 32 * p + 32]
        hs_ref[p + 1, 56:64, :] = jnp.zeros((8, 128), f32)
    wrap_slabs(hs_ref)
    y_ref[...] = jnp.zeros(y_ref.shape, f32)
    edge_ref[...] = jnp.zeros(edge_ref.shape, f32)

    def second_body(p):
        before = depthwise(taps_two_ref, hs_ref, p, 7, 16)
        after = depthwise(taps_two_ref, hs_ref, p, 39, 16)
        edge_ref[pl.ds(p, 1), :] = before[7:8]
        edge_ref[pl.ds(16 + p, 1), :] = after[8:9]
        edge = jnp.concatenate([before[8:16], after[0:8]], axis=0)
        second = with_edges(main_second_ref[p], edge).astype(bf16)
        second_ref[p] = second
        y = dot(two, second, 1, 1) + bias_ref[...]
        y_ref[pl.ds(p, 16, stride=chunk), :] = y[0:16]
        y_ref[pl.ds(16 + p, 16, stride=chunk), :] = y[16:32]

    each_slab(second_body)
    y = dot(two, edge_ref[...].astype(bf16), 1, 1) + bias_ref[...]
    lane = lanes_of((16, 128))
    y = jnp.where(lane < 32, y[0:16], jnp.where(lane < 64, pltpu.roll(y[16:32], 32, 1), 0.0))
    y_ref[pl.ds(32, 16, stride=chunk), :] = y
    send = y_ref[...].astype(bf16).reshape(16, chunk, 128)
    send_ref[...] = send
    out_ref[0] = send[:, 0:32]


def slope(diff):
    return diff * lax.rsqrt(diff * diff + smooth_width * smooth_width)


def crps_kernel(cells_all, x_ref, target_ref, left_ref, right_ref, out_ref):
    members = x_ref.shape[0]
    me = lax.axis_index("member")
    turn = lax.rem(4 - lax.rem(me, 4), 4) * 32
    left = left_ref[pl.ds(48 + me // 4, 1), :]
    right = right_ref[pl.ds(48 + me // 4, 1), :]
    left = pltpu.roll(jnp.broadcast_to(left, (16, 128)), turn, 1)
    right = pltpu.roll(jnp.broadcast_to(right, (16, 128)), turn, 1)
    lane = lanes_of((16, 128))
    halo = jnp.where(
        lane < 16,
        left,
        jnp.where(
            lane < 32,
            pltpu.roll(right, 16, 1),
            jnp.where(lane < 48, pltpu.roll(left, 16, 1), pltpu.roll(right, 32, 1)),
        ),
    )
    for part in range(3):
        rows = slice(16 * part, 16 * part + 16)
        used = 8 if part == 2 else 16
        x = [x_ref[i, rows, :].astype(f32)[0:used] for i in range(members)]
        total = [None] * members
        for i in range(members):
            for j in range(i + 1, members):
                s = slope(x[i] - x[j])
                total[i] = s if total[i] is None else total[i] + s
                total[j] = -s if total[j] is None else total[j] - s
        aim = halo[0:8] if part == 2 else target_ref[me, rows, :]
        for i in range(members):
            value = slope(x[i] - aim) - pair_weight / (members - 1) * total[i]
            if part == 2:
                value = jnp.concatenate([value, jnp.zeros((8, 128), f32)], axis=0)
            out_ref[i, rows, :] = (value / cells_all).astype(bf16)


def tap_sum(value):
    return jnp.sum(value.reshape(16, 8, 128), axis=0)


def backward_kernel(
    cot_ref, xs_ref, first_ref, gate_ref, hidden_ref, edge_first_ref, edge_gate_ref, edge_hidden_ref,
    second_ref, one_ref, two_ref, taps_two_ref,
    out_ref,
    cf_ref, bs_ref, sums_ref, cot_sum_ref, point_two_ref, point_one_ref, other_ref,
):
    cf_ref[...] = cot_ref[...].reshape(16 * chunk, 128).astype(f32)
    two = two_ref[...]
    one = one_ref[...]
    sums_ref[...] = jnp.zeros(sums_ref.shape, f32)
    cot_sum_ref[...] = jnp.zeros(cot_sum_ref.shape, f32)
    point_two_ref[...] = jnp.zeros(point_two_ref.shape, f32)
    point_one_ref[...] = jnp.zeros(point_one_ref.shape, f32)
    other_ref[...] = jnp.zeros(other_ref.shape, f32)

    def cot_body(p):
        cot = jnp.concatenate(
            [cf_ref[pl.ds(p, 16, stride=chunk), :], cf_ref[pl.ds(16 + p, 16, stride=chunk), :]], axis=0
        )
        cot_sum_ref[0:32] += cot
        cot = cot.astype(bf16)
        bs_ref[p + 1, own : own + 128, :] = rounded(dot(cot, two, 0, 0))
        point_two_ref[...] += dot(cot, second_ref[p], 1, 0)

    each_slab(cot_body)
    halo = cf_ref[pl.ds(32, 16, stride=chunk), :]
    halo = jnp.concatenate([halo, pltpu.roll(halo, 96, 1)], axis=0).astype(bf16)
    halo = rounded(dot(halo, two, 0, 0))
    for p in range(slabs):
        bs_ref[p + 1, 15:16, :] = halo[p : p + 1]
        bs_ref[p + 1, 144:145, :] = halo[16 + p : 17 + p]
    wrap_slabs(bs_ref)

    def body(p):
        total = jnp.zeros((128, 128), f32)
        hidden = with_edges(hidden_ref[p], edge_hidden_ref[p])
        for a in range(3):
            for b in range(3):
                t = 3 * a + b
                back = bs_ref[p + 2 - a, 17 - b : 145 - b, :]
                total = total + taps_two_ref[t : t + 1, :] * back
                sums_ref[9 + t] += tap_sum(back * hidden)
        back_pre = (total * with_edges(gate_ref[p], edge_gate_ref[p])).astype(bf16)
        sums_ref[18] += tap_sum(back_pre.astype(f32))
        first = with_edges(first_ref[p], edge_first_ref[p]).astype(bf16)
        point_one_ref[...] += dot(back_pre, first, 0, 0)
        back_first = dot(back_pre, one, 1, 0)
        for a in range(3):
            for b in range(3):
                sums_ref[3 * a + b] += tap_sum(back_first * xs_ref[p + a, 15 + b : 143 + b, :])

    each_slab(body)
    for t in range(19):
        total = jnp.sum(sums_ref[t], axis=0, keepdims=True)
        other_ref[t : t + 1, :] = total + pltpu.roll(total, 64, 1)
    other_ref[24:40, :] = pltpu.roll(point_two_ref[0:16], 64, 1) + point_two_ref[16:32]
    bias_two = jnp.sum(cot_sum_ref[...].T, axis=0, keepdims=True)
    bias_two = bias_two + pltpu.roll(bias_two, 112, 1)
    other_ref[19:20, :] = pltpu.roll(bias_two, 64, 1)
    point_one = point_one_ref[0:64] + pltpu.roll(point_one_ref[64:128], 64, 1)
    packed = jnp.where(lanes_of((64, 128)) < 64, point_one, other_ref[...])
    out_ref[...] = packed.reshape(out_ref.shape)


def output_kernel(total_ref, depth_one_ref, point_one_ref, bias_one_ref, depth_two_ref, point_two_ref, bias_two_ref, rows_ref):
    rows_ref[...] = total_ref[...].reshape(64, 128)
    point_one_ref[...] = rows_ref[:, 0:64]
    depth_one_ref[...] = rows_ref[0:9, 64:128]
    depth_two_ref[...] = rows_ref[9:18, 64:128]
    bias_one_ref[...] = rows_ref[18:19, 64:128]
    bias_two_ref[...] = rows_ref[19:20, 64:80]
    point_two_ref[...] = rows_ref[24:40, 64:128]


def call(kernel, out_shape, scratch, flops, fetched=0, passed=0):
    hbm = pl.BlockSpec(memory_space=pltpu.HBM)
    vmem = pl.BlockSpec(memory_space=pltpu.VMEM)
    return pl.pallas_call(
        kernel,
        out_shape=out_shape,
        in_specs=[hbm] * fetched + [vmem] * passed,
        scratch_shapes=scratch,
        compiler_params=pltpu.CompilerParams(vmem_limit_bytes=24 * 1024 * 1024),
        cost_estimate=pl.CostEstimate(flops=flops, bytes_accessed=4 << 20, transcendentals=0),
    )


def in_hbm(*arrays):
    return [pltpu.with_memory_space_constraint(array, pltpu.HBM) for array in arrays]


def shape(dims, dtype):
    return jax.ShapeDtypeStruct(dims, dtype)


def local(predictor_inputs, target, depth_one, point_one, bias_one, depth_two, point_two, bias_two):
    members = lax.axis_size("member")
    tiles = lax.axis_size("tile")
    _, chans, rows, cols = predictor_inputs.shape
    slab = (slabs, cols, 128)
    xt, first_cols, last_cols = call(
        edge_kernel,
        (shape(slab, f32), shape((edge_rows, 128), f32), shape((edge_rows, 128), f32)),
        [
            pltpu.VMEM((chans, rows, cols), bf16),
            pltpu.VMEM((16, rows, cols), f32),
            pltpu.VMEM((chans * rows, 128), f32),
            pltpu.SemaphoreType.DMA((2,)),
        ],
        1 << 20,
        fetched=2,
    )(*in_hbm(predictor_inputs, target))
    up = [(i, (i + 1) % tiles) for i in range(tiles)]
    left = lax.ppermute(last_cols, "tile", up)
    right = lax.ppermute(first_cols, "tile", [(j, i) for i, j in up])
    (
        taps_one, one, one_turned, bias_one, taps_two, two, bias_two,
        first, gate, hidden, main_second,
    ) = call(
        main_kernel,
        (
            shape((16, 128), f32),
            shape((128, 128), bf16),
            shape((128, 128), bf16),
            shape((8, 128), f32),
            shape((16, 128), f32),
            shape((32, 128), bf16),
            shape((32, 128), f32),
            shape(slab, f32),
            shape(slab, f32),
            shape(slab, f32),
            shape(slab, f32),
        ),
        [
            pltpu.VMEM((9, 64), f32),
            pltpu.VMEM((64, 64), bf16),
            pltpu.VMEM((1, 64), f32),
            pltpu.VMEM((9, 64), f32),
            pltpu.VMEM((16, 64), bf16),
            pltpu.VMEM((1, 16), f32),
            pltpu.VMEM((128, 128), f32),
            pltpu.VMEM((slabs + 2, wide, 128), f32),
            pltpu.VMEM((slabs + 2, wide, 128), f32),
            pltpu.SemaphoreType.DMA((6,)),
        ],
        1 << 28,
        fetched=6,
        passed=1,
    )(
        *in_hbm(
            depth_one.T, point_one, bias_one[None], depth_two.T, point_two, bias_two[None]
        ),
        xt,
    )
    edge = (slabs, 16, 128)
    out, send, xs, edge_first, edge_gate, edge_hidden, second = call(
        halo_kernel,
        (
            shape((1, 16, rows, cols), bf16),
            shape((16, chunk, 128), bf16),
            shape((slabs + 2, pitch, 128), f32),
            shape(edge, f32),
            shape(edge, f32),
            shape(edge, f32),
            shape(slab, bf16),
        ),
        [
            pltpu.VMEM((slabs + 2, 64, 128), f32),
            pltpu.VMEM((32 * slabs, 128), f32),
            pltpu.VMEM((16 * chunk, 128), f32),
            pltpu.VMEM((128, 128), f32),
        ],
        1 << 27,
        passed=11,
    )(
        xt, left, right, hidden, main_second, taps_one, one_turned, bias_one, taps_two, two, bias_two
    )
    seen = lax.all_to_all(send, "member", 0, 0, tiled=True)
    cot = call(
        functools.partial(crps_kernel, rows * cols * tiles),
        shape((members, chunk, 128), bf16),
        [],
        1 << 24,
        passed=4,
    )(seen, target, left, right)
    cot = lax.all_to_all(cot, "member", 0, 0, tiled=True)
    packed = call(
        backward_kernel,
        shape((16, 4, 128), f32),
        [
            pltpu.VMEM((16 * chunk, 128), f32),
            pltpu.VMEM((slabs + 2, pitch, 128), f32),
            pltpu.VMEM((19, 8, 128), f32),
            pltpu.VMEM((128, 128), f32),
            pltpu.VMEM((32, 128), f32),
            pltpu.VMEM((128, 128), f32),
            pltpu.VMEM((64, 128), f32),
        ],
        1 << 28,
        passed=12,
    )(
        cot, xs, first, gate, hidden, edge_first, edge_gate, edge_hidden, second, one, two, taps_two
    )
    axes = ("member", "tile")
    near = [[16 * g + k for k in range(16)] for g in range(members * tiles // 16)]
    far = [list(group) for group in zip(*near)]
    part = lax.all_to_all(packed, axes, 0, 0, tiled=True, axis_index_groups=near)
    part = jnp.sum(part, axis=0)
    part = jnp.broadcast_to(part[None], (len(near),) + part.shape)
    part = lax.all_to_all(part, axes, 0, 0, tiled=True, axis_index_groups=far)
    part = jnp.sum(part, axis=0)
    part = jnp.broadcast_to(part[None], (len(far),) + part.shape)
    total = lax.all_to_all(part, axes, 0, 0, tiled=True, axis_index_groups=near)
    g_depth_one, g_point_one, g_bias_one, g_depth_two, g_point_two, g_bias_two = call(
        output_kernel,
        (
            shape((9, 64), f32),
            shape((64, 64), f32),
            shape((1, 64), f32),
            shape((9, 64), f32),
            shape((16, 64), f32),
            shape((1, 16), f32),
        ),
        [pltpu.VMEM((64, 128), f32)],
        1 << 20,
        passed=1,
    )(total)
    return (
        out,
        g_depth_one.T,
        g_point_one,
        g_bias_one[0],
        g_depth_two.T,
        g_point_two,
        g_bias_two[0],
    )


def solution(mesh):
    return jax.shard_map(
        local,
        mesh=mesh,
        in_specs=(
            P("member", None, None, "tile"),
            P(None, None, "tile"),
            P(),
            P(),
            P(),
            P(),
            P(),
            P(),
        ),
        out_specs=(P("member", None, None, "tile"), P(), P(), P(), P(), P(), P()),
        check_vma=False,
    )
```

```python
import functools

import jax
import jax.numpy as jnp
from jax import lax
from jax.experimental import pallas as pl
from jax.experimental.pallas import tpu as pltpu
from jax.sharding import PartitionSpec as P

smooth_width = 0.25
pair_weight = 0.95

slabs = 16
pitch = 160
own = 16
wide = 144
chunk = 40
chunk_pitch = 50
lat_pitch = 34
edge_rows = 56

f32 = jnp.float32
bf16 = jnp.bfloat16


def lanes_of(shape):
    return lax.broadcasted_iota(jnp.int32, shape, len(shape) - 1)


def dot(left, right, left_dim, right_dim):
    return lax.dot_general(
        left, right, (((left_dim,), (right_dim,)), ((), ())), preferred_element_type=f32
    )


def rounded(value):
    return value.astype(bf16).astype(f32)


def wrap_slabs(ref):
    last = pltpu.roll(ref[slabs], 64, 1)
    ref[0] = jnp.where(lanes_of(last.shape) >= 64, last, 0.0)
    first = pltpu.roll(ref[1], 64, 1)
    ref[slabs + 1] = jnp.where(lanes_of(first.shape) < 64, first, 0.0)


def both_halves(row):
    return jnp.concatenate([row, row], axis=1)


def each_slab(body):
    def step(p, carry):
        body(p)
        return carry

    lax.fori_loop(0, slabs, step, 0, unroll=True)


def fetch(sources, places, sems):
    copies = [
        pltpu.make_async_copy(source, place, sems.at[k])
        for k, (source, place) in enumerate(zip(sources, places))
    ]
    for copy in copies:
        copy.start()
    return copies


def edge_kernel(x_hbm, target_hbm, xt_ref, first_ref, last_ref, x_ref, target_ref, rows_scr, sems):
    target_copy, x_copy = fetch((target_hbm, x_hbm.at[0]), (target_ref, x_ref), sems)
    target_copy.wait()
    for k in range(4):
        turned = target_ref[4 * k : 4 * k + 4].reshape(128, 128).T
        first_ref[48 + k : 49 + k, :] = turned[0:1]
        last_ref[48 + k : 49 + k, :] = turned[127:128]
    first_ref[52:56, :] = jnp.zeros((4, 128), f32)
    last_ref[52:56, :] = jnp.zeros((4, 128), f32)
    x_copy.wait()
    for c in range(64):
        rows_scr[lat_pitch * c : lat_pitch * c + 32, :] = x_ref[c].astype(f32)

    def body(p):
        here = jnp.concatenate(
            [rows_scr[pl.ds(p, 64, stride=lat_pitch), :], rows_scr[pl.ds(p + 16, 64, stride=lat_pitch), :]],
            axis=0,
        )
        turned = here.T
        xt_ref[p] = turned
        for j in range(3):
            first_ref[pl.ds(16 * j + p, 1), :] = turned[j : j + 1]
            last_ref[pl.ds(16 * j + p, 1), :] = turned[125 + j : 126 + j]

    each_slab(body)


def main_kernel(
    depth_one_hbm, point_one_hbm, bias_one_hbm, depth_two_hbm, point_two_hbm, bias_two_hbm, xt_ref,
    taps_one_ref, one_ref, one_turned_ref, bias_one_ref, taps_two_ref, two_ref, bias_two_ref,
    first_ref, gate_ref, hidden_ref, second_ref,
    d1_ref, p1_ref, b1_ref, d2_ref, p2_ref, b2_ref, turn_ref, xs_ref, hs_ref, sems,
):
    places = (d1_ref, p1_ref, b1_ref, d2_ref, p2_ref, b2_ref)
    sources = (
        depth_one_hbm, point_one_hbm, bias_one_hbm, depth_two_hbm, point_two_hbm, bias_two_hbm
    )
    copies = fetch(sources, places, sems)
    turn_ref[...] = jnp.zeros((128, 128), f32)
    for ref in (xs_ref, hs_ref):
        for k in range(slabs + 2):
            ref[k, 0:8, :] = jnp.zeros((8, 128), f32)
            ref[k, 136:144, :] = jnp.zeros((8, 128), f32)
    for p in range(slabs):
        xs_ref[p + 1, 8:136, :] = xt_ref[p]
    wrap_slabs(xs_ref)
    for copy in copies:
        copy.wait()
    zero = jnp.zeros((7, 128), f32)
    taps_one_ref[...] = jnp.concatenate([both_halves(d1_ref[...]), zero], axis=0)
    taps_two_ref[...] = jnp.concatenate([both_halves(d2_ref[...]), zero], axis=0)
    bias_one_ref[...] = jnp.broadcast_to(both_halves(b1_ref[...]), (8, 128))
    turn_ref[0:1, 0:16] = b2_ref[...]
    column = jnp.broadcast_to(turn_ref[...].T[0:16, 0:1], (16, 128))
    bias_two_ref[0:16] = column
    bias_two_ref[16:32] = column
    turn_ref[0:1, :] = jnp.zeros((1, 128), f32)
    weight = p1_ref[...].astype(f32)
    turn_ref[0:64, 0:64] = weight
    turn_ref[64:128, 64:128] = weight
    one_ref[...] = turn_ref[...].astype(bf16)
    one_turned = turn_ref[...].T.astype(bf16)
    one_turned_ref[...] = one_turned
    weight = p2_ref[...].astype(f32)
    zero = jnp.zeros((16, 64), f32)
    two_ref[...] = jnp.concatenate(
        [jnp.concatenate([weight, zero], axis=1), jnp.concatenate([zero, weight], axis=1)], axis=0
    ).astype(bf16)

    def first_body(p):
        first = rounded(depthwise(taps_one_ref, xs_ref, p, 7, 128))
        first_ref[p] = first
        hidden, gate = activation(first, one_turned, bias_one_ref)
        hidden_ref[p] = hidden
        hs_ref[p + 1, 8:136, :] = hidden
        gate_ref[p] = gate

    def second_body(p):
        second_ref[p] = depthwise(taps_two_ref, hs_ref, p, 7, 128)

    each_slab(first_body)
    wrap_slabs(hs_ref)
    each_slab(second_body)


def depthwise(taps_ref, ref, p, row, count):
    total = None
    for a in range(3):
        for b in range(3):
            tap = taps_ref[3 * a + b : 3 * a + b + 1, :]
            term = tap * ref[p + a, row + b : row + b + count, :]
            total = term if total is None else total + term
    return total


def activation(first, one_turned, bias_ref):
    pre = dot(first.astype(bf16), one_turned, 1, 0) + bias_ref[0:1]
    gate = 1.0 / (1.0 + jnp.exp(-pre))
    return rounded(pre * gate), gate * (1.0 + pre * (1.0 - gate))


def with_edges(main, edge):
    return jnp.concatenate([edge[0:8], main[8:120], edge[8:16]], axis=0)


def halo_kernel(
    xt_ref, left_ref, right_ref, hidden_ref, main_second_ref,
    taps_one_ref, one_turned_ref, bias_one_ref, taps_two_ref, two_ref, bias_ref,
    out_ref, send_ref, xs_ref, first_ref, gate_ref, edge_hidden_ref, second_ref,
    hs_ref, first_scr, y_ref, edge_ref,
):
    two = two_ref[...]

    for k in range(slabs + 2):
        xs_ref[k, 0:16, :] = jnp.zeros((16, 128), f32)
        xs_ref[k, 144:160, :] = jnp.zeros((16, 128), f32)
    for p in range(slabs):
        xs_ref[p + 1, own : own + 128, :] = xt_ref[p]
        for j in range(3):
            xs_ref[p + 1, 13 + j : 14 + j, :] = left_ref[16 * j + p : 16 * j + p + 1, :]
            xs_ref[p + 1, 144 + j : 145 + j, :] = right_ref[16 * j + p : 16 * j + p + 1, :]
    wrap_slabs(xs_ref)

    def first_body(p):
        first = jnp.concatenate(
            [depthwise(taps_one_ref, xs_ref, p, 7, 16), depthwise(taps_one_ref, xs_ref, p, 135, 16)],
            axis=0,
        )
        first_scr[pl.ds(32 * p, 32), :] = rounded(first)

    each_slab(first_body)
    first = first_scr[...]
    hidden, gate = activation(first, one_turned_ref[...], bias_one_ref)
    for p in range(slabs):
        rows = slice(32 * p + 8, 32 * p + 24)
        first_ref[p] = first[rows]
        gate_ref[p] = gate[rows]
        edge_hidden_ref[p] = hidden[rows]
        hs_ref[p + 1, 0:8, :] = jnp.zeros((8, 128), f32)
        hs_ref[p + 1, 8:24, :] = hidden[32 * p : 32 * p + 16]
        hs_ref[p + 1, 24:32, :] = hidden_ref[p, 8:16, :]
        hs_ref[p + 1, 32:40, :] = hidden_ref[p, 112:120, :]
        hs_ref[p + 1, 40:56, :] = hidden[32 * p + 16 : 32 * p + 32]
        hs_ref[p + 1, 56:64, :] = jnp.zeros((8, 128), f32)
    wrap_slabs(hs_ref)
    y_ref[...] = jnp.zeros(y_ref.shape, f32)
    edge_ref[...] = jnp.zeros(edge_ref.shape, f32)

    def second_body(p):
        before = depthwise(taps_two_ref, hs_ref, p, 7, 16)
        after = depthwise(taps_two_ref, hs_ref, p, 39, 16)
        edge_ref[pl.ds(p, 1), :] = before[7:8]
        edge_ref[pl.ds(16 + p, 1), :] = after[8:9]
        edge = jnp.concatenate([before[8:16], after[0:8]], axis=0)
        second = with_edges(main_second_ref[p], edge).astype(bf16)
        second_ref[p] = second
        y = dot(two, second, 1, 1) + bias_ref[...]
        y_ref[pl.ds(p, 16, stride=chunk_pitch), :] = y[0:16]
        y_ref[pl.ds(16 + p, 16, stride=chunk_pitch), :] = y[16:32]

    each_slab(second_body)
    y = dot(two, edge_ref[...].astype(bf16), 1, 1) + bias_ref[...]
    lane = lanes_of((16, 128))
    y = jnp.where(lane < 32, y[0:16], jnp.where(lane < 64, pltpu.roll(y[16:32], 32, 1), 0.0))
    y_ref[pl.ds(32, 16, stride=chunk_pitch), :] = y
    for o in range(16):
        send = y_ref[chunk_pitch * o : chunk_pitch * o + chunk, :].astype(bf16)
        send_ref[o] = send
        out_ref[0, o] = send[0:32]


def slope(diff):
    return diff * lax.rsqrt(diff * diff + smooth_width * smooth_width)


def crps_kernel(cells_all, x_ref, target_ref, left_ref, right_ref, out_ref):
    members = x_ref.shape[0]
    me = lax.axis_index("member")
    turn = lax.rem(4 - lax.rem(me, 4), 4) * 32
    left = left_ref[pl.ds(48 + me // 4, 1), :]
    right = right_ref[pl.ds(48 + me // 4, 1), :]
    left = pltpu.roll(jnp.broadcast_to(left, (8, 128)), turn, 1)
    right = pltpu.roll(jnp.broadcast_to(right, (8, 128)), turn, 1)
    lane = lanes_of((8, 128))
    halo = jnp.where(
        lane < 16,
        left,
        jnp.where(
            lane < 32,
            pltpu.roll(right, 16, 1),
            jnp.where(lane < 48, pltpu.roll(left, 16, 1), pltpu.roll(right, 32, 1)),
        ),
    )
    for rows in (slice(0, 16), slice(16, 32), slice(32, 40)):
        x = [x_ref[i, rows, :].astype(f32) for i in range(members)]
        total = [None] * members
        for i in range(members):
            for j in range(i + 1, members):
                s = slope(x[i] - x[j])
                total[i] = s if total[i] is None else total[i] + s
                total[j] = -s if total[j] is None else total[j] - s
        aim = halo if rows.start == 32 else target_ref[me, rows, :]
        for i in range(members):
            value = slope(x[i] - aim) - pair_weight / (members - 1) * total[i]
            out_ref[i, rows, :] = (value / cells_all).astype(bf16)


def tap_sum(value):
    return jnp.sum(value.reshape(16, 8, 128), axis=0)


def backward_kernel(
    cot_ref, xs_ref, first_ref, gate_ref, hidden_ref, edge_first_ref, edge_gate_ref, edge_hidden_ref,
    second_ref, one_ref, two_ref, taps_two_ref,
    out_ref,
    cf_ref, bs_ref, sums_ref, cot_sum_ref, point_two_ref, point_one_ref, other_ref,
):
    for o in range(16):
        cf_ref[chunk_pitch * o : chunk_pitch * o + chunk, :] = cot_ref[o].astype(f32)
    two = two_ref[...]
    one = one_ref[...]
    sums_ref[...] = jnp.zeros(sums_ref.shape, f32)
    cot_sum_ref[...] = jnp.zeros(cot_sum_ref.shape, f32)
    point_two_ref[...] = jnp.zeros(point_two_ref.shape, f32)
    point_one_ref[...] = jnp.zeros(point_one_ref.shape, f32)
    other_ref[...] = jnp.zeros(other_ref.shape, f32)

    def cot_body(p):
        cot = jnp.concatenate(
            [cf_ref[pl.ds(p, 16, stride=chunk_pitch), :], cf_ref[pl.ds(16 + p, 16, stride=chunk_pitch), :]], axis=0
        )
        cot_sum_ref[0:32] += cot
        cot = cot.astype(bf16)
        bs_ref[p + 1, own : own + 128, :] = rounded(dot(cot, two, 0, 0))
        point_two_ref[...] += dot(cot, second_ref[p], 1, 0)

    each_slab(cot_body)
    halo = cf_ref[pl.ds(32, 16, stride=chunk_pitch), :]
    halo = jnp.concatenate([halo, pltpu.roll(halo, 96, 1)], axis=0).astype(bf16)
    halo = rounded(dot(halo, two, 0, 0))
    for p in range(slabs):
        bs_ref[p + 1, 15:16, :] = halo[p : p + 1]
        bs_ref[p + 1, 144:145, :] = halo[16 + p : 17 + p]
    wrap_slabs(bs_ref)

    def body(p):
        total = None
        hidden = with_edges(hidden_ref[p], edge_hidden_ref[p])
        for a in range(3):
            for b in range(3):
                t = 3 * a + b
                back = bs_ref[p + 2 - a, 17 - b : 145 - b, :]
                term = taps_two_ref[t : t + 1, :] * back
                total = term if total is None else total + term
                sums_ref[9 + t] += tap_sum(back * hidden)
        back_pre = (total * with_edges(gate_ref[p], edge_gate_ref[p])).astype(bf16)
        sums_ref[18] += tap_sum(back_pre.astype(f32))
        first = with_edges(first_ref[p], edge_first_ref[p]).astype(bf16)
        point_one_ref[...] += dot(back_pre, first, 0, 0)
        back_first = dot(back_pre, one, 1, 0)
        for a in range(3):
            for b in range(3):
                sums_ref[3 * a + b] += tap_sum(back_first * xs_ref[p + a, 15 + b : 143 + b, :])

    each_slab(body)
    for t in range(19):
        total = jnp.sum(sums_ref[t], axis=0, keepdims=True)
        other_ref[t : t + 1, :] = total + pltpu.roll(total, 64, 1)
    other_ref[24:40, :] = pltpu.roll(point_two_ref[0:16], 64, 1) + point_two_ref[16:32]
    bias_two = jnp.sum(cot_sum_ref[...].T, axis=0, keepdims=True)
    bias_two = bias_two + pltpu.roll(bias_two, 112, 1)
    other_ref[19:20, :] = pltpu.roll(bias_two, 64, 1)
    point_one = point_one_ref[0:64] + pltpu.roll(point_one_ref[64:128], 64, 1)
    packed = jnp.where(lanes_of((64, 128)) < 64, point_one, other_ref[...])
    out_ref[...] = packed.reshape(out_ref.shape)


def output_kernel(total_ref, depth_one_ref, point_one_ref, bias_one_ref, depth_two_ref, point_two_ref, bias_two_ref, rows_ref):
    rows_ref[...] = total_ref[...].reshape(64, 128)
    point_one_ref[...] = rows_ref[:, 0:64]
    depth_one_ref[...] = rows_ref[0:9, 64:128]
    depth_two_ref[...] = rows_ref[9:18, 64:128]
    bias_one_ref[...] = rows_ref[18:19, 64:128]
    bias_two_ref[...] = rows_ref[19:20, 64:80]
    point_two_ref[...] = rows_ref[24:40, 64:128]


def call(kernel, out_shape, scratch, flops, fetched=0, passed=0):
    hbm = pl.BlockSpec(memory_space=pltpu.HBM)
    vmem = pl.BlockSpec(memory_space=pltpu.VMEM)
    return pl.pallas_call(
        kernel,
        out_shape=out_shape,
        in_specs=[hbm] * fetched + [vmem] * passed,
        scratch_shapes=scratch,
        compiler_params=pltpu.CompilerParams(vmem_limit_bytes=24 * 1024 * 1024),
        cost_estimate=pl.CostEstimate(flops=flops, bytes_accessed=4 << 20, transcendentals=0),
    )


def in_hbm(*arrays):
    return [pltpu.with_memory_space_constraint(array, pltpu.HBM) for array in arrays]


def shape(dims, dtype):
    return jax.ShapeDtypeStruct(dims, dtype)


def local(predictor_inputs, target, depth_one, point_one, bias_one, depth_two, point_two, bias_two):
    members = lax.axis_size("member")
    tiles = lax.axis_size("tile")
    _, chans, rows, cols = predictor_inputs.shape
    slab = (slabs, cols, 128)
    xt, first_cols, last_cols = call(
        edge_kernel,
        (shape(slab, f32), shape((edge_rows, 128), f32), shape((edge_rows, 128), f32)),
        [
            pltpu.VMEM((chans, rows, cols), bf16),
            pltpu.VMEM((16, rows, cols), f32),
            pltpu.VMEM((chans * lat_pitch, 128), f32),
            pltpu.SemaphoreType.DMA((2,)),
        ],
        1 << 20,
        fetched=2,
    )(*in_hbm(predictor_inputs, target))
    up = [(i, (i + 1) % tiles) for i in range(tiles)]
    left = lax.ppermute(last_cols, "tile", up)
    right = lax.ppermute(first_cols, "tile", [(j, i) for i, j in up])
    (
        taps_one, one, one_turned, bias_one, taps_two, two, bias_two,
        first, gate, hidden, main_second,
    ) = call(
        main_kernel,
        (
            shape((16, 128), f32),
            shape((128, 128), bf16),
            shape((128, 128), bf16),
            shape((8, 128), f32),
            shape((16, 128), f32),
            shape((32, 128), bf16),
            shape((32, 128), f32),
            shape(slab, f32),
            shape(slab, f32),
            shape(slab, f32),
            shape(slab, f32),
        ),
        [
            pltpu.VMEM((9, 64), f32),
            pltpu.VMEM((64, 64), bf16),
            pltpu.VMEM((1, 64), f32),
            pltpu.VMEM((9, 64), f32),
            pltpu.VMEM((16, 64), bf16),
            pltpu.VMEM((1, 16), f32),
            pltpu.VMEM((128, 128), f32),
            pltpu.VMEM((slabs + 2, wide, 128), f32),
            pltpu.VMEM((slabs + 2, wide, 128), f32),
            pltpu.SemaphoreType.DMA((6,)),
        ],
        1 << 28,
        fetched=6,
        passed=1,
    )(
        *in_hbm(
            depth_one.T, point_one, bias_one[None], depth_two.T, point_two, bias_two[None]
        ),
        xt,
    )
    edge = (slabs, 16, 128)
    out, send, xs, edge_first, edge_gate, edge_hidden, second = call(
        halo_kernel,
        (
            shape((1, 16, rows, cols), bf16),
            shape((16, chunk, 128), bf16),
            shape((slabs + 2, pitch, 128), f32),
            shape(edge, f32),
            shape(edge, f32),
            shape(edge, f32),
            shape(slab, bf16),
        ),
        [
            pltpu.VMEM((slabs + 2, 64, 128), f32),
            pltpu.VMEM((32 * slabs, 128), f32),
            pltpu.VMEM((16 * chunk_pitch, 128), f32),
            pltpu.VMEM((128, 128), f32),
        ],
        1 << 27,
        passed=11,
    )(
        xt, left, right, hidden, main_second, taps_one, one_turned, bias_one, taps_two, two, bias_two
    )
    seen = lax.all_to_all(send, "member", 0, 0, tiled=True)
    cot = call(
        functools.partial(crps_kernel, rows * cols * tiles),
        shape((members, chunk, 128), bf16),
        [],
        1 << 24,
        passed=4,
    )(seen, target, left, right)
    cot = lax.all_to_all(cot, "member", 0, 0, tiled=True)
    packed = call(
        backward_kernel,
        shape((16, 4, 128), f32),
        [
            pltpu.VMEM((16 * chunk_pitch, 128), f32),
            pltpu.VMEM((slabs + 2, pitch, 128), f32),
            pltpu.VMEM((19, 8, 128), f32),
            pltpu.VMEM((128, 128), f32),
            pltpu.VMEM((32, 128), f32),
            pltpu.VMEM((128, 128), f32),
            pltpu.VMEM((64, 128), f32),
        ],
        1 << 28,
        passed=12,
    )(
        cot, xs, first, gate, hidden, edge_first, edge_gate, edge_hidden, second, one, two, taps_two
    )
    axes = ("member", "tile")
    near = [[16 * g + k for k in range(16)] for g in range(members * tiles // 16)]
    far = [list(group) for group in zip(*near)]
    part = lax.all_to_all(packed, axes, 0, 0, tiled=True, axis_index_groups=near)
    part = jnp.sum(part, axis=0)
    part = jnp.broadcast_to(part[None], (len(near),) + part.shape)
    part = lax.all_to_all(part, axes, 0, 0, tiled=True, axis_index_groups=far)
    part = jnp.sum(part, axis=0)
    part = jnp.broadcast_to(part[None], (len(far),) + part.shape)
    total = lax.all_to_all(part, axes, 0, 0, tiled=True, axis_index_groups=near)
    g_depth_one, g_point_one, g_bias_one, g_depth_two, g_point_two, g_bias_two = call(
        output_kernel,
        (
            shape((9, 64), f32),
            shape((64, 64), f32),
            shape((1, 64), f32),
            shape((9, 64), f32),
            shape((16, 64), f32),
            shape((1, 16), f32),
        ),
        [pltpu.VMEM((64, 128), f32)],
        1 << 20,
        passed=1,
    )(total)
    return (
        out,
        g_depth_one.T,
        g_point_one,
        g_bias_one[0],
        g_depth_two.T,
        g_point_two,
        g_bias_two[0],
    )


def solution(mesh):
    return jax.shard_map(
        local,
        mesh=mesh,
        in_specs=(
            P("member", None, None, "tile"),
            P(None, None, "tile"),
            P(),
            P(),
            P(),
            P(),
            P(),
            P(),
        ),
        out_specs=(P("member", None, None, "tile"), P(), P(), P(), P(), P(), P()),
        check_vma=False,
    )
```

```python
import functools

import jax
import jax.numpy as jnp
from jax import lax
from jax.experimental import pallas as pl
from jax.experimental.pallas import tpu as pltpu
from jax.sharding import PartitionSpec as P

smooth_width = 0.25
pair_weight = 0.95

slabs = 16
pitch = 160
own = 16
wide = 144
chunk = 40
chunk_pitch = 50
lat_pitch = 34
edge_rows = 56

f32 = jnp.float32
bf16 = jnp.bfloat16


def lanes_of(shape):
    return lax.broadcasted_iota(jnp.int32, shape, len(shape) - 1)


def dot(left, right, left_dim, right_dim):
    return lax.dot_general(
        left, right, (((left_dim,), (right_dim,)), ((), ())), preferred_element_type=f32
    )


def rounded(value):
    return value.astype(bf16).astype(f32)


def wrap_slabs(ref):
    last = pltpu.roll(ref[slabs], 64, 1)
    ref[0] = jnp.where(lanes_of(last.shape) >= 64, last, 0.0)
    first = pltpu.roll(ref[1], 64, 1)
    ref[slabs + 1] = jnp.where(lanes_of(first.shape) < 64, first, 0.0)


def both_halves(row):
    return jnp.concatenate([row, row], axis=1)


def each_slab(body):
    def step(p, carry):
        body(p)
        return carry

    lax.fori_loop(0, slabs, step, 0, unroll=True)


def fetch(sources, places, sems):
    copies = [
        pltpu.make_async_copy(source, place, sems.at[k])
        for k, (source, place) in enumerate(zip(sources, places))
    ]
    for copy in copies:
        copy.start()
    return copies


def edge_kernel(x_hbm, target_hbm, xt_ref, first_ref, last_ref, x_ref, target_ref, rows_scr, sems):
    target_copy, x_copy = fetch((target_hbm, x_hbm.at[0]), (target_ref, x_ref), sems)
    target_copy.wait()
    for k in range(4):
        turned = target_ref[4 * k : 4 * k + 4].reshape(128, 128).T
        first_ref[48 + k : 49 + k, :] = turned[0:1]
        last_ref[48 + k : 49 + k, :] = turned[127:128]
    first_ref[52:56, :] = jnp.zeros((4, 128), f32)
    last_ref[52:56, :] = jnp.zeros((4, 128), f32)
    x_copy.wait()
    for c in range(64):
        rows_scr[lat_pitch * c : lat_pitch * c + 32, :] = x_ref[c].astype(f32)

    def body(p):
        here = jnp.concatenate(
            [rows_scr[pl.ds(p, 64, stride=lat_pitch), :], rows_scr[pl.ds(p + 16, 64, stride=lat_pitch), :]],
            axis=0,
        )
        turned = here.T
        xt_ref[p] = turned
        for j in range(3):
            first_ref[pl.ds(16 * j + p, 1), :] = turned[j : j + 1]
            last_ref[pl.ds(16 * j + p, 1), :] = turned[125 + j : 126 + j]

    each_slab(body)


def main_kernel(
    depth_one_hbm, point_one_hbm, bias_one_hbm, depth_two_hbm, point_two_hbm, bias_two_hbm, xt_ref,
    columns_ref,
    taps_one_ref, one_ref, one_turned_ref, bias_one_ref, taps_two_ref, two_ref, bias_two_ref,
    first_ref, gate_ref, hidden_ref, hs_ref, columns_out_ref,
    d1_ref, p1_ref, b1_ref, d2_ref, p2_ref, b2_ref, turn_ref, xs_ref, sems,
):
    columns_out_ref[...] = columns_ref[...]
    places = (d1_ref, p1_ref, b1_ref, d2_ref, p2_ref, b2_ref)
    sources = (
        depth_one_hbm, point_one_hbm, bias_one_hbm, depth_two_hbm, point_two_hbm, bias_two_hbm
    )
    copies = fetch(sources, places, sems)
    turn_ref[...] = jnp.zeros((128, 128), f32)
    for ref in (xs_ref, hs_ref):
        for k in range(slabs + 2):
            ref[k, 0:8, :] = jnp.zeros((8, 128), f32)
            ref[k, 136:144, :] = jnp.zeros((8, 128), f32)
    for p in range(slabs):
        xs_ref[p + 1, 8:136, :] = xt_ref[p]
    wrap_slabs(xs_ref)
    for copy in copies:
        copy.wait()
    zero = jnp.zeros((7, 128), f32)
    taps_one_ref[...] = jnp.concatenate([both_halves(d1_ref[...]), zero], axis=0)
    taps_two_ref[...] = jnp.concatenate([both_halves(d2_ref[...]), zero], axis=0)
    bias_one_ref[...] = jnp.broadcast_to(both_halves(b1_ref[...]), (8, 128))
    turn_ref[0:1, 0:16] = b2_ref[...]
    column = jnp.broadcast_to(turn_ref[...].T[0:16, 0:1], (16, 128))
    bias_two_ref[0:16] = column
    bias_two_ref[16:32] = column
    turn_ref[0:1, :] = jnp.zeros((1, 128), f32)
    weight = p1_ref[...].astype(f32)
    turn_ref[0:64, 0:64] = weight
    turn_ref[64:128, 64:128] = weight
    one_ref[...] = turn_ref[...].astype(bf16)
    one_turned = turn_ref[...].T.astype(bf16)
    one_turned_ref[...] = one_turned
    weight = p2_ref[...].astype(f32)
    zero = jnp.zeros((16, 64), f32)
    two_ref[...] = jnp.concatenate(
        [jnp.concatenate([weight, zero], axis=1), jnp.concatenate([zero, weight], axis=1)], axis=0
    ).astype(bf16)

    def first_body(p):
        first = rounded(depthwise(taps_one_ref, xs_ref, p, 7, 128))
        first_ref[p] = first
        hidden, gate = activation(first, one_turned, bias_one_ref)
        hidden_ref[p] = hidden
        hs_ref[p + 1, 8:136, :] = hidden
        gate_ref[p] = gate

    each_slab(first_body)
    wrap_slabs(hs_ref)


def second_kernel(hs_ref, taps_ref, second_ref):
    def body(p):
        second_ref[p] = depthwise(taps_ref, hs_ref, p, 7, 128)

    each_slab(body)


def depthwise(taps_ref, ref, p, row, count):
    total = None
    for a in range(3):
        for b in range(3):
            tap = taps_ref[3 * a + b : 3 * a + b + 1, :]
            term = tap * ref[p + a, row + b : row + b + count, :]
            total = term if total is None else total + term
    return total


def activation(first, one_turned, bias_ref):
    pre = dot(first.astype(bf16), one_turned, 1, 0) + bias_ref[0:1]
    gate = 1.0 / (1.0 + jnp.exp(-pre))
    return rounded(pre * gate), gate * (1.0 + pre * (1.0 - gate))


def with_edges(main, edge):
    return jnp.concatenate([edge[0:8], main[8:120], edge[8:16]], axis=0)


def halo_kernel(
    xt_ref, left_ref, right_ref, hidden_ref, main_second_ref,
    taps_one_ref, one_turned_ref, bias_one_ref, taps_two_ref, two_ref, bias_ref,
    out_ref, send_ref, xs_ref, first_ref, gate_ref, edge_hidden_ref, second_ref,
    hs_ref, first_scr, y_ref, edge_ref,
):
    two = two_ref[...]

    for k in range(slabs + 2):
        xs_ref[k, 0:16, :] = jnp.zeros((16, 128), f32)
        xs_ref[k, 144:160, :] = jnp.zeros((16, 128), f32)
    for p in range(slabs):
        xs_ref[p + 1, own : own + 128, :] = xt_ref[p]
        for j in range(3):
            xs_ref[p + 1, 13 + j : 14 + j, :] = left_ref[16 * j + p : 16 * j + p + 1, :]
            xs_ref[p + 1, 144 + j : 145 + j, :] = right_ref[16 * j + p : 16 * j + p + 1, :]
    wrap_slabs(xs_ref)

    def first_body(p):
        first = jnp.concatenate(
            [depthwise(taps_one_ref, xs_ref, p, 7, 16), depthwise(taps_one_ref, xs_ref, p, 135, 16)],
            axis=0,
        )
        first_scr[pl.ds(32 * p, 32), :] = rounded(first)

    each_slab(first_body)
    first = first_scr[...]
    hidden, gate = activation(first, one_turned_ref[...], bias_one_ref)
    for p in range(slabs):
        rows = slice(32 * p + 8, 32 * p + 24)
        first_ref[p] = first[rows]
        gate_ref[p] = gate[rows]
        edge_hidden_ref[p] = hidden[rows]
        hs_ref[p + 1, 0:8, :] = jnp.zeros((8, 128), f32)
        hs_ref[p + 1, 8:24, :] = hidden[32 * p : 32 * p + 16]
        hs_ref[p + 1, 24:32, :] = hidden_ref[p, 8:16, :]
        hs_ref[p + 1, 32:40, :] = hidden_ref[p, 112:120, :]
        hs_ref[p + 1, 40:56, :] = hidden[32 * p + 16 : 32 * p + 32]
        hs_ref[p + 1, 56:64, :] = jnp.zeros((8, 128), f32)
    wrap_slabs(hs_ref)
    y_ref[...] = jnp.zeros(y_ref.shape, f32)
    edge_ref[...] = jnp.zeros(edge_ref.shape, f32)

    def second_body(p):
        before = depthwise(taps_two_ref, hs_ref, p, 7, 16)
        after = depthwise(taps_two_ref, hs_ref, p, 39, 16)
        edge_ref[pl.ds(p, 1), :] = before[7:8]
        edge_ref[pl.ds(16 + p, 1), :] = after[8:9]
        edge = jnp.concatenate([before[8:16], after[0:8]], axis=0)
        second = with_edges(main_second_ref[p], edge).astype(bf16)
        second_ref[p] = second
        y = dot(two, second, 1, 1) + bias_ref[...]
        y_ref[pl.ds(p, 16, stride=chunk_pitch), :] = y[0:16]
        y_ref[pl.ds(16 + p, 16, stride=chunk_pitch), :] = y[16:32]

    each_slab(second_body)
    y = dot(two, edge_ref[...].astype(bf16), 1, 1) + bias_ref[...]
    lane = lanes_of((16, 128))
    y = jnp.where(lane < 32, y[0:16], jnp.where(lane < 64, pltpu.roll(y[16:32], 32, 1), 0.0))
    y_ref[pl.ds(32, 16, stride=chunk_pitch), :] = y
    for o in range(16):
        send = y_ref[chunk_pitch * o : chunk_pitch * o + chunk, :].astype(bf16)
        send_ref[o] = send
        out_ref[0, o] = send[0:32]


def slope(diff):
    return diff * lax.rsqrt(diff * diff + smooth_width * smooth_width)


def crps_kernel(cells_all, x_ref, target_ref, left_ref, right_ref, out_ref):
    members = x_ref.shape[0]
    me = lax.axis_index("member")
    turn = lax.rem(4 - lax.rem(me, 4), 4) * 32
    left = left_ref[pl.ds(48 + me // 4, 1), :]
    right = right_ref[pl.ds(48 + me // 4, 1), :]
    left = pltpu.roll(jnp.broadcast_to(left, (8, 128)), turn, 1)
    right = pltpu.roll(jnp.broadcast_to(right, (8, 128)), turn, 1)
    lane = lanes_of((8, 128))
    halo = jnp.where(
        lane < 16,
        left,
        jnp.where(
            lane < 32,
            pltpu.roll(right, 16, 1),
            jnp.where(lane < 48, pltpu.roll(left, 16, 1), pltpu.roll(right, 32, 1)),
        ),
    )
    for rows in (slice(0, 16), slice(16, 32), slice(32, 40)):
        x = [x_ref[i, rows, :].astype(f32) for i in range(members)]
        total = [None] * members
        for i in range(members):
            for j in range(i + 1, members):
                s = slope(x[i] - x[j])
                total[i] = s if total[i] is None else total[i] + s
                total[j] = -s if total[j] is None else total[j] - s
        aim = halo if rows.start == 32 else target_ref[me, rows, :]
        for i in range(members):
            value = slope(x[i] - aim) - pair_weight / (members - 1) * total[i]
            out_ref[i, rows, :] = (value / cells_all).astype(bf16)


def tap_sum(value):
    return jnp.sum(value.reshape(16, 8, 128), axis=0)


def backward_kernel(
    cot_ref, xs_ref, first_ref, gate_ref, hidden_ref, edge_first_ref, edge_gate_ref, edge_hidden_ref,
    second_ref, one_ref, two_ref, taps_two_ref,
    out_ref,
    cf_ref, bs_ref, sums_ref, cot_sum_ref, point_two_ref, point_one_ref, other_ref,
):
    for o in range(16):
        cf_ref[chunk_pitch * o : chunk_pitch * o + chunk, :] = cot_ref[o].astype(f32)
    two = two_ref[...]
    one = one_ref[...]
    sums_ref[...] = jnp.zeros(sums_ref.shape, f32)
    cot_sum_ref[...] = jnp.zeros(cot_sum_ref.shape, f32)
    point_two_ref[...] = jnp.zeros(point_two_ref.shape, f32)
    point_one_ref[...] = jnp.zeros(point_one_ref.shape, f32)
    other_ref[...] = jnp.zeros(other_ref.shape, f32)

    def cot_body(p):
        cot = jnp.concatenate(
            [cf_ref[pl.ds(p, 16, stride=chunk_pitch), :], cf_ref[pl.ds(16 + p, 16, stride=chunk_pitch), :]], axis=0
        )
        cot_sum_ref[0:32] += cot
        cot = cot.astype(bf16)
        bs_ref[p + 1, own : own + 128, :] = rounded(dot(cot, two, 0, 0))
        point_two_ref[...] += dot(cot, second_ref[p], 1, 0)

    each_slab(cot_body)
    halo = cf_ref[pl.ds(32, 16, stride=chunk_pitch), :]
    halo = jnp.concatenate([halo, pltpu.roll(halo, 96, 1)], axis=0).astype(bf16)
    halo = rounded(dot(halo, two, 0, 0))
    for p in range(slabs):
        bs_ref[p + 1, 15:16, :] = halo[p : p + 1]
        bs_ref[p + 1, 144:145, :] = halo[16 + p : 17 + p]
    wrap_slabs(bs_ref)

    def body(p):
        total = None
        hidden = with_edges(hidden_ref[p], edge_hidden_ref[p])
        for a in range(3):
            for b in range(3):
                t = 3 * a + b
                back = bs_ref[p + 2 - a, 17 - b : 145 - b, :]
                term = taps_two_ref[t : t + 1, :] * back
                total = term if total is None else total + term
                sums_ref[9 + t] += tap_sum(back * hidden)
        back_pre = (total * with_edges(gate_ref[p], edge_gate_ref[p])).astype(bf16)
        sums_ref[18] += tap_sum(back_pre.astype(f32))
        first = with_edges(first_ref[p], edge_first_ref[p]).astype(bf16)
        point_one_ref[...] += dot(back_pre, first, 0, 0)
        back_first = dot(back_pre, one, 1, 0)
        for a in range(3):
            for b in range(3):
                sums_ref[3 * a + b] += tap_sum(back_first * xs_ref[p + a, 15 + b : 143 + b, :])

    each_slab(body)
    for t in range(19):
        total = jnp.sum(sums_ref[t], axis=0, keepdims=True)
        other_ref[t : t + 1, :] = total + pltpu.roll(total, 64, 1)
    other_ref[24:40, :] = pltpu.roll(point_two_ref[0:16], 64, 1) + point_two_ref[16:32]
    bias_two = jnp.sum(cot_sum_ref[...].T, axis=0, keepdims=True)
    bias_two = bias_two + pltpu.roll(bias_two, 112, 1)
    other_ref[19:20, :] = pltpu.roll(bias_two, 64, 1)
    point_one = point_one_ref[0:64] + pltpu.roll(point_one_ref[64:128], 64, 1)
    packed = jnp.where(lanes_of((64, 128)) < 64, point_one, other_ref[...])
    out_ref[...] = packed.reshape(out_ref.shape)


def output_kernel(total_ref, depth_one_ref, point_one_ref, bias_one_ref, depth_two_ref, point_two_ref, bias_two_ref, rows_ref):
    rows_ref[...] = total_ref[...].reshape(64, 128)
    point_one_ref[...] = rows_ref[:, 0:64]
    depth_one_ref[...] = rows_ref[0:9, 64:128]
    depth_two_ref[...] = rows_ref[9:18, 64:128]
    bias_one_ref[...] = rows_ref[18:19, 64:128]
    bias_two_ref[...] = rows_ref[19:20, 64:80]
    point_two_ref[...] = rows_ref[24:40, 64:128]


def call(kernel, out_shape, scratch, flops, fetched=0, passed=0):
    hbm = pl.BlockSpec(memory_space=pltpu.HBM)
    vmem = pl.BlockSpec(memory_space=pltpu.VMEM)
    return pl.pallas_call(
        kernel,
        out_shape=out_shape,
        in_specs=[hbm] * fetched + [vmem] * passed,
        scratch_shapes=scratch,
        compiler_params=pltpu.CompilerParams(vmem_limit_bytes=24 * 1024 * 1024),
        cost_estimate=pl.CostEstimate(flops=flops, bytes_accessed=4 << 20, transcendentals=0),
    )


def in_hbm(*arrays):
    return [pltpu.with_memory_space_constraint(array, pltpu.HBM) for array in arrays]


def shape(dims, dtype):
    return jax.ShapeDtypeStruct(dims, dtype)


def local(predictor_inputs, target, depth_one, point_one, bias_one, depth_two, point_two, bias_two):
    members = lax.axis_size("member")
    tiles = lax.axis_size("tile")
    _, chans, rows, cols = predictor_inputs.shape
    slab = (slabs, cols, 128)
    xt, first_cols, last_cols = call(
        edge_kernel,
        (shape(slab, f32), shape((edge_rows, 128), f32), shape((edge_rows, 128), f32)),
        [
            pltpu.VMEM((chans, rows, cols), bf16),
            pltpu.VMEM((16, rows, cols), f32),
            pltpu.VMEM((chans * lat_pitch, 128), f32),
            pltpu.SemaphoreType.DMA((2,)),
        ],
        1 << 20,
        fetched=2,
    )(*in_hbm(predictor_inputs, target))
    up = [(i, (i + 1) % tiles) for i in range(tiles)]
    left = lax.ppermute(last_cols, "tile", up)
    (
        taps_one, one, one_turned, bias_one, taps_two, two, bias_two,
        first, gate, hidden, hs, first_cols,
    ) = call(
        main_kernel,
        (
            shape((16, 128), f32),
            shape((128, 128), bf16),
            shape((128, 128), bf16),
            shape((8, 128), f32),
            shape((16, 128), f32),
            shape((32, 128), bf16),
            shape((32, 128), f32),
            shape(slab, f32),
            shape(slab, f32),
            shape(slab, f32),
            shape((slabs + 2, wide, 128), f32),
            shape((edge_rows, 128), f32),
        ),
        [
            pltpu.VMEM((9, 64), f32),
            pltpu.VMEM((64, 64), bf16),
            pltpu.VMEM((1, 64), f32),
            pltpu.VMEM((9, 64), f32),
            pltpu.VMEM((16, 64), bf16),
            pltpu.VMEM((1, 16), f32),
            pltpu.VMEM((128, 128), f32),
            pltpu.VMEM((slabs + 2, wide, 128), f32),
            pltpu.SemaphoreType.DMA((6,)),
        ],
        1 << 28,
        fetched=6,
        passed=2,
    )(
        *in_hbm(
            depth_one.T, point_one, bias_one[None], depth_two.T, point_two, bias_two[None]
        ),
        xt,
        first_cols,
    )
    right = lax.ppermute(first_cols, "tile", [(j, i) for i, j in up])
    main_second = call(second_kernel, shape(slab, f32), [], 1 << 27, passed=2)(hs, taps_two)
    edge = (slabs, 16, 128)
    out, send, xs, edge_first, edge_gate, edge_hidden, second = call(
        halo_kernel,
        (
            shape((1, 16, rows, cols), bf16),
            shape((16, chunk, 128), bf16),
            shape((slabs + 2, pitch, 128), f32),
            shape(edge, f32),
            shape(edge, f32),
            shape(edge, f32),
            shape(slab, bf16),
        ),
        [
            pltpu.VMEM((slabs + 2, 64, 128), f32),
            pltpu.VMEM((32 * slabs, 128), f32),
            pltpu.VMEM((16 * chunk_pitch, 128), f32),
            pltpu.VMEM((128, 128), f32),
        ],
        1 << 27,
        passed=11,
    )(
        xt, left, right, hidden, main_second, taps_one, one_turned, bias_one, taps_two, two, bias_two
    )
    seen = lax.all_to_all(send, "member", 0, 0, tiled=True)
    cot = call(
        functools.partial(crps_kernel, rows * cols * tiles),
        shape((members, chunk, 128), bf16),
        [],
        1 << 24,
        passed=4,
    )(seen, target, left, right)
    cot = lax.all_to_all(cot, "member", 0, 0, tiled=True)
    packed = call(
        backward_kernel,
        shape((16, 4, 128), f32),
        [
            pltpu.VMEM((16 * chunk_pitch, 128), f32),
            pltpu.VMEM((slabs + 2, pitch, 128), f32),
            pltpu.VMEM((19, 8, 128), f32),
            pltpu.VMEM((128, 128), f32),
            pltpu.VMEM((32, 128), f32),
            pltpu.VMEM((128, 128), f32),
            pltpu.VMEM((64, 128), f32),
        ],
        1 << 28,
        passed=12,
    )(
        cot, xs, first, gate, hidden, edge_first, edge_gate, edge_hidden, second, one, two, taps_two
    )
    axes = ("member", "tile")
    near = [[16 * g + k for k in range(16)] for g in range(members * tiles // 16)]
    far = [list(group) for group in zip(*near)]
    part = lax.all_to_all(packed, axes, 0, 0, tiled=True, axis_index_groups=near)
    part = jnp.sum(part, axis=0)
    part = jnp.broadcast_to(part[None], (len(near),) + part.shape)
    part = lax.all_to_all(part, axes, 0, 0, tiled=True, axis_index_groups=far)
    part = jnp.sum(part, axis=0)
    part = jnp.broadcast_to(part[None], (len(far),) + part.shape)
    total = lax.all_to_all(part, axes, 0, 0, tiled=True, axis_index_groups=near)
    g_depth_one, g_point_one, g_bias_one, g_depth_two, g_point_two, g_bias_two = call(
        output_kernel,
        (
            shape((9, 64), f32),
            shape((64, 64), f32),
            shape((1, 64), f32),
            shape((9, 64), f32),
            shape((16, 64), f32),
            shape((1, 16), f32),
        ),
        [pltpu.VMEM((64, 128), f32)],
        1 << 20,
        passed=1,
    )(total)
    return (
        out,
        g_depth_one.T,
        g_point_one,
        g_bias_one[0],
        g_depth_two.T,
        g_point_two,
        g_bias_two[0],
    )


def solution(mesh):
    return jax.shard_map(
        local,
        mesh=mesh,
        in_specs=(
            P("member", None, None, "tile"),
            P(None, None, "tile"),
            P(),
            P(),
            P(),
            P(),
            P(),
            P(),
        ),
        out_specs=(P("member", None, None, "tile"), P(), P(), P(), P(), P(), P()),
        check_vma=False,
    )
```

```python
import functools

import jax
import jax.numpy as jnp
from jax import lax
from jax.experimental import pallas as pl
from jax.experimental.pallas import tpu as pltpu
from jax.sharding import PartitionSpec as P

smooth_width = 0.25
pair_weight = 0.95

slabs = 16
pitch = 160
own = 16
wide = 144
chunk = 40
chunk_pitch = 50
lat_pitch = 34
edge_rows = 56

f32 = jnp.float32
bf16 = jnp.bfloat16


def lanes_of(shape):
    return lax.broadcasted_iota(jnp.int32, shape, len(shape) - 1)


def dot(left, right, left_dim, right_dim):
    return lax.dot_general(
        left, right, (((left_dim,), (right_dim,)), ((), ())), preferred_element_type=f32
    )


def rounded(value):
    return value.astype(bf16).astype(f32)


def wrap_slabs(ref):
    last = pltpu.roll(ref[slabs], 64, 1)
    ref[0] = jnp.where(lanes_of(last.shape) >= 64, last, 0.0)
    first = pltpu.roll(ref[1], 64, 1)
    ref[slabs + 1] = jnp.where(lanes_of(first.shape) < 64, first, 0.0)


def both_halves(row):
    return jnp.concatenate([row, row], axis=1)


def each_slab(body):
    def step(p, carry):
        body(p)
        return carry

    lax.fori_loop(0, slabs, step, 0, unroll=True)


def fetch(sources, places, sems):
    copies = [
        pltpu.make_async_copy(source, place, sems.at[k])
        for k, (source, place) in enumerate(zip(sources, places))
    ]
    for copy in copies:
        copy.start()
    return copies


def even_tile():
    return lax.rem(lax.axis_index("tile"), 2) == 0


def edge_kernel(
    x_hbm, target_hbm, xt_ref, outer_ref, inner_ref,
    x_ref, target_ref, rows_scr, first_ref, last_ref, sems,
):
    target_copy, x_copy = fetch((target_hbm, x_hbm.at[0]), (target_ref, x_ref), sems)
    target_copy.wait()
    for k in range(4):
        turned = target_ref[4 * k : 4 * k + 4].reshape(128, 128).T
        first_ref[48 + k : 49 + k, :] = turned[0:1]
        last_ref[48 + k : 49 + k, :] = turned[127:128]
    first_ref[52:56, :] = jnp.zeros((4, 128), f32)
    last_ref[52:56, :] = jnp.zeros((4, 128), f32)
    x_copy.wait()
    for c in range(64):
        rows_scr[lat_pitch * c : lat_pitch * c + 32, :] = x_ref[c].astype(f32)

    def body(p):
        here = jnp.concatenate(
            [rows_scr[pl.ds(p, 64, stride=lat_pitch), :], rows_scr[pl.ds(p + 16, 64, stride=lat_pitch), :]],
            axis=0,
        )
        turned = here.T
        xt_ref[p] = turned
        for j in range(3):
            first_ref[pl.ds(16 * j + p, 1), :] = turned[j : j + 1]
            last_ref[pl.ds(16 * j + p, 1), :] = turned[125 + j : 126 + j]

    each_slab(body)
    even = even_tile()
    first, last = first_ref[...], last_ref[...]
    outer_ref[...] = jnp.where(even, first, last)
    inner_ref[...] = jnp.where(even, last, first)


def main_kernel(
    depth_one_hbm, point_one_hbm, bias_one_hbm, depth_two_hbm, point_two_hbm, bias_two_hbm, xt_ref,
    taps_one_ref, one_ref, one_turned_ref, bias_one_ref, taps_two_ref, two_ref, bias_two_ref,
    first_ref, gate_ref, hidden_ref, second_ref,
    d1_ref, p1_ref, b1_ref, d2_ref, p2_ref, b2_ref, turn_ref, xs_ref, hs_ref, sems,
):
    places = (d1_ref, p1_ref, b1_ref, d2_ref, p2_ref, b2_ref)
    sources = (
        depth_one_hbm, point_one_hbm, bias_one_hbm, depth_two_hbm, point_two_hbm, bias_two_hbm
    )
    copies = fetch(sources, places, sems)
    turn_ref[...] = jnp.zeros((128, 128), f32)
    for ref in (xs_ref, hs_ref):
        for k in range(slabs + 2):
            ref[k, 0:8, :] = jnp.zeros((8, 128), f32)
            ref[k, 136:144, :] = jnp.zeros((8, 128), f32)
    for p in range(slabs):
        xs_ref[p + 1, 8:136, :] = xt_ref[p]
    wrap_slabs(xs_ref)
    for copy in copies:
        copy.wait()
    zero = jnp.zeros((7, 128), f32)
    taps_one_ref[...] = jnp.concatenate([both_halves(d1_ref[...]), zero], axis=0)
    taps_two_ref[...] = jnp.concatenate([both_halves(d2_ref[...]), zero], axis=0)
    bias_one_ref[...] = jnp.broadcast_to(both_halves(b1_ref[...]), (8, 128))
    turn_ref[0:1, 0:16] = b2_ref[...]
    column = jnp.broadcast_to(turn_ref[...].T[0:16, 0:1], (16, 128))
    bias_two_ref[0:16] = column
    bias_two_ref[16:32] = column
    turn_ref[0:1, :] = jnp.zeros((1, 128), f32)
    weight = p1_ref[...].astype(f32)
    turn_ref[0:64, 0:64] = weight
    turn_ref[64:128, 64:128] = weight
    one_ref[...] = turn_ref[...].astype(bf16)
    one_turned = turn_ref[...].T.astype(bf16)
    one_turned_ref[...] = one_turned
    weight = p2_ref[...].astype(f32)
    zero = jnp.zeros((16, 64), f32)
    two_ref[...] = jnp.concatenate(
        [jnp.concatenate([weight, zero], axis=1), jnp.concatenate([zero, weight], axis=1)], axis=0
    ).astype(bf16)

    def first_body(p):
        first = rounded(depthwise(taps_one_ref, xs_ref, p, 7, 128))
        first_ref[p] = first
        hidden, gate = activation(first, one_turned, bias_one_ref)
        hidden_ref[p] = hidden
        hs_ref[p + 1, 8:136, :] = hidden
        gate_ref[p] = gate

    def second_body(p):
        second_ref[p] = depthwise(taps_two_ref, hs_ref, p, 7, 128)

    each_slab(first_body)
    wrap_slabs(hs_ref)
    each_slab(second_body)


def depthwise(taps_ref, ref, p, row, count):
    total = None
    for a in range(3):
        for b in range(3):
            tap = taps_ref[3 * a + b : 3 * a + b + 1, :]
            term = tap * ref[p + a, row + b : row + b + count, :]
            total = term if total is None else total + term
    return total


def activation(first, one_turned, bias_ref):
    pre = dot(first.astype(bf16), one_turned, 1, 0) + bias_ref[0:1]
    gate = 1.0 / (1.0 + jnp.exp(-pre))
    return rounded(pre * gate), gate * (1.0 + pre * (1.0 - gate))


def with_edges(main, edge):
    return jnp.concatenate([edge[0:8], main[8:120], edge[8:16]], axis=0)


def halo_kernel(
    xt_ref, outer_ref, inner_ref, hidden_ref, main_second_ref,
    taps_one_ref, one_turned_ref, bias_one_ref, taps_two_ref, two_ref, bias_ref,
    out_ref, send_ref, xs_ref, first_ref, gate_ref, edge_hidden_ref, second_ref,
    hs_ref, first_scr, y_ref, edge_ref, left_ref, right_ref,
):
    two = two_ref[...]
    even = even_tile()
    outer, inner = outer_ref[...], inner_ref[...]
    left_ref[...] = jnp.where(even, outer, inner)
    right_ref[...] = jnp.where(even, inner, outer)

    for k in range(slabs + 2):
        xs_ref[k, 0:16, :] = jnp.zeros((16, 128), f32)
        xs_ref[k, 144:160, :] = jnp.zeros((16, 128), f32)
    for p in range(slabs):
        xs_ref[p + 1, own : own + 128, :] = xt_ref[p]
        for j in range(3):
            xs_ref[p + 1, 13 + j : 14 + j, :] = left_ref[16 * j + p : 16 * j + p + 1, :]
            xs_ref[p + 1, 144 + j : 145 + j, :] = right_ref[16 * j + p : 16 * j + p + 1, :]
    wrap_slabs(xs_ref)

    def first_body(p):
        first = jnp.concatenate(
            [depthwise(taps_one_ref, xs_ref, p, 7, 16), depthwise(taps_one_ref, xs_ref, p, 135, 16)],
            axis=0,
        )
        first_scr[pl.ds(32 * p, 32), :] = rounded(first)

    each_slab(first_body)
    first = first_scr[...]
    hidden, gate = activation(first, one_turned_ref[...], bias_one_ref)
    for p in range(slabs):
        rows = slice(32 * p + 8, 32 * p + 24)
        first_ref[p] = first[rows]
        gate_ref[p] = gate[rows]
        edge_hidden_ref[p] = hidden[rows]
        hs_ref[p + 1, 0:8, :] = jnp.zeros((8, 128), f32)
        hs_ref[p + 1, 8:24, :] = hidden[32 * p : 32 * p + 16]
        hs_ref[p + 1, 24:32, :] = hidden_ref[p, 8:16, :]
        hs_ref[p + 1, 32:40, :] = hidden_ref[p, 112:120, :]
        hs_ref[p + 1, 40:56, :] = hidden[32 * p + 16 : 32 * p + 32]
        hs_ref[p + 1, 56:64, :] = jnp.zeros((8, 128), f32)
    wrap_slabs(hs_ref)
    y_ref[...] = jnp.zeros(y_ref.shape, f32)
    edge_ref[...] = jnp.zeros(edge_ref.shape, f32)

    def second_body(p):
        before = depthwise(taps_two_ref, hs_ref, p, 7, 16)
        after = depthwise(taps_two_ref, hs_ref, p, 39, 16)
        edge_ref[pl.ds(p, 1), :] = before[7:8]
        edge_ref[pl.ds(16 + p, 1), :] = after[8:9]
        edge = jnp.concatenate([before[8:16], after[0:8]], axis=0)
        second = with_edges(main_second_ref[p], edge).astype(bf16)
        second_ref[p] = second
        y = dot(two, second, 1, 1) + bias_ref[...]
        y_ref[pl.ds(p, 16, stride=chunk_pitch), :] = y[0:16]
        y_ref[pl.ds(16 + p, 16, stride=chunk_pitch), :] = y[16:32]

    each_slab(second_body)
    y = dot(two, edge_ref[...].astype(bf16), 1, 1) + bias_ref[...]
    lane = lanes_of((16, 128))
    y = jnp.where(lane < 32, y[0:16], jnp.where(lane < 64, pltpu.roll(y[16:32], 32, 1), 0.0))
    y_ref[pl.ds(32, 16, stride=chunk_pitch), :] = y
    for o in range(16):
        send = y_ref[chunk_pitch * o : chunk_pitch * o + chunk, :].astype(bf16)
        send_ref[o] = send
        out_ref[0, o] = send[0:32]


def slope(diff):
    return diff * lax.rsqrt(diff * diff + smooth_width * smooth_width)


def crps_kernel(cells_all, x_ref, target_ref, outer_ref, inner_ref, out_ref):
    members = x_ref.shape[0]
    me = lax.axis_index("member")
    turn = lax.rem(4 - lax.rem(me, 4), 4) * 32
    even = even_tile()
    outer = outer_ref[pl.ds(48 + me // 4, 1), :]
    inner = inner_ref[pl.ds(48 + me // 4, 1), :]
    left = jnp.where(even, outer, inner)
    right = jnp.where(even, inner, outer)
    left = pltpu.roll(jnp.broadcast_to(left, (8, 128)), turn, 1)
    right = pltpu.roll(jnp.broadcast_to(right, (8, 128)), turn, 1)
    lane = lanes_of((8, 128))
    halo = jnp.where(
        lane < 16,
        left,
        jnp.where(
            lane < 32,
            pltpu.roll(right, 16, 1),
            jnp.where(lane < 48, pltpu.roll(left, 16, 1), pltpu.roll(right, 32, 1)),
        ),
    )
    for rows in (slice(0, 16), slice(16, 32), slice(32, 40)):
        x = [x_ref[i, rows, :].astype(f32) for i in range(members)]
        total = [None] * members
        for i in range(members):
            for j in range(i + 1, members):
                s = slope(x[i] - x[j])
                total[i] = s if total[i] is None else total[i] + s
                total[j] = -s if total[j] is None else total[j] - s
        aim = halo if rows.start == 32 else target_ref[me, rows, :]
        for i in range(members):
            value = slope(x[i] - aim) - pair_weight / (members - 1) * total[i]
            out_ref[i, rows, :] = (value / cells_all).astype(bf16)


def tap_sum(value):
    return jnp.sum(value.reshape(16, 8, 128), axis=0)


def backward_kernel(
    cot_ref, xs_ref, first_ref, gate_ref, hidden_ref, edge_first_ref, edge_gate_ref, edge_hidden_ref,
    second_ref, one_ref, two_ref, taps_two_ref,
    out_ref,
    cf_ref, bs_ref, sums_ref, cot_sum_ref, point_two_ref, point_one_ref, other_ref,
):
    for o in range(16):
        cf_ref[chunk_pitch * o : chunk_pitch * o + chunk, :] = cot_ref[o].astype(f32)
    two = two_ref[...]
    one = one_ref[...]
    sums_ref[...] = jnp.zeros(sums_ref.shape, f32)
    cot_sum_ref[...] = jnp.zeros(cot_sum_ref.shape, f32)
    point_two_ref[...] = jnp.zeros(point_two_ref.shape, f32)
    point_one_ref[...] = jnp.zeros(point_one_ref.shape, f32)
    other_ref[...] = jnp.zeros(other_ref.shape, f32)

    def cot_body(p):
        cot = jnp.concatenate(
            [cf_ref[pl.ds(p, 16, stride=chunk_pitch), :], cf_ref[pl.ds(16 + p, 16, stride=chunk_pitch), :]], axis=0
        )
        cot_sum_ref[0:32] += cot
        cot = cot.astype(bf16)
        bs_ref[p + 1, own : own + 128, :] = rounded(dot(cot, two, 0, 0))
        point_two_ref[...] += dot(cot, second_ref[p], 1, 0)

    each_slab(cot_body)
    halo = cf_ref[pl.ds(32, 16, stride=chunk_pitch), :]
    halo = jnp.concatenate([halo, pltpu.roll(halo, 96, 1)], axis=0).astype(bf16)
    halo = rounded(dot(halo, two, 0, 0))
    for p in range(slabs):
        bs_ref[p + 1, 15:16, :] = halo[p : p + 1]
        bs_ref[p + 1, 144:145, :] = halo[16 + p : 17 + p]
    wrap_slabs(bs_ref)

    def body(p):
        total = None
        hidden = with_edges(hidden_ref[p], edge_hidden_ref[p])
        for a in range(3):
            for b in range(3):
                t = 3 * a + b
                back = bs_ref[p + 2 - a, 17 - b : 145 - b, :]
                term = taps_two_ref[t : t + 1, :] * back
                total = term if total is None else total + term
                sums_ref[9 + t] += tap_sum(back * hidden)
        back_pre = (total * with_edges(gate_ref[p], edge_gate_ref[p])).astype(bf16)
        sums_ref[18] += tap_sum(back_pre.astype(f32))
        first = with_edges(first_ref[p], edge_first_ref[p]).astype(bf16)
        point_one_ref[...] += dot(back_pre, first, 0, 0)
        back_first = dot(back_pre, one, 1, 0)
        for a in range(3):
            for b in range(3):
                sums_ref[3 * a + b] += tap_sum(back_first * xs_ref[p + a, 15 + b : 143 + b, :])

    each_slab(body)
    for t in range(19):
        total = jnp.sum(sums_ref[t], axis=0, keepdims=True)
        other_ref[t : t + 1, :] = total + pltpu.roll(total, 64, 1)
    other_ref[24:40, :] = pltpu.roll(point_two_ref[0:16], 64, 1) + point_two_ref[16:32]
    bias_two = jnp.sum(cot_sum_ref[...].T, axis=0, keepdims=True)
    bias_two = bias_two + pltpu.roll(bias_two, 112, 1)
    other_ref[19:20, :] = pltpu.roll(bias_two, 64, 1)
    point_one = point_one_ref[0:64] + pltpu.roll(point_one_ref[64:128], 64, 1)
    packed = jnp.where(lanes_of((64, 128)) < 64, point_one, other_ref[...])
    out_ref[...] = packed.reshape(out_ref.shape)


def output_kernel(total_ref, depth_one_ref, point_one_ref, bias_one_ref, depth_two_ref, point_two_ref, bias_two_ref, rows_ref):
    rows_ref[...] = total_ref[...].reshape(64, 128)
    point_one_ref[...] = rows_ref[:, 0:64]
    depth_one_ref[...] = rows_ref[0:9, 64:128]
    depth_two_ref[...] = rows_ref[9:18, 64:128]
    bias_one_ref[...] = rows_ref[18:19, 64:128]
    bias_two_ref[...] = rows_ref[19:20, 64:80]
    point_two_ref[...] = rows_ref[24:40, 64:128]


def call(kernel, out_shape, scratch, flops, fetched=0, passed=0):
    hbm = pl.BlockSpec(memory_space=pltpu.HBM)
    vmem = pl.BlockSpec(memory_space=pltpu.VMEM)
    return pl.pallas_call(
        kernel,
        out_shape=out_shape,
        in_specs=[hbm] * fetched + [vmem] * passed,
        scratch_shapes=scratch,
        compiler_params=pltpu.CompilerParams(vmem_limit_bytes=24 * 1024 * 1024),
        cost_estimate=pl.CostEstimate(flops=flops, bytes_accessed=4 << 20, transcendentals=0),
    )


def in_hbm(*arrays):
    return [pltpu.with_memory_space_constraint(array, pltpu.HBM) for array in arrays]


def shape(dims, dtype):
    return jax.ShapeDtypeStruct(dims, dtype)


def local(predictor_inputs, target, depth_one, point_one, bias_one, depth_two, point_two, bias_two):
    members = lax.axis_size("member")
    tiles = lax.axis_size("tile")
    _, chans, rows, cols = predictor_inputs.shape
    slab = (slabs, cols, 128)
    xt, outer, inner = call(
        edge_kernel,
        (shape(slab, f32), shape((edge_rows, 128), f32), shape((edge_rows, 128), f32)),
        [
            pltpu.VMEM((chans, rows, cols), bf16),
            pltpu.VMEM((16, rows, cols), f32),
            pltpu.VMEM((chans * lat_pitch, 128), f32),
            pltpu.VMEM((edge_rows, 128), f32),
            pltpu.VMEM((edge_rows, 128), f32),
            pltpu.SemaphoreType.DMA((2,)),
        ],
        1 << 20,
        fetched=2,
    )(*in_hbm(predictor_inputs, target))
    outer = lax.ppermute(outer, "tile", [(i, (i + 2 * (i % 2) - 1) % tiles) for i in range(tiles)])
    inner = lax.ppermute(inner, "tile", [(i, i + 1 - 2 * (i % 2)) for i in range(tiles)])
    (
        taps_one, one, one_turned, bias_one, taps_two, two, bias_two,
        first, gate, hidden, main_second,
    ) = call(
        main_kernel,
        (
            shape((16, 128), f32),
            shape((128, 128), bf16),
            shape((128, 128), bf16),
            shape((8, 128), f32),
            shape((16, 128), f32),
            shape((32, 128), bf16),
            shape((32, 128), f32),
            shape(slab, f32),
            shape(slab, f32),
            shape(slab, f32),
            shape(slab, f32),
        ),
        [
            pltpu.VMEM((9, 64), f32),
            pltpu.VMEM((64, 64), bf16),
            pltpu.VMEM((1, 64), f32),
            pltpu.VMEM((9, 64), f32),
            pltpu.VMEM((16, 64), bf16),
            pltpu.VMEM((1, 16), f32),
            pltpu.VMEM((128, 128), f32),
            pltpu.VMEM((slabs + 2, wide, 128), f32),
            pltpu.VMEM((slabs + 2, wide, 128), f32),
            pltpu.SemaphoreType.DMA((6,)),
        ],
        1 << 28,
        fetched=6,
        passed=1,
    )(
        *in_hbm(
            depth_one.T, point_one, bias_one[None], depth_two.T, point_two, bias_two[None]
        ),
        xt,
    )
    edge = (slabs, 16, 128)
    out, send, xs, edge_first, edge_gate, edge_hidden, second = call(
        halo_kernel,
        (
            shape((1, 16, rows, cols), bf16),
            shape((16, chunk, 128), bf16),
            shape((slabs + 2, pitch, 128), f32),
            shape(edge, f32),
            shape(edge, f32),
            shape(edge, f32),
            shape(slab, bf16),
        ),
        [
            pltpu.VMEM((slabs + 2, 64, 128), f32),
            pltpu.VMEM((32 * slabs, 128), f32),
            pltpu.VMEM((16 * chunk_pitch, 128), f32),
            pltpu.VMEM((128, 128), f32),
            pltpu.VMEM((edge_rows, 128), f32),
            pltpu.VMEM((edge_rows, 128), f32),
        ],
        1 << 27,
        passed=11,
    )(
        xt, outer, inner, hidden, main_second, taps_one, one_turned, bias_one, taps_two, two, bias_two
    )
    seen = lax.all_to_all(send, "member", 0, 0, tiled=True)
    cot = call(
        functools.partial(crps_kernel, rows * cols * tiles),
        shape((members, chunk, 128), bf16),
        [],
        1 << 24,
        passed=4,
    )(seen, target, outer, inner)
    cot = lax.all_to_all(cot, "member", 0, 0, tiled=True)
    packed = call(
        backward_kernel,
        shape((16, 4, 128), f32),
        [
            pltpu.VMEM((16 * chunk_pitch, 128), f32),
            pltpu.VMEM((slabs + 2, pitch, 128), f32),
            pltpu.VMEM((19, 8, 128), f32),
            pltpu.VMEM((128, 128), f32),
            pltpu.VMEM((32, 128), f32),
            pltpu.VMEM((128, 128), f32),
            pltpu.VMEM((64, 128), f32),
        ],
        1 << 28,
        passed=12,
    )(
        cot, xs, first, gate, hidden, edge_first, edge_gate, edge_hidden, second, one, two, taps_two
    )
    axes = ("member", "tile")
    near = [[16 * g + k for k in range(16)] for g in range(members * tiles // 16)]
    far = [list(group) for group in zip(*near)]
    part = lax.all_to_all(packed, axes, 0, 0, tiled=True, axis_index_groups=near)
    part = jnp.sum(part, axis=0)
    part = jnp.broadcast_to(part[None], (len(near),) + part.shape)
    part = lax.all_to_all(part, axes, 0, 0, tiled=True, axis_index_groups=far)
    part = jnp.sum(part, axis=0)
    part = jnp.broadcast_to(part[None], (len(far),) + part.shape)
    total = lax.all_to_all(part, axes, 0, 0, tiled=True, axis_index_groups=near)
    g_depth_one, g_point_one, g_bias_one, g_depth_two, g_point_two, g_bias_two = call(
        output_kernel,
        (
            shape((9, 64), f32),
            shape((64, 64), f32),
            shape((1, 64), f32),
            shape((9, 64), f32),
            shape((16, 64), f32),
            shape((1, 16), f32),
        ),
        [pltpu.VMEM((64, 128), f32)],
        1 << 20,
        passed=1,
    )(total)
    return (
        out,
        g_depth_one.T,
        g_point_one,
        g_bias_one[0],
        g_depth_two.T,
        g_point_two,
        g_bias_two[0],
    )


def solution(mesh):
    return jax.shard_map(
        local,
        mesh=mesh,
        in_specs=(
            P("member", None, None, "tile"),
            P(None, None, "tile"),
            P(),
            P(),
            P(),
            P(),
            P(),
            P(),
        ),
        out_specs=(P("member", None, None, "tile"), P(), P(), P(), P(), P(), P()),
        check_vma=False,
    )
```

```python
import functools

import jax
import jax.numpy as jnp
from jax import lax
from jax.experimental import pallas as pl
from jax.experimental.pallas import tpu as pltpu
from jax.sharding import PartitionSpec as P

smooth_width = 0.25
pair_weight = 0.95

slabs = 16
pitch = 160
own = 16
wide = 144
chunk = 40
chunk_pitch = 50
lat_pitch = 34
edge_rows = 56

f32 = jnp.float32
bf16 = jnp.bfloat16


def lanes_of(shape):
    return lax.broadcasted_iota(jnp.int32, shape, len(shape) - 1)


def dot(left, right, left_dim, right_dim):
    return lax.dot_general(
        left, right, (((left_dim,), (right_dim,)), ((), ())), preferred_element_type=f32
    )


def rounded(value):
    return value.astype(bf16).astype(f32)


def wrap_slabs(ref):
    last = pltpu.roll(ref[slabs], 64, 1)
    ref[0] = jnp.where(lanes_of(last.shape) >= 64, last, 0.0)
    first = pltpu.roll(ref[1], 64, 1)
    ref[slabs + 1] = jnp.where(lanes_of(first.shape) < 64, first, 0.0)


def both_halves(row):
    return jnp.concatenate([row, row], axis=1)


def each_slab(body):
    def step(p, carry):
        body(p)
        return carry

    lax.fori_loop(0, slabs, step, 0, unroll=True)


def fetch(sources, places, sems):
    copies = [
        pltpu.make_async_copy(source, place, sems.at[k])
        for k, (source, place) in enumerate(zip(sources, places))
    ]
    for copy in copies:
        copy.start()
    return copies


def even_tile():
    return lax.rem(lax.axis_index("tile"), 2) == 0


def edge_kernel(
    x_hbm, target_hbm, depth_one_hbm, point_one_hbm, bias_one_hbm, depth_two_hbm, point_two_hbm,
    bias_two_hbm,
    xt_ref, outer_ref, inner_ref, d1_ref, p1_ref, b1_ref, d2_ref, p2_ref, b2_ref,
    x_ref, target_ref, rows_scr, first_ref, last_ref, sems,
):
    sources = (
        target_hbm, x_hbm.at[0], depth_one_hbm, point_one_hbm, bias_one_hbm, depth_two_hbm,
        point_two_hbm, bias_two_hbm,
    )
    places = (target_ref, x_ref, d1_ref, p1_ref, b1_ref, d2_ref, p2_ref, b2_ref)
    target_copy, x_copy, *weight_copies = fetch(sources, places, sems)
    target_copy.wait()
    for k in range(4):
        turned = target_ref[4 * k : 4 * k + 4].reshape(128, 128).T
        first_ref[48 + k : 49 + k, :] = turned[0:1]
        last_ref[48 + k : 49 + k, :] = turned[127:128]
    first_ref[52:56, :] = jnp.zeros((4, 128), f32)
    last_ref[52:56, :] = jnp.zeros((4, 128), f32)
    x_copy.wait()
    for c in range(64):
        rows_scr[lat_pitch * c : lat_pitch * c + 32, :] = x_ref[c].astype(f32)

    def body(p):
        here = jnp.concatenate(
            [rows_scr[pl.ds(p, 64, stride=lat_pitch), :], rows_scr[pl.ds(p + 16, 64, stride=lat_pitch), :]],
            axis=0,
        )
        turned = here.T
        xt_ref[p] = turned
        for j in range(3):
            first_ref[pl.ds(16 * j + p, 1), :] = turned[j : j + 1]
            last_ref[pl.ds(16 * j + p, 1), :] = turned[125 + j : 126 + j]

    each_slab(body)
    even = even_tile()
    first, last = first_ref[...], last_ref[...]
    outer_ref[...] = jnp.where(even, first, last)
    inner_ref[...] = jnp.where(even, last, first)
    for copy in weight_copies:
        copy.wait()


def main_kernel(
    d1_ref, p1_ref, b1_ref, d2_ref, p2_ref, b2_ref, xt_ref,
    taps_one_ref, one_ref, one_turned_ref, bias_one_ref, taps_two_ref, two_ref, bias_two_ref,
    first_ref, gate_ref, hidden_ref, second_ref,
    turn_ref, xs_ref, hs_ref,
):
    turn_ref[...] = jnp.zeros((128, 128), f32)
    for ref in (xs_ref, hs_ref):
        for k in range(slabs + 2):
            ref[k, 0:8, :] = jnp.zeros((8, 128), f32)
            ref[k, 136:144, :] = jnp.zeros((8, 128), f32)
    for p in range(slabs):
        xs_ref[p + 1, 8:136, :] = xt_ref[p]
    wrap_slabs(xs_ref)
    zero = jnp.zeros((7, 128), f32)
    taps_one_ref[...] = jnp.concatenate([both_halves(d1_ref[...]), zero], axis=0)
    taps_two_ref[...] = jnp.concatenate([both_halves(d2_ref[...]), zero], axis=0)
    bias_one_ref[...] = jnp.broadcast_to(both_halves(b1_ref[...]), (8, 128))
    turn_ref[0:1, 0:16] = b2_ref[...]
    column = jnp.broadcast_to(turn_ref[...].T[0:16, 0:1], (16, 128))
    bias_two_ref[0:16] = column
    bias_two_ref[16:32] = column
    turn_ref[0:1, :] = jnp.zeros((1, 128), f32)
    weight = p1_ref[...].astype(f32)
    turn_ref[0:64, 0:64] = weight
    turn_ref[64:128, 64:128] = weight
    one_ref[...] = turn_ref[...].astype(bf16)
    one_turned = turn_ref[...].T.astype(bf16)
    one_turned_ref[...] = one_turned
    weight = p2_ref[...].astype(f32)
    zero = jnp.zeros((16, 64), f32)
    two_ref[...] = jnp.concatenate(
        [jnp.concatenate([weight, zero], axis=1), jnp.concatenate([zero, weight], axis=1)], axis=0
    ).astype(bf16)

    def first_body(p):
        first = rounded(depthwise(taps_one_ref, xs_ref, p, 7, 128))
        first_ref[p] = first
        hidden, gate = activation(first, one_turned, bias_one_ref)
        hidden_ref[p] = hidden
        hs_ref[p + 1, 8:136, :] = hidden
        gate_ref[p] = gate

    def second_body(p):
        second_ref[p] = depthwise(taps_two_ref, hs_ref, p, 7, 128)

    each_slab(first_body)
    wrap_slabs(hs_ref)
    each_slab(second_body)


def depthwise(taps_ref, ref, p, row, count):
    total = None
    for a in range(3):
        for b in range(3):
            tap = taps_ref[3 * a + b : 3 * a + b + 1, :]
            term = tap * ref[p + a, row + b : row + b + count, :]
            total = term if total is None else total + term
    return total


def activation(first, one_turned, bias_ref):
    pre = dot(first.astype(bf16), one_turned, 1, 0) + bias_ref[0:1]
    gate = 1.0 / (1.0 + jnp.exp(-pre))
    return rounded(pre * gate), gate * (1.0 + pre * (1.0 - gate))


def with_edges(main, edge):
    return jnp.concatenate([edge[0:8], main[8:120], edge[8:16]], axis=0)


def halo_kernel(
    xt_ref, outer_ref, inner_ref, hidden_ref, main_second_ref,
    taps_one_ref, one_turned_ref, bias_one_ref, taps_two_ref, two_ref, bias_ref,
    out_ref, send_ref, xs_ref, first_ref, gate_ref, edge_hidden_ref, second_ref,
    hs_ref, y_ref, edge_ref, left_ref, right_ref,
):
    two = two_ref[...]
    even = even_tile()
    outer, inner = outer_ref[...], inner_ref[...]
    left_ref[...] = jnp.where(even, outer, inner)
    right_ref[...] = jnp.where(even, inner, outer)

    for k in range(slabs + 2):
        xs_ref[k, 0:16, :] = jnp.zeros((16, 128), f32)
        xs_ref[k, 144:160, :] = jnp.zeros((16, 128), f32)
    for p in range(slabs):
        xs_ref[p + 1, own : own + 128, :] = xt_ref[p]
        for j in range(3):
            xs_ref[p + 1, 13 + j : 14 + j, :] = left_ref[16 * j + p : 16 * j + p + 1, :]
            xs_ref[p + 1, 144 + j : 145 + j, :] = right_ref[16 * j + p : 16 * j + p + 1, :]
    wrap_slabs(xs_ref)

    one_turned = one_turned_ref[...]
    for k in range(0, slabs, 8):
        first = [
            depthwise(taps_one_ref, xs_ref, p, row, 16) for p in range(k, k + 8) for row in (7, 135)
        ]
        first = rounded(jnp.concatenate(first, axis=0))
        hidden, gate = activation(first, one_turned, bias_one_ref)
        for p in range(k, k + 8):
            at = 32 * (p - k)
            rows = slice(at + 8, at + 24)
            first_ref[p] = first[rows]
            gate_ref[p] = gate[rows]
            edge_hidden_ref[p] = hidden[rows]
            hs_ref[p + 1, 0:8, :] = jnp.zeros((8, 128), f32)
            hs_ref[p + 1, 8:24, :] = hidden[at : at + 16]
            hs_ref[p + 1, 24:32, :] = hidden_ref[p, 8:16, :]
            hs_ref[p + 1, 32:40, :] = hidden_ref[p, 112:120, :]
            hs_ref[p + 1, 40:56, :] = hidden[at + 16 : at + 32]
            hs_ref[p + 1, 56:64, :] = jnp.zeros((8, 128), f32)
    wrap_slabs(hs_ref)
    y_ref[...] = jnp.zeros(y_ref.shape, f32)
    edge_ref[...] = jnp.zeros(edge_ref.shape, f32)

    def second_body(p):
        before = depthwise(taps_two_ref, hs_ref, p, 7, 16)
        after = depthwise(taps_two_ref, hs_ref, p, 39, 16)
        edge_ref[pl.ds(p, 1), :] = before[7:8]
        edge_ref[pl.ds(16 + p, 1), :] = after[8:9]
        edge = jnp.concatenate([before[8:16], after[0:8]], axis=0)
        second = with_edges(main_second_ref[p], edge).astype(bf16)
        second_ref[p] = second
        y = dot(two, second, 1, 1) + bias_ref[...]
        y_ref[pl.ds(p, 16, stride=chunk_pitch), :] = y[0:16]
        y_ref[pl.ds(16 + p, 16, stride=chunk_pitch), :] = y[16:32]

    each_slab(second_body)
    y = dot(two, edge_ref[...].astype(bf16), 1, 1) + bias_ref[...]
    lane = lanes_of((16, 128))
    y = jnp.where(lane < 32, y[0:16], jnp.where(lane < 64, pltpu.roll(y[16:32], 32, 1), 0.0))
    y_ref[pl.ds(32, 16, stride=chunk_pitch), :] = y
    for o in range(16):
        send = y_ref[chunk_pitch * o : chunk_pitch * o + chunk, :].astype(bf16)
        send_ref[o] = send
        out_ref[0, o] = send[0:32]


def slope(diff):
    return diff * lax.rsqrt(diff * diff + smooth_width * smooth_width)


def crps_kernel(cells_all, x_ref, target_ref, outer_ref, inner_ref, out_ref):
    members = x_ref.shape[0]
    me = lax.axis_index("member")
    turn = lax.rem(4 - lax.rem(me, 4), 4) * 32
    even = even_tile()
    outer = outer_ref[pl.ds(48 + me // 4, 1), :]
    inner = inner_ref[pl.ds(48 + me // 4, 1), :]
    left = jnp.where(even, outer, inner)
    right = jnp.where(even, inner, outer)
    left = pltpu.roll(jnp.broadcast_to(left, (8, 128)), turn, 1)
    right = pltpu.roll(jnp.broadcast_to(right, (8, 128)), turn, 1)
    lane = lanes_of((8, 128))
    halo = jnp.where(
        lane < 16,
        left,
        jnp.where(
            lane < 32,
            pltpu.roll(right, 16, 1),
            jnp.where(lane < 48, pltpu.roll(left, 16, 1), pltpu.roll(right, 32, 1)),
        ),
    )
    for rows in (slice(0, 16), slice(16, 32), slice(32, 40)):
        x = [x_ref[i, rows, :].astype(f32) for i in range(members)]
        total = [None] * members
        for i in range(members):
            for j in range(i + 1, members):
                s = slope(x[i] - x[j])
                total[i] = s if total[i] is None else total[i] + s
                total[j] = -s if total[j] is None else total[j] - s
        aim = halo if rows.start == 32 else target_ref[me, rows, :]
        for i in range(members):
            value = slope(x[i] - aim) - pair_weight / (members - 1) * total[i]
            out_ref[i, rows, :] = (value / cells_all).astype(bf16)


def tap_sum(value):
    return jnp.sum(value.reshape(16, 8, 128), axis=0)


def backward_kernel(
    cot_ref, xs_ref, first_ref, gate_ref, hidden_ref, edge_first_ref, edge_gate_ref, edge_hidden_ref,
    second_ref, one_ref, two_ref, taps_two_ref,
    out_ref,
    cf_ref, bs_ref, sums_ref, cot_sum_ref, point_two_ref, point_one_ref, other_ref,
):
    for o in range(16):
        cf_ref[chunk_pitch * o : chunk_pitch * o + chunk, :] = cot_ref[o].astype(f32)
    two = two_ref[...]
    one = one_ref[...]
    sums_ref[...] = jnp.zeros(sums_ref.shape, f32)
    cot_sum_ref[...] = jnp.zeros(cot_sum_ref.shape, f32)
    point_two_ref[...] = jnp.zeros(point_two_ref.shape, f32)
    point_one_ref[...] = jnp.zeros(point_one_ref.shape, f32)
    other_ref[...] = jnp.zeros(other_ref.shape, f32)

    def cot_body(p):
        cot = jnp.concatenate(
            [cf_ref[pl.ds(p, 16, stride=chunk_pitch), :], cf_ref[pl.ds(16 + p, 16, stride=chunk_pitch), :]], axis=0
        )
        cot_sum_ref[0:32] += cot
        cot = cot.astype(bf16)
        bs_ref[p + 1, own : own + 128, :] = rounded(dot(cot, two, 0, 0))
        point_two_ref[...] += dot(cot, second_ref[p], 1, 0)

    each_slab(cot_body)
    halo = cf_ref[pl.ds(32, 16, stride=chunk_pitch), :]
    halo = jnp.concatenate([halo, pltpu.roll(halo, 96, 1)], axis=0).astype(bf16)
    halo = rounded(dot(halo, two, 0, 0))
    for p in range(slabs):
        bs_ref[p + 1, 15:16, :] = halo[p : p + 1]
        bs_ref[p + 1, 144:145, :] = halo[16 + p : 17 + p]
    wrap_slabs(bs_ref)

    def body(p):
        total = None
        hidden = with_edges(hidden_ref[p], edge_hidden_ref[p])
        for a in range(3):
            for b in range(3):
                t = 3 * a + b
                back = bs_ref[p + 2 - a, 17 - b : 145 - b, :]
                term = taps_two_ref[t : t + 1, :] * back
                total = term if total is None else total + term
                sums_ref[9 + t] += tap_sum(back * hidden)
        back_pre = (total * with_edges(gate_ref[p], edge_gate_ref[p])).astype(bf16)
        sums_ref[18] += tap_sum(back_pre.astype(f32))
        first = with_edges(first_ref[p], edge_first_ref[p]).astype(bf16)
        point_one_ref[...] += dot(back_pre, first, 0, 0)
        back_first = dot(back_pre, one, 1, 0)
        for a in range(3):
            for b in range(3):
                sums_ref[3 * a + b] += tap_sum(back_first * xs_ref[p + a, 15 + b : 143 + b, :])

    each_slab(body)
    for t in range(19):
        total = jnp.sum(sums_ref[t], axis=0, keepdims=True)
        other_ref[t : t + 1, :] = total + pltpu.roll(total, 64, 1)
    other_ref[24:40, :] = pltpu.roll(point_two_ref[0:16], 64, 1) + point_two_ref[16:32]
    bias_two = jnp.sum(cot_sum_ref[...].T, axis=0, keepdims=True)
    bias_two = bias_two + pltpu.roll(bias_two, 112, 1)
    other_ref[19:20, :] = pltpu.roll(bias_two, 64, 1)
    point_one = point_one_ref[0:64] + pltpu.roll(point_one_ref[64:128], 64, 1)
    packed = jnp.where(lanes_of((64, 128)) < 64, point_one, other_ref[...])
    out_ref[...] = packed.reshape(out_ref.shape)


def output_kernel(total_ref, depth_one_ref, point_one_ref, bias_one_ref, depth_two_ref, point_two_ref, bias_two_ref, rows_ref):
    rows_ref[...] = total_ref[...].reshape(64, 128)
    point_one_ref[...] = rows_ref[:, 0:64]
    depth_one_ref[...] = rows_ref[0:9, 64:128]
    depth_two_ref[...] = rows_ref[9:18, 64:128]
    bias_one_ref[...] = rows_ref[18:19, 64:128]
    bias_two_ref[...] = rows_ref[19:20, 64:80]
    point_two_ref[...] = rows_ref[24:40, 64:128]


def call(kernel, out_shape, scratch, flops, fetched=0, passed=0):
    hbm = pl.BlockSpec(memory_space=pltpu.HBM)
    vmem = pl.BlockSpec(memory_space=pltpu.VMEM)
    return pl.pallas_call(
        kernel,
        out_shape=out_shape,
        in_specs=[hbm] * fetched + [vmem] * passed,
        scratch_shapes=scratch,
        compiler_params=pltpu.CompilerParams(vmem_limit_bytes=24 * 1024 * 1024),
        cost_estimate=pl.CostEstimate(flops=flops, bytes_accessed=4 << 20, transcendentals=0),
    )


def in_hbm(*arrays):
    return [pltpu.with_memory_space_constraint(array, pltpu.HBM) for array in arrays]


def shape(dims, dtype):
    return jax.ShapeDtypeStruct(dims, dtype)


def local(predictor_inputs, target, depth_one, point_one, bias_one, depth_two, point_two, bias_two):
    members = lax.axis_size("member")
    tiles = lax.axis_size("tile")
    _, chans, rows, cols = predictor_inputs.shape
    slab = (slabs, cols, 128)
    xt, outer, inner, *weights = call(
        edge_kernel,
        (
            shape(slab, f32),
            shape((edge_rows, 128), f32),
            shape((edge_rows, 128), f32),
            shape((9, 64), f32),
            shape((64, 64), bf16),
            shape((1, 64), f32),
            shape((9, 64), f32),
            shape((16, 64), bf16),
            shape((1, 16), f32),
        ),
        [
            pltpu.VMEM((chans, rows, cols), bf16),
            pltpu.VMEM((16, rows, cols), f32),
            pltpu.VMEM((chans * lat_pitch, 128), f32),
            pltpu.VMEM((edge_rows, 128), f32),
            pltpu.VMEM((edge_rows, 128), f32),
            pltpu.SemaphoreType.DMA((8,)),
        ],
        1 << 20,
        fetched=8,
    )(
        *in_hbm(
            predictor_inputs, target, depth_one.T, point_one, bias_one[None], depth_two.T, point_two,
            bias_two[None],
        )
    )
    outer = lax.ppermute(outer, "tile", [(i, (i + 2 * (i % 2) - 1) % tiles) for i in range(tiles)])
    inner = lax.ppermute(inner, "tile", [(i, i + 1 - 2 * (i % 2)) for i in range(tiles)])
    (
        taps_one, one, one_turned, bias_one, taps_two, two, bias_two,
        first, gate, hidden, main_second,
    ) = call(
        main_kernel,
        (
            shape((16, 128), f32),
            shape((128, 128), bf16),
            shape((128, 128), bf16),
            shape((8, 128), f32),
            shape((16, 128), f32),
            shape((32, 128), bf16),
            shape((32, 128), f32),
            shape(slab, f32),
            shape(slab, f32),
            shape(slab, f32),
            shape(slab, f32),
        ),
        [
            pltpu.VMEM((128, 128), f32),
            pltpu.VMEM((slabs + 2, wide, 128), f32),
            pltpu.VMEM((slabs + 2, wide, 128), f32),
        ],
        1 << 28,
        passed=7,
    )(*weights, xt)
    edge = (slabs, 16, 128)
    out, send, xs, edge_first, edge_gate, edge_hidden, second = call(
        halo_kernel,
        (
            shape((1, 16, rows, cols), bf16),
            shape((16, chunk, 128), bf16),
            shape((slabs + 2, pitch, 128), f32),
            shape(edge, f32),
            shape(edge, f32),
            shape(edge, f32),
            shape(slab, bf16),
        ),
        [
            pltpu.VMEM((slabs + 2, 64, 128), f32),
            pltpu.VMEM((16 * chunk_pitch, 128), f32),
            pltpu.VMEM((128, 128), f32),
            pltpu.VMEM((edge_rows, 128), f32),
            pltpu.VMEM((edge_rows, 128), f32),
        ],
        1 << 27,
        passed=11,
    )(
        xt, outer, inner, hidden, main_second, taps_one, one_turned, bias_one, taps_two, two, bias_two
    )
    seen = lax.all_to_all(send, "member", 0, 0, tiled=True)
    cot = call(
        functools.partial(crps_kernel, rows * cols * tiles),
        shape((members, chunk, 128), bf16),
        [],
        1 << 24,
        passed=4,
    )(seen, target, outer, inner)
    cot = lax.all_to_all(cot, "member", 0, 0, tiled=True)
    packed = call(
        backward_kernel,
        shape((16, 4, 128), f32),
        [
            pltpu.VMEM((16 * chunk_pitch, 128), f32),
            pltpu.VMEM((slabs + 2, pitch, 128), f32),
            pltpu.VMEM((19, 8, 128), f32),
            pltpu.VMEM((128, 128), f32),
            pltpu.VMEM((32, 128), f32),
            pltpu.VMEM((128, 128), f32),
            pltpu.VMEM((64, 128), f32),
        ],
        1 << 28,
        passed=12,
    )(
        cot, xs, first, gate, hidden, edge_first, edge_gate, edge_hidden, second, one, two, taps_two
    )
    axes = ("member", "tile")
    near = [[16 * g + k for k in range(16)] for g in range(members * tiles // 16)]
    far = [list(group) for group in zip(*near)]
    part = lax.all_to_all(packed, axes, 0, 0, tiled=True, axis_index_groups=near)
    part = jnp.sum(part, axis=0)
    part = jnp.broadcast_to(part[None], (len(near),) + part.shape)
    part = lax.all_to_all(part, axes, 0, 0, tiled=True, axis_index_groups=far)
    part = jnp.sum(part, axis=0)
    part = jnp.broadcast_to(part[None], (len(far),) + part.shape)
    total = lax.all_to_all(part, axes, 0, 0, tiled=True, axis_index_groups=near)
    g_depth_one, g_point_one, g_bias_one, g_depth_two, g_point_two, g_bias_two = call(
        output_kernel,
        (
            shape((9, 64), f32),
            shape((64, 64), f32),
            shape((1, 64), f32),
            shape((9, 64), f32),
            shape((16, 64), f32),
            shape((1, 16), f32),
        ),
        [pltpu.VMEM((64, 128), f32)],
        1 << 20,
        passed=1,
    )(total)
    return (
        out,
        g_depth_one.T,
        g_point_one,
        g_bias_one[0],
        g_depth_two.T,
        g_point_two,
        g_bias_two[0],
    )


def solution(mesh):
    return jax.shard_map(
        local,
        mesh=mesh,
        in_specs=(
            P("member", None, None, "tile"),
            P(None, None, "tile"),
            P(),
            P(),
            P(),
            P(),
            P(),
            P(),
        ),
        out_specs=(P("member", None, None, "tile"), P(), P(), P(), P(), P(), P()),
        check_vma=False,
    )
```

```python
import functools

import jax
import jax.numpy as jnp
from jax import lax
from jax.experimental import pallas as pl
from jax.experimental.pallas import tpu as pltpu
from jax.sharding import PartitionSpec as P

smooth_width = 0.25
pair_weight = 0.95

slabs = 16
pitch = 160
own = 16
wide = 144
chunk = 40
chunk_pitch = 50
lat_pitch = 34
edge_rows = 56

f32 = jnp.float32
bf16 = jnp.bfloat16


def lanes_of(shape):
    return lax.broadcasted_iota(jnp.int32, shape, len(shape) - 1)


def dot(left, right, left_dim, right_dim):
    return lax.dot_general(
        left, right, (((left_dim,), (right_dim,)), ((), ())), preferred_element_type=f32
    )


def rounded(value):
    return value.astype(bf16).astype(f32)


def wrap_slabs(ref):
    last = pltpu.roll(ref[slabs], 64, 1)
    ref[0] = jnp.where(lanes_of(last.shape) >= 64, last, 0.0)
    first = pltpu.roll(ref[1], 64, 1)
    ref[slabs + 1] = jnp.where(lanes_of(first.shape) < 64, first, 0.0)


def both_halves(row):
    return jnp.concatenate([row, row], axis=1)


def each_slab(body):
    def step(p, carry):
        body(p)
        return carry

    lax.fori_loop(0, slabs, step, 0, unroll=True)


def fetch(sources, places, sems):
    copies = [
        pltpu.make_async_copy(source, place, sems.at[k])
        for k, (source, place) in enumerate(zip(sources, places))
    ]
    for copy in copies:
        copy.start()
    return copies


def even_tile():
    return lax.rem(lax.axis_index("tile"), 2) == 0


def edge_kernel(
    x_hbm, target_hbm, depth_one_hbm, point_one_hbm, bias_one_hbm, depth_two_hbm, point_two_hbm,
    bias_two_hbm,
    xt_ref, outer_ref, inner_ref, d1_ref, p1_ref, b1_ref, d2_ref, p2_ref, b2_ref,
    x_ref, target_ref, rows_scr, first_ref, last_ref, sems,
):
    sources = (
        target_hbm, x_hbm.at[0], depth_one_hbm, point_one_hbm, bias_one_hbm, depth_two_hbm,
        point_two_hbm, bias_two_hbm,
    )
    places = (target_ref, x_ref, d1_ref, p1_ref, b1_ref, d2_ref, p2_ref, b2_ref)
    target_copy, x_copy, *weight_copies = fetch(sources, places, sems)
    target_copy.wait()
    for k in range(4):
        turned = target_ref[4 * k : 4 * k + 4].reshape(128, 128).T
        first_ref[48 + k : 49 + k, :] = turned[0:1]
        last_ref[48 + k : 49 + k, :] = turned[127:128]
    first_ref[52:56, :] = jnp.zeros((4, 128), f32)
    last_ref[52:56, :] = jnp.zeros((4, 128), f32)
    x_copy.wait()
    for c in range(64):
        rows_scr[lat_pitch * c : lat_pitch * c + 32, :] = x_ref[c].astype(f32)

    def body(p):
        here = jnp.concatenate(
            [rows_scr[pl.ds(p, 64, stride=lat_pitch), :], rows_scr[pl.ds(p + 16, 64, stride=lat_pitch), :]],
            axis=0,
        )
        turned = here.T
        xt_ref[p] = turned
        for j in range(3):
            first_ref[pl.ds(16 * j + p, 1), :] = turned[j : j + 1]
            last_ref[pl.ds(16 * j + p, 1), :] = turned[125 + j : 126 + j]

    each_slab(body)
    even = even_tile()
    first, last = first_ref[...], last_ref[...]
    outer_ref[...] = jnp.where(even, first, last)
    inner_ref[...] = jnp.where(even, last, first)
    for copy in weight_copies:
        copy.wait()


def main_kernel(
    d1_ref, p1_ref, b1_ref, d2_ref, p2_ref, b2_ref, xt_ref,
    taps_one_ref, one_ref, one_turned_ref, bias_one_ref, taps_two_ref, two_ref, bias_two_ref,
    first_ref, gate_ref, hidden_ref, second_ref,
    turn_ref, xs_ref, hs_ref,
):
    turn_ref[...] = jnp.zeros((128, 128), f32)
    for ref in (xs_ref, hs_ref):
        for k in range(slabs + 2):
            ref[k, 0:8, :] = jnp.zeros((8, 128), f32)
            ref[k, 136:144, :] = jnp.zeros((8, 128), f32)
    for p in range(slabs):
        xs_ref[p + 1, 8:136, :] = xt_ref[p]
    wrap_slabs(xs_ref)
    zero = jnp.zeros((7, 128), f32)
    taps_one_ref[...] = jnp.concatenate([both_halves(d1_ref[...]), zero], axis=0)
    taps_two_ref[...] = jnp.concatenate([both_halves(d2_ref[...]), zero], axis=0)
    bias_one_ref[...] = jnp.broadcast_to(both_halves(b1_ref[...]), (8, 128))
    turn_ref[0:1, 0:16] = b2_ref[...]
    column = jnp.broadcast_to(turn_ref[...].T[0:16, 0:1], (16, 128))
    bias_two_ref[0:16] = column
    bias_two_ref[16:32] = column
    turn_ref[0:1, :] = jnp.zeros((1, 128), f32)
    weight = p1_ref[...].astype(f32)
    turn_ref[0:64, 0:64] = weight
    turn_ref[64:128, 64:128] = weight
    one_ref[...] = turn_ref[...].astype(bf16)
    one_turned = turn_ref[...].T.astype(bf16)
    one_turned_ref[...] = one_turned
    weight = p2_ref[...].astype(f32)
    zero = jnp.zeros((16, 64), f32)
    two_ref[...] = jnp.concatenate(
        [jnp.concatenate([weight, zero], axis=1), jnp.concatenate([zero, weight], axis=1)], axis=0
    ).astype(bf16)

    def first_body(p):
        first = rounded(depthwise(taps_one_ref, xs_ref, p, 7, 128))
        first_ref[p] = first
        hidden, gate = activation(first, one_turned, bias_one_ref)
        hidden_ref[p] = hidden
        hs_ref[p + 1, 8:136, :] = hidden
        gate_ref[p] = gate

    def second_body(p):
        second_ref[p] = depthwise(taps_two_ref, hs_ref, p, 7, 128)

    each_slab(first_body)
    wrap_slabs(hs_ref)
    each_slab(second_body)


def depthwise(taps_ref, ref, p, row, count):
    total = None
    for a in range(3):
        for b in range(3):
            tap = taps_ref[3 * a + b : 3 * a + b + 1, :]
            term = tap * ref[p + a, row + b : row + b + count, :]
            total = term if total is None else total + term
    return total


def activation(first, one_turned, bias_ref):
    pre = dot(first.astype(bf16), one_turned, 1, 0) + bias_ref[0:1]
    gate = 1.0 / (1.0 + jnp.exp(-pre))
    return rounded(pre * gate), gate * (1.0 + pre * (1.0 - gate))


def with_edges(main, edge):
    return jnp.concatenate([edge[0:8], main[8:120], edge[8:16]], axis=0)


def halo_kernel(
    xt_ref, outer_ref, inner_ref, hidden_ref, main_second_ref,
    taps_one_ref, one_turned_ref, bias_one_ref, taps_two_ref, two_ref, bias_ref,
    send_ref, xs_ref, first_ref, gate_ref, edge_hidden_ref, second_ref,
    hs_ref, y_ref, edge_ref, left_ref, right_ref,
):
    two = two_ref[...]
    even = even_tile()
    outer, inner = outer_ref[...], inner_ref[...]
    left_ref[...] = jnp.where(even, outer, inner)
    right_ref[...] = jnp.where(even, inner, outer)

    for k in range(slabs + 2):
        xs_ref[k, 0:16, :] = jnp.zeros((16, 128), f32)
        xs_ref[k, 144:160, :] = jnp.zeros((16, 128), f32)
    for p in range(slabs):
        xs_ref[p + 1, own : own + 128, :] = xt_ref[p]
        for j in range(3):
            xs_ref[p + 1, 13 + j : 14 + j, :] = left_ref[16 * j + p : 16 * j + p + 1, :]
            xs_ref[p + 1, 144 + j : 145 + j, :] = right_ref[16 * j + p : 16 * j + p + 1, :]
    wrap_slabs(xs_ref)

    one_turned = one_turned_ref[...]
    for k in range(0, slabs, 8):
        first = [
            depthwise(taps_one_ref, xs_ref, p, row, 16) for p in range(k, k + 8) for row in (7, 135)
        ]
        first = rounded(jnp.concatenate(first, axis=0))
        hidden, gate = activation(first, one_turned, bias_one_ref)
        for p in range(k, k + 8):
            at = 32 * (p - k)
            rows = slice(at + 8, at + 24)
            first_ref[p] = first[rows]
            gate_ref[p] = gate[rows]
            edge_hidden_ref[p] = hidden[rows]
            hs_ref[p + 1, 0:8, :] = jnp.zeros((8, 128), f32)
            hs_ref[p + 1, 8:24, :] = hidden[at : at + 16]
            hs_ref[p + 1, 24:32, :] = hidden_ref[p, 8:16, :]
            hs_ref[p + 1, 32:40, :] = hidden_ref[p, 112:120, :]
            hs_ref[p + 1, 40:56, :] = hidden[at + 16 : at + 32]
            hs_ref[p + 1, 56:64, :] = jnp.zeros((8, 128), f32)
    wrap_slabs(hs_ref)
    y_ref[...] = jnp.zeros(y_ref.shape, f32)
    edge_ref[...] = jnp.zeros(edge_ref.shape, f32)

    def second_body(p):
        before = depthwise(taps_two_ref, hs_ref, p, 7, 16)
        after = depthwise(taps_two_ref, hs_ref, p, 39, 16)
        edge_ref[pl.ds(p, 1), :] = before[7:8]
        edge_ref[pl.ds(16 + p, 1), :] = after[8:9]
        edge = jnp.concatenate([before[8:16], after[0:8]], axis=0)
        second = with_edges(main_second_ref[p], edge).astype(bf16)
        second_ref[p] = second
        y = dot(two, second, 1, 1) + bias_ref[...]
        y_ref[pl.ds(p, 16, stride=chunk_pitch), :] = y[0:16]
        y_ref[pl.ds(16 + p, 16, stride=chunk_pitch), :] = y[16:32]

    each_slab(second_body)
    y = dot(two, edge_ref[...].astype(bf16), 1, 1) + bias_ref[...]
    lane = lanes_of((16, 128))
    y = jnp.where(lane < 32, y[0:16], jnp.where(lane < 64, pltpu.roll(y[16:32], 32, 1), 0.0))
    y_ref[pl.ds(32, 16, stride=chunk_pitch), :] = y
    for o in range(16):
        send_ref[o] = y_ref[chunk_pitch * o : chunk_pitch * o + chunk, :].astype(bf16)


def slope(diff):
    return diff * lax.rsqrt(diff * diff + smooth_width * smooth_width)


def crps_kernel(
    cells_all, x_ref, target_ref, outer_ref, inner_ref, send_ref, out_ref, forecast_hbm, sem
):
    forecast_copy = pltpu.make_async_copy(send_ref.at[:, 0:32], forecast_hbm.at[0], sem)
    forecast_copy.start()
    members = x_ref.shape[0]
    me = lax.axis_index("member")
    turn = lax.rem(4 - lax.rem(me, 4), 4) * 32
    even = even_tile()
    outer = outer_ref[pl.ds(48 + me // 4, 1), :]
    inner = inner_ref[pl.ds(48 + me // 4, 1), :]
    left = jnp.where(even, outer, inner)
    right = jnp.where(even, inner, outer)
    left = pltpu.roll(jnp.broadcast_to(left, (8, 128)), turn, 1)
    right = pltpu.roll(jnp.broadcast_to(right, (8, 128)), turn, 1)
    lane = lanes_of((8, 128))
    halo = jnp.where(
        lane < 16,
        left,
        jnp.where(
            lane < 32,
            pltpu.roll(right, 16, 1),
            jnp.where(lane < 48, pltpu.roll(left, 16, 1), pltpu.roll(right, 32, 1)),
        ),
    )
    for rows in (slice(0, 16), slice(16, 32), slice(32, 40)):
        x = [x_ref[i, rows, :].astype(f32) for i in range(members)]
        total = [None] * members
        for i in range(members):
            for j in range(i + 1, members):
                s = slope(x[i] - x[j])
                total[i] = s if total[i] is None else total[i] + s
                total[j] = -s if total[j] is None else total[j] - s
        aim = halo if rows.start == 32 else target_ref[me, rows, :]
        for i in range(members):
            value = slope(x[i] - aim) - pair_weight / (members - 1) * total[i]
            out_ref[i, rows, :] = (value / cells_all).astype(bf16)
    forecast_copy.wait()


def tap_sum(value):
    return jnp.sum(value.reshape(16, 8, 128), axis=0)


def backward_kernel(
    cot_ref, xs_ref, first_ref, gate_ref, hidden_ref, edge_first_ref, edge_gate_ref, edge_hidden_ref,
    second_ref, one_ref, two_ref, taps_two_ref,
    out_ref,
    cf_ref, bs_ref, sums_ref, cot_sum_ref, point_two_ref, point_one_ref, other_ref,
):
    for o in range(16):
        cf_ref[chunk_pitch * o : chunk_pitch * o + chunk, :] = cot_ref[o].astype(f32)
    two = two_ref[...]
    one = one_ref[...]
    sums_ref[...] = jnp.zeros(sums_ref.shape, f32)
    cot_sum_ref[...] = jnp.zeros(cot_sum_ref.shape, f32)
    point_two_ref[...] = jnp.zeros(point_two_ref.shape, f32)
    point_one_ref[...] = jnp.zeros(point_one_ref.shape, f32)
    other_ref[...] = jnp.zeros(other_ref.shape, f32)

    def cot_body(p):
        cot = jnp.concatenate(
            [cf_ref[pl.ds(p, 16, stride=chunk_pitch), :], cf_ref[pl.ds(16 + p, 16, stride=chunk_pitch), :]], axis=0
        )
        cot_sum_ref[0:32] += cot
        cot = cot.astype(bf16)
        bs_ref[p + 1, own : own + 128, :] = rounded(dot(cot, two, 0, 0))
        point_two_ref[...] += dot(cot, second_ref[p], 1, 0)

    each_slab(cot_body)
    halo = cf_ref[pl.ds(32, 16, stride=chunk_pitch), :]
    halo = jnp.concatenate([halo, pltpu.roll(halo, 96, 1)], axis=0).astype(bf16)
    halo = rounded(dot(halo, two, 0, 0))
    for p in range(slabs):
        bs_ref[p + 1, 15:16, :] = halo[p : p + 1]
        bs_ref[p + 1, 144:145, :] = halo[16 + p : 17 + p]
    wrap_slabs(bs_ref)

    def body(p):
        total = None
        hidden = with_edges(hidden_ref[p], edge_hidden_ref[p])
        for a in range(3):
            for b in range(3):
                t = 3 * a + b
                back = bs_ref[p + 2 - a, 17 - b : 145 - b, :]
                term = taps_two_ref[t : t + 1, :] * back
                total = term if total is None else total + term
                sums_ref[9 + t] += tap_sum(back * hidden)
        back_pre = (total * with_edges(gate_ref[p], edge_gate_ref[p])).astype(bf16)
        sums_ref[18] += tap_sum(back_pre.astype(f32))
        first = with_edges(first_ref[p], edge_first_ref[p]).astype(bf16)
        point_one_ref[...] += dot(back_pre, first, 0, 0)
        back_first = dot(back_pre, one, 1, 0)
        for a in range(3):
            for b in range(3):
                sums_ref[3 * a + b] += tap_sum(back_first * xs_ref[p + a, 15 + b : 143 + b, :])

    each_slab(body)
    for t in range(19):
        total = jnp.sum(sums_ref[t], axis=0, keepdims=True)
        other_ref[t : t + 1, :] = total + pltpu.roll(total, 64, 1)
    other_ref[24:40, :] = pltpu.roll(point_two_ref[0:16], 64, 1) + point_two_ref[16:32]
    bias_two = jnp.sum(cot_sum_ref[...].T, axis=0, keepdims=True)
    bias_two = bias_two + pltpu.roll(bias_two, 112, 1)
    other_ref[19:20, :] = pltpu.roll(bias_two, 64, 1)
    point_one = point_one_ref[0:64] + pltpu.roll(point_one_ref[64:128], 64, 1)
    packed = jnp.where(lanes_of((64, 128)) < 64, point_one, other_ref[...])
    out_ref[...] = packed.reshape(out_ref.shape)


def output_kernel(total_ref, depth_one_ref, point_one_ref, bias_one_ref, depth_two_ref, point_two_ref, bias_two_ref, rows_ref):
    rows_ref[...] = total_ref[...].reshape(64, 128)
    point_one_ref[...] = rows_ref[:, 0:64]
    depth_one_ref[...] = rows_ref[0:9, 64:128]
    depth_two_ref[...] = rows_ref[9:18, 64:128]
    bias_one_ref[...] = rows_ref[18:19, 64:128]
    bias_two_ref[...] = rows_ref[19:20, 64:80]
    point_two_ref[...] = rows_ref[24:40, 64:128]


def call(kernel, out_shape, scratch, flops, fetched=0, passed=0, **out):
    hbm = pl.BlockSpec(memory_space=pltpu.HBM)
    vmem = pl.BlockSpec(memory_space=pltpu.VMEM)
    return pl.pallas_call(
        kernel,
        out_shape=out_shape,
        in_specs=[hbm] * fetched + [vmem] * passed,
        scratch_shapes=scratch,
        **out,
        compiler_params=pltpu.CompilerParams(vmem_limit_bytes=24 * 1024 * 1024),
        cost_estimate=pl.CostEstimate(flops=flops, bytes_accessed=4 << 20, transcendentals=0),
    )


def in_hbm(*arrays):
    return [pltpu.with_memory_space_constraint(array, pltpu.HBM) for array in arrays]


def shape(dims, dtype):
    return jax.ShapeDtypeStruct(dims, dtype)


def local(predictor_inputs, target, depth_one, point_one, bias_one, depth_two, point_two, bias_two):
    members = lax.axis_size("member")
    tiles = lax.axis_size("tile")
    _, chans, rows, cols = predictor_inputs.shape
    slab = (slabs, cols, 128)
    xt, outer, inner, *weights = call(
        edge_kernel,
        (
            shape(slab, f32),
            shape((edge_rows, 128), f32),
            shape((edge_rows, 128), f32),
            shape((9, 64), f32),
            shape((64, 64), bf16),
            shape((1, 64), f32),
            shape((9, 64), f32),
            shape((16, 64), bf16),
            shape((1, 16), f32),
        ),
        [
            pltpu.VMEM((chans, rows, cols), bf16),
            pltpu.VMEM((16, rows, cols), f32),
            pltpu.VMEM((chans * lat_pitch, 128), f32),
            pltpu.VMEM((edge_rows, 128), f32),
            pltpu.VMEM((edge_rows, 128), f32),
            pltpu.SemaphoreType.DMA((8,)),
        ],
        1 << 20,
        fetched=8,
    )(
        *in_hbm(
            predictor_inputs, target, depth_one.T, point_one, bias_one[None], depth_two.T, point_two,
            bias_two[None],
        )
    )
    outer = lax.ppermute(outer, "tile", [(i, (i + 2 * (i % 2) - 1) % tiles) for i in range(tiles)])
    inner = lax.ppermute(inner, "tile", [(i, i + 1 - 2 * (i % 2)) for i in range(tiles)])
    (
        taps_one, one, one_turned, bias_one, taps_two, two, bias_two,
        first, gate, hidden, main_second,
    ) = call(
        main_kernel,
        (
            shape((16, 128), f32),
            shape((128, 128), bf16),
            shape((128, 128), bf16),
            shape((8, 128), f32),
            shape((16, 128), f32),
            shape((32, 128), bf16),
            shape((32, 128), f32),
            shape(slab, f32),
            shape(slab, f32),
            shape(slab, f32),
            shape(slab, f32),
        ),
        [
            pltpu.VMEM((128, 128), f32),
            pltpu.VMEM((slabs + 2, wide, 128), f32),
            pltpu.VMEM((slabs + 2, wide, 128), f32),
        ],
        1 << 28,
        passed=7,
    )(*weights, xt)
    edge = (slabs, 16, 128)
    send, xs, edge_first, edge_gate, edge_hidden, second = call(
        halo_kernel,
        (
            shape((16, chunk, 128), bf16),
            shape((slabs + 2, pitch, 128), f32),
            shape(edge, f32),
            shape(edge, f32),
            shape(edge, f32),
            shape(slab, bf16),
        ),
        [
            pltpu.VMEM((slabs + 2, 64, 128), f32),
            pltpu.VMEM((16 * chunk_pitch, 128), f32),
            pltpu.VMEM((128, 128), f32),
            pltpu.VMEM((edge_rows, 128), f32),
            pltpu.VMEM((edge_rows, 128), f32),
        ],
        1 << 27,
        passed=11,
    )(
        xt, outer, inner, hidden, main_second, taps_one, one_turned, bias_one, taps_two, two, bias_two
    )
    seen = lax.all_to_all(send, "member", 0, 0, tiled=True)
    cot, out = call(
        functools.partial(crps_kernel, rows * cols * tiles),
        (shape((members, chunk, 128), bf16), shape((1, 16, rows, cols), bf16)),
        [pltpu.SemaphoreType.DMA],
        1 << 24,
        passed=5,
        out_specs=(pl.BlockSpec(memory_space=pltpu.VMEM), pl.BlockSpec(memory_space=pltpu.HBM)),
    )(seen, target, outer, inner, send)
    cot = lax.all_to_all(cot, "member", 0, 0, tiled=True)
    packed = call(
        backward_kernel,
        shape((16, 4, 128), f32),
        [
            pltpu.VMEM((16 * chunk_pitch, 128), f32),
            pltpu.VMEM((slabs + 2, pitch, 128), f32),
            pltpu.VMEM((19, 8, 128), f32),
            pltpu.VMEM((128, 128), f32),
            pltpu.VMEM((32, 128), f32),
            pltpu.VMEM((128, 128), f32),
            pltpu.VMEM((64, 128), f32),
        ],
        1 << 28,
        passed=12,
    )(
        cot, xs, first, gate, hidden, edge_first, edge_gate, edge_hidden, second, one, two, taps_two
    )
    axes = ("member", "tile")
    near = [[16 * g + k for k in range(16)] for g in range(members * tiles // 16)]
    far = [list(group) for group in zip(*near)]
    part = lax.all_to_all(packed, axes, 0, 0, tiled=True, axis_index_groups=near)
    part = jnp.sum(part, axis=0)
    part = jnp.broadcast_to(part[None], (len(near),) + part.shape)
    part = lax.all_to_all(part, axes, 0, 0, tiled=True, axis_index_groups=far)
    part = jnp.sum(part, axis=0)
    part = jnp.broadcast_to(part[None], (len(far),) + part.shape)
    total = lax.all_to_all(part, axes, 0, 0, tiled=True, axis_index_groups=near)
    g_depth_one, g_point_one, g_bias_one, g_depth_two, g_point_two, g_bias_two = call(
        output_kernel,
        (
            shape((9, 64), f32),
            shape((64, 64), f32),
            shape((1, 64), f32),
            shape((9, 64), f32),
            shape((16, 64), f32),
            shape((1, 16), f32),
        ),
        [pltpu.VMEM((64, 128), f32)],
        1 << 20,
        passed=1,
    )(total)
    return (
        out,
        g_depth_one.T,
        g_point_one,
        g_bias_one[0],
        g_depth_two.T,
        g_point_two,
        g_bias_two[0],
    )


def solution(mesh):
    return jax.shard_map(
        local,
        mesh=mesh,
        in_specs=(
            P("member", None, None, "tile"),
            P(None, None, "tile"),
            P(),
            P(),
            P(),
            P(),
            P(),
            P(),
        ),
        out_specs=(P("member", None, None, "tile"), P(), P(), P(), P(), P(), P()),
        check_vma=False,
    )
```

```python
import functools

import jax
import jax.numpy as jnp
from jax import lax
from jax.experimental import pallas as pl
from jax.experimental.pallas import tpu as pltpu
from jax.sharding import PartitionSpec as P

smooth_width = 0.25
pair_weight = 0.95

slabs = 16
pitch = 160
own = 16
chunk = 40
chunk_pitch = 50
lat_pitch = 34
edge_rows = 56

f32 = jnp.float32
bf16 = jnp.bfloat16


def lanes_of(shape):
    return lax.broadcasted_iota(jnp.int32, shape, len(shape) - 1)


def dot(left, right, left_dim, right_dim):
    return lax.dot_general(
        left, right, (((left_dim,), (right_dim,)), ((), ())), preferred_element_type=f32
    )


def rounded(value):
    return value.astype(bf16).astype(f32)


def wrap_slabs(ref):
    last = pltpu.roll(ref[slabs], 64, 1)
    ref[0] = jnp.where(lanes_of(last.shape) >= 64, last, 0.0)
    first = pltpu.roll(ref[1], 64, 1)
    ref[slabs + 1] = jnp.where(lanes_of(first.shape) < 64, first, 0.0)


def both_halves(row):
    return jnp.concatenate([row, row], axis=1)


def each_slab(body):
    for p in range(slabs):
        body(p)


def in_turn(make, ref, use):
    for p in (0, slabs - 1, 1):
        make(p)
    wrap_slabs(ref)
    for p in range(slabs):
        if p + 2 < slabs - 1:
            make(p + 2)
        use(p)


def fetch(sources, places, sems):
    copies = [
        pltpu.make_async_copy(source, place, sems.at[k])
        for k, (source, place) in enumerate(zip(sources, places))
    ]
    for copy in copies:
        copy.start()
    return copies


def even_tile():
    return lax.rem(lax.axis_index("tile"), 2) == 0


def edge_kernel(
    x_hbm, target_hbm, depth_one_hbm, point_one_hbm, bias_one_hbm, depth_two_hbm, point_two_hbm,
    bias_two_hbm,
    xt_ref, outer_ref, inner_ref, d1_ref, p1_ref, b1_ref, d2_ref, p2_ref, b2_ref,
    x_ref, target_ref, rows_scr, first_ref, last_ref, sems,
):
    sources = (
        target_hbm, x_hbm.at[0], depth_one_hbm, point_one_hbm, bias_one_hbm, depth_two_hbm,
        point_two_hbm, bias_two_hbm,
    )
    places = (target_ref, x_ref, d1_ref, p1_ref, b1_ref, d2_ref, p2_ref, b2_ref)
    target_copy, x_copy, *weight_copies = fetch(sources, places, sems)
    target_copy.wait()
    for k in range(4):
        turned = target_ref[4 * k : 4 * k + 4].reshape(128, 128).T
        first_ref[48 + k : 49 + k, :] = turned[0:1]
        last_ref[48 + k : 49 + k, :] = turned[127:128]
    first_ref[52:56, :] = jnp.zeros((4, 128), f32)
    last_ref[52:56, :] = jnp.zeros((4, 128), f32)
    x_copy.wait()
    for c in range(64):
        rows_scr[lat_pitch * c : lat_pitch * c + 32, :] = x_ref[c].astype(f32)

    def body(p):
        here = jnp.concatenate(
            [rows_scr[pl.ds(p, 64, stride=lat_pitch), :], rows_scr[pl.ds(p + 16, 64, stride=lat_pitch), :]],
            axis=0,
        )
        turned = here.T
        xt_ref[p] = turned
        for j in range(3):
            first_ref[pl.ds(16 * j + p, 1), :] = turned[j : j + 1]
            last_ref[pl.ds(16 * j + p, 1), :] = turned[125 + j : 126 + j]

    each_slab(body)
    even = even_tile()
    first, last = first_ref[...], last_ref[...]
    outer_ref[...] = jnp.where(even, first, last)
    inner_ref[...] = jnp.where(even, last, first)
    for copy in weight_copies:
        copy.wait()


def main_kernel(
    d1_ref, p1_ref, b1_ref, d2_ref, p2_ref, b2_ref, xt_ref,
    taps_one_ref, one_ref, one_turned_ref, bias_one_ref, taps_two_ref, two_ref, bias_two_ref,
    first_ref, gate_ref, hidden_ref, second_ref,
    turn_ref, xs_ref, hs_ref,
):
    turn_ref[...] = jnp.zeros((128, 128), f32)
    for p in range(slabs):
        xs_ref[p + 1] = xt_ref[p]
    wrap_slabs(xs_ref)
    zero = jnp.zeros((7, 128), f32)
    taps_one_ref[...] = jnp.concatenate([both_halves(d1_ref[...]), zero], axis=0)
    taps_two_ref[...] = jnp.concatenate([both_halves(d2_ref[...]), zero], axis=0)
    bias_one_ref[...] = jnp.broadcast_to(both_halves(b1_ref[...]), (8, 128))
    turn_ref[0:1, 0:16] = b2_ref[...]
    column = jnp.broadcast_to(turn_ref[...].T[0:16, 0:1], (16, 128))
    bias_two_ref[0:16] = column
    bias_two_ref[16:32] = column
    turn_ref[0:1, :] = jnp.zeros((1, 128), f32)
    weight = p1_ref[...].astype(f32)
    turn_ref[0:64, 0:64] = weight
    turn_ref[64:128, 64:128] = weight
    one_ref[...] = turn_ref[...].astype(bf16)
    one_turned = turn_ref[...].T.astype(bf16)
    one_turned_ref[...] = one_turned
    weight = p2_ref[...].astype(f32)
    zero = jnp.zeros((16, 64), f32)
    two_ref[...] = jnp.concatenate(
        [jnp.concatenate([weight, zero], axis=1), jnp.concatenate([zero, weight], axis=1)], axis=0
    ).astype(bf16)

    def first_body(p):
        first = rounded(depthwise(taps_one_ref, xs_ref, p, 7, 112))
        first_ref[p] = first
        hidden, gate = activation(first, one_turned, bias_one_ref)
        hidden_ref[p] = hidden
        hs_ref[p + 1] = hidden
        gate_ref[p] = gate

    def second_body(p):
        second_ref[p] = depthwise(taps_two_ref, hs_ref, p, 7, 96).astype(bf16)

    in_turn(first_body, hs_ref, second_body)


def depthwise(taps_ref, ref, p, row, count):
    total = None
    for a in range(3):
        for b in range(3):
            tap = taps_ref[3 * a + b : 3 * a + b + 1, :]
            term = tap * ref[p + a, row + b : row + b + count, :]
            total = term if total is None else total + term
    return total


def activation(first, one_turned, bias_ref):
    pre = dot(first.astype(bf16), one_turned, 1, 0) + bias_ref[0:1]
    gate = 1.0 / (1.0 + jnp.exp(-pre))
    return rounded(pre * gate), gate * (1.0 + pre * (1.0 - gate))


def with_edges(main, edge):
    return jnp.concatenate([edge[0:8], main, edge[8:16]], axis=0)


def halo_kernel(
    xt_ref, outer_ref, inner_ref, hidden_ref, main_second_ref,
    taps_one_ref, one_turned_ref, bias_one_ref, taps_two_ref, two_ref, bias_ref,
    send_ref, xs_ref, first_ref, gate_ref, edge_hidden_ref, second_ref,
    hs_ref, y_ref, edge_ref, left_ref, right_ref,
):
    two = two_ref[...]
    even = even_tile()
    outer, inner = outer_ref[...], inner_ref[...]
    left_ref[...] = jnp.where(even, outer, inner)
    right_ref[...] = jnp.where(even, inner, outer)

    for k in range(slabs + 2):
        xs_ref[k, 0:16, :] = jnp.zeros((16, 128), f32)
        xs_ref[k, 144:160, :] = jnp.zeros((16, 128), f32)
    for p in range(slabs):
        xs_ref[p + 1, own : own + 128, :] = xt_ref[p]
        for j in range(3):
            xs_ref[p + 1, 13 + j : 14 + j, :] = left_ref[16 * j + p : 16 * j + p + 1, :]
            xs_ref[p + 1, 144 + j : 145 + j, :] = right_ref[16 * j + p : 16 * j + p + 1, :]
    wrap_slabs(xs_ref)

    one_turned = one_turned_ref[...]
    for k in range(0, slabs, 8):
        first = [
            depthwise(taps_one_ref, xs_ref, p, row, 16) for p in range(k, k + 8) for row in (7, 135)
        ]
        first = rounded(jnp.concatenate(first, axis=0))
        hidden, gate = activation(first, one_turned, bias_one_ref)
        for p in range(k, k + 8):
            at = 32 * (p - k)
            rows = slice(at + 8, at + 24)
            first_ref[p] = first[rows]
            gate_ref[p] = gate[rows]
            edge_hidden_ref[p] = hidden[rows]
            hs_ref[p + 1, 0:8, :] = jnp.zeros((8, 128), f32)
            hs_ref[p + 1, 8:24, :] = hidden[at : at + 16]
            hs_ref[p + 1, 24:40, :] = hidden_ref[p, 0:16, :]
            hs_ref[p + 1, 40:56, :] = hidden_ref[p, 96:112, :]
            hs_ref[p + 1, 56:72, :] = hidden[at + 16 : at + 32]
            hs_ref[p + 1, 72:80, :] = jnp.zeros((8, 128), f32)
    wrap_slabs(hs_ref)
    y_ref[...] = jnp.zeros(y_ref.shape, f32)
    edge_ref[...] = jnp.zeros(edge_ref.shape, f32)

    def second_body(p):
        before = depthwise(taps_two_ref, hs_ref, p, 7, 24)
        after = depthwise(taps_two_ref, hs_ref, p, 47, 24)
        edge_ref[pl.ds(p, 1), :] = before[7:8]
        edge_ref[pl.ds(16 + p, 1), :] = after[16:17]
        second = jnp.concatenate(
            [before[8:24].astype(bf16), main_second_ref[p], after[0:16].astype(bf16)], axis=0
        )
        second_ref[p] = second
        y = dot(two, second, 1, 1) + bias_ref[...]
        y_ref[pl.ds(p, 16, stride=chunk_pitch), :] = y[0:16]
        y_ref[pl.ds(16 + p, 16, stride=chunk_pitch), :] = y[16:32]

    each_slab(second_body)
    y = dot(two, edge_ref[...].astype(bf16), 1, 1) + bias_ref[...]
    lane = lanes_of((16, 128))
    y = jnp.where(lane < 32, y[0:16], jnp.where(lane < 64, pltpu.roll(y[16:32], 32, 1), 0.0))
    y_ref[pl.ds(32, 16, stride=chunk_pitch), :] = y
    for o in range(16):
        send_ref[o] = y_ref[chunk_pitch * o : chunk_pitch * o + chunk, :].astype(bf16)


def slope(diff):
    return diff * lax.rsqrt(diff * diff + smooth_width * smooth_width)


def crps_kernel(
    cells_all, x_ref, target_ref, outer_ref, inner_ref, send_ref, out_ref, forecast_hbm, sem
):
    forecast_copy = pltpu.make_async_copy(send_ref.at[:, 0:32], forecast_hbm.at[0], sem)
    forecast_copy.start()
    members = x_ref.shape[0]
    me = lax.axis_index("member")
    turn = lax.rem(4 - lax.rem(me, 4), 4) * 32
    even = even_tile()
    outer = outer_ref[pl.ds(48 + me // 4, 1), :]
    inner = inner_ref[pl.ds(48 + me // 4, 1), :]
    left = jnp.where(even, outer, inner)
    right = jnp.where(even, inner, outer)
    left = pltpu.roll(jnp.broadcast_to(left, (8, 128)), turn, 1)
    right = pltpu.roll(jnp.broadcast_to(right, (8, 128)), turn, 1)
    lane = lanes_of((8, 128))
    halo = jnp.where(
        lane < 16,
        left,
        jnp.where(
            lane < 32,
            pltpu.roll(right, 16, 1),
            jnp.where(lane < 48, pltpu.roll(left, 16, 1), pltpu.roll(right, 32, 1)),
        ),
    )
    for rows in (slice(0, 16), slice(16, 32), slice(32, 40)):
        x = [x_ref[i, rows, :].astype(f32) for i in range(members)]
        total = [None] * members
        for i in range(members):
            for j in range(i + 1, members):
                s = slope(x[i] - x[j])
                total[i] = s if total[i] is None else total[i] + s
                total[j] = -s if total[j] is None else total[j] - s
        aim = halo if rows.start == 32 else target_ref[me, rows, :]
        for i in range(members):
            value = slope(x[i] - aim) - pair_weight / (members - 1) * total[i]
            out_ref[i, rows, :] = (value / cells_all).astype(bf16)
    forecast_copy.wait()


def tap_sum(value):
    return jnp.sum(value.reshape(16, 8, 128), axis=0)


def backward_kernel(
    cot_ref, xs_ref, first_ref, gate_ref, hidden_ref, edge_first_ref, edge_gate_ref, edge_hidden_ref,
    second_ref, one_ref, two_ref, taps_two_ref,
    out_ref,
    cf_ref, bs_ref, sums_ref, cot_sum_ref, point_two_ref, point_one_ref, other_ref,
):
    for o in range(16):
        cf_ref[chunk_pitch * o : chunk_pitch * o + chunk, :] = cot_ref[o].astype(f32)
    two = two_ref[...]
    one = one_ref[...]
    sums_ref[...] = jnp.zeros(sums_ref.shape, f32)
    cot_sum_ref[...] = jnp.zeros(cot_sum_ref.shape, f32)
    point_two_ref[...] = jnp.zeros(point_two_ref.shape, f32)
    point_one_ref[...] = jnp.zeros(point_one_ref.shape, f32)
    other_ref[...] = jnp.zeros(other_ref.shape, f32)

    def cot_body(p):
        cot = jnp.concatenate(
            [cf_ref[pl.ds(p, 16, stride=chunk_pitch), :], cf_ref[pl.ds(16 + p, 16, stride=chunk_pitch), :]], axis=0
        )
        cot_sum_ref[0:32] += cot
        cot = cot.astype(bf16)
        bs_ref[p + 1, own : own + 128, :] = rounded(dot(cot, two, 0, 0))
        point_two_ref[...] += dot(cot, second_ref[p], 1, 0)

    each_slab(cot_body)
    halo = cf_ref[pl.ds(32, 16, stride=chunk_pitch), :]
    halo = jnp.concatenate([halo, pltpu.roll(halo, 96, 1)], axis=0).astype(bf16)
    halo = rounded(dot(halo, two, 0, 0))
    for p in range(slabs):
        bs_ref[p + 1, 15:16, :] = halo[p : p + 1]
        bs_ref[p + 1, 144:145, :] = halo[16 + p : 17 + p]
    wrap_slabs(bs_ref)

    def body(p):
        total = None
        hidden = with_edges(hidden_ref[p], edge_hidden_ref[p])
        for a in range(3):
            for b in range(3):
                t = 3 * a + b
                back = bs_ref[p + 2 - a, 17 - b : 145 - b, :]
                term = taps_two_ref[t : t + 1, :] * back
                total = term if total is None else total + term
                sums_ref[9 + t] += tap_sum(back * hidden)
        back_pre = (total * with_edges(gate_ref[p], edge_gate_ref[p])).astype(bf16)
        sums_ref[18] += tap_sum(back_pre.astype(f32))
        first = with_edges(first_ref[p], edge_first_ref[p]).astype(bf16)
        point_one_ref[...] += dot(back_pre, first, 0, 0)
        back_first = dot(back_pre, one, 1, 0)
        for a in range(3):
            for b in range(3):
                sums_ref[3 * a + b] += tap_sum(back_first * xs_ref[p + a, 15 + b : 143 + b, :])

    each_slab(body)
    for t in range(19):
        total = jnp.sum(sums_ref[t], axis=0, keepdims=True)
        other_ref[t : t + 1, :] = total + pltpu.roll(total, 64, 1)
    other_ref[24:40, :] = pltpu.roll(point_two_ref[0:16], 64, 1) + point_two_ref[16:32]
    bias_two = jnp.sum(cot_sum_ref[...].T, axis=0, keepdims=True)
    bias_two = bias_two + pltpu.roll(bias_two, 112, 1)
    other_ref[19:20, :] = pltpu.roll(bias_two, 64, 1)
    point_one = point_one_ref[0:64] + pltpu.roll(point_one_ref[64:128], 64, 1)
    packed = jnp.where(lanes_of((64, 128)) < 64, point_one, other_ref[...])
    out_ref[...] = packed.reshape(out_ref.shape)


def output_kernel(total_ref, depth_one_ref, point_one_ref, bias_one_ref, depth_two_ref, point_two_ref, bias_two_ref, rows_ref):
    rows_ref[...] = total_ref[...].reshape(64, 128)
    point_one_ref[...] = rows_ref[:, 0:64]
    depth_one_ref[...] = rows_ref[0:9, 64:128]
    depth_two_ref[...] = rows_ref[9:18, 64:128]
    bias_one_ref[...] = rows_ref[18:19, 64:128]
    bias_two_ref[...] = rows_ref[19:20, 64:80]
    point_two_ref[...] = rows_ref[24:40, 64:128]


def call(kernel, out_shape, scratch, flops, fetched=0, passed=0, **out):
    hbm = pl.BlockSpec(memory_space=pltpu.HBM)
    vmem = pl.BlockSpec(memory_space=pltpu.VMEM)
    return pl.pallas_call(
        kernel,
        out_shape=out_shape,
        in_specs=[hbm] * fetched + [vmem] * passed,
        scratch_shapes=scratch,
        **out,
        compiler_params=pltpu.CompilerParams(vmem_limit_bytes=24 * 1024 * 1024),
        cost_estimate=pl.CostEstimate(flops=flops, bytes_accessed=4 << 20, transcendentals=0),
    )


def in_hbm(*arrays):
    return [pltpu.with_memory_space_constraint(array, pltpu.HBM) for array in arrays]


def shape(dims, dtype):
    return jax.ShapeDtypeStruct(dims, dtype)


def local(predictor_inputs, target, depth_one, point_one, bias_one, depth_two, point_two, bias_two):
    members = lax.axis_size("member")
    tiles = lax.axis_size("tile")
    _, chans, rows, cols = predictor_inputs.shape
    slab = (slabs, cols, 128)
    xt, outer, inner, *weights = call(
        edge_kernel,
        (
            shape(slab, f32),
            shape((edge_rows, 128), f32),
            shape((edge_rows, 128), f32),
            shape((9, 64), f32),
            shape((64, 64), bf16),
            shape((1, 64), f32),
            shape((9, 64), f32),
            shape((16, 64), bf16),
            shape((1, 16), f32),
        ),
        [
            pltpu.VMEM((chans, rows, cols), bf16),
            pltpu.VMEM((16, rows, cols), f32),
            pltpu.VMEM((chans * lat_pitch + 32, 128), f32),
            pltpu.VMEM((edge_rows, 128), f32),
            pltpu.VMEM((edge_rows, 128), f32),
            pltpu.SemaphoreType.DMA((8,)),
        ],
        1 << 20,
        fetched=8,
    )(
        *in_hbm(
            predictor_inputs, target, depth_one.T, point_one, bias_one[None], depth_two.T, point_two,
            bias_two[None],
        )
    )
    outer = lax.ppermute(outer, "tile", [(i, (i + 2 * (i % 2) - 1) % tiles) for i in range(tiles)])
    inner = lax.ppermute(inner, "tile", [(i, i + 1 - 2 * (i % 2)) for i in range(tiles)])
    (
        taps_one, one, one_turned, bias_one, taps_two, two, bias_two,
        first, gate, hidden, main_second,
    ) = call(
        main_kernel,
        (
            shape((16, 128), f32),
            shape((128, 128), bf16),
            shape((128, 128), bf16),
            shape((8, 128), f32),
            shape((16, 128), f32),
            shape((32, 128), bf16),
            shape((32, 128), f32),
            shape((slabs, 112, 128), f32),
            shape((slabs, 112, 128), f32),
            shape((slabs, 112, 128), f32),
            shape((slabs, 96, 128), bf16),
        ),
        [
            pltpu.VMEM((128, 128), f32),
            pltpu.VMEM((slabs + 2, cols, 128), f32),
            pltpu.VMEM((slabs + 2, 112, 128), f32),
        ],
        1 << 28,
        passed=7,
    )(*weights, xt)
    edge = (slabs, 16, 128)
    send, xs, edge_first, edge_gate, edge_hidden, second = call(
        halo_kernel,
        (
            shape((16, chunk, 128), bf16),
            shape((slabs + 2, pitch, 128), f32),
            shape(edge, f32),
            shape(edge, f32),
            shape(edge, f32),
            shape(slab, bf16),
        ),
        [
            pltpu.VMEM((slabs + 2, 80, 128), f32),
            pltpu.VMEM((16 * chunk_pitch + 40, 128), f32),
            pltpu.VMEM((128, 128), f32),
            pltpu.VMEM((edge_rows, 128), f32),
            pltpu.VMEM((edge_rows, 128), f32),
        ],
        1 << 27,
        passed=11,
    )(
        xt, outer, inner, hidden, main_second, taps_one, one_turned, bias_one, taps_two, two, bias_two
    )
    seen = lax.all_to_all(send, "member", 0, 0, tiled=True)
    cot, out = call(
        functools.partial(crps_kernel, rows * cols * tiles),
        (shape((members, chunk, 128), bf16), shape((1, 16, rows, cols), bf16)),
        [pltpu.SemaphoreType.DMA],
        1 << 24,
        passed=5,
        out_specs=(pl.BlockSpec(memory_space=pltpu.VMEM), pl.BlockSpec(memory_space=pltpu.HBM)),
    )(seen, target, outer, inner, send)
    cot = lax.all_to_all(cot, "member", 0, 0, tiled=True)
    packed = call(
        backward_kernel,
        shape((16, 4, 128), f32),
        [
            pltpu.VMEM((16 * chunk_pitch + 40, 128), f32),
            pltpu.VMEM((slabs + 2, pitch, 128), f32),
            pltpu.VMEM((19, 8, 128), f32),
            pltpu.VMEM((128, 128), f32),
            pltpu.VMEM((32, 128), f32),
            pltpu.VMEM((128, 128), f32),
            pltpu.VMEM((64, 128), f32),
        ],
        1 << 28,
        passed=12,
    )(
        cot, xs, first, gate, hidden, edge_first, edge_gate, edge_hidden, second, one, two, taps_two
    )
    axes = ("member", "tile")
    near = [[16 * g + k for k in range(16)] for g in range(members * tiles // 16)]
    far = [list(group) for group in zip(*near)]
    part = lax.all_to_all(packed, axes, 0, 0, tiled=True, axis_index_groups=near)
    part = jnp.sum(part, axis=0)
    part = jnp.broadcast_to(part[None], (len(near),) + part.shape)
    part = lax.all_to_all(part, axes, 0, 0, tiled=True, axis_index_groups=far)
    part = jnp.sum(part, axis=0)
    part = jnp.broadcast_to(part[None], (len(far),) + part.shape)
    total = lax.all_to_all(part, axes, 0, 0, tiled=True, axis_index_groups=near)
    g_depth_one, g_point_one, g_bias_one, g_depth_two, g_point_two, g_bias_two = call(
        output_kernel,
        (
            shape((9, 64), f32),
            shape((64, 64), f32),
            shape((1, 64), f32),
            shape((9, 64), f32),
            shape((16, 64), f32),
            shape((1, 16), f32),
        ),
        [pltpu.VMEM((64, 128), f32)],
        1 << 20,
        passed=1,
    )(total)
    return (
        out,
        g_depth_one.T,
        g_point_one,
        g_bias_one[0],
        g_depth_two.T,
        g_point_two,
        g_bias_two[0],
    )


def solution(mesh):
    return jax.shard_map(
        local,
        mesh=mesh,
        in_specs=(
            P("member", None, None, "tile"),
            P(None, None, "tile"),
            P(),
            P(),
            P(),
            P(),
            P(),
            P(),
        ),
        out_specs=(P("member", None, None, "tile"), P(), P(), P(), P(), P(), P()),
        check_vma=False,
    )
```

```python
import functools

import jax
import jax.numpy as jnp
from jax import lax
from jax.experimental import pallas as pl
from jax.experimental.pallas import tpu as pltpu
from jax.sharding import PartitionSpec as P

smooth_width = 0.25
pair_weight = 0.95

slabs = 16
pitch = 160
own = 16
chunk = 40
chunk_pitch = 50
lat_pitch = 34
edge_rows = 56

f32 = jnp.float32
bf16 = jnp.bfloat16


def lanes_of(shape):
    return lax.broadcasted_iota(jnp.int32, shape, len(shape) - 1)


def dot(left, right, left_dim, right_dim):
    return lax.dot_general(
        left, right, (((left_dim,), (right_dim,)), ((), ())), preferred_element_type=f32
    )


def rounded(value):
    return value.astype(bf16).astype(f32)


def wrap_slabs(ref):
    last = pltpu.roll(ref[slabs], 64, 1)
    ref[0] = jnp.where(lanes_of(last.shape) >= 64, last, 0.0)
    first = pltpu.roll(ref[1], 64, 1)
    ref[slabs + 1] = jnp.where(lanes_of(first.shape) < 64, first, 0.0)


def both_halves(row):
    return jnp.concatenate([row, row], axis=1)


def each_slab(body):
    for p in range(slabs):
        body(p)


def in_turn(make, ref, use):
    for p in (0, slabs - 1, 1):
        make(p)
    wrap_slabs(ref)
    for p in range(slabs):
        if p + 2 < slabs - 1:
            make(p + 2)
        use(p)


def fetch(sources, places, sems):
    copies = [
        pltpu.make_async_copy(source, place, sems.at[k])
        for k, (source, place) in enumerate(zip(sources, places))
    ]
    for copy in copies:
        copy.start()
    return copies


def even_tile():
    return lax.rem(lax.axis_index("tile"), 2) == 0


def edge_kernel(
    x_hbm, target_hbm, depth_one_hbm, point_one_hbm, bias_one_hbm, depth_two_hbm, point_two_hbm,
    bias_two_hbm,
    xt_ref, outer_ref, inner_ref, d1_ref, p1_ref, b1_ref, d2_ref, p2_ref, b2_ref,
    x_ref, target_ref, rows_scr, first_ref, last_ref, sems,
):
    sources = (
        target_hbm, x_hbm.at[0], depth_one_hbm, point_one_hbm, bias_one_hbm, depth_two_hbm,
        point_two_hbm, bias_two_hbm,
    )
    places = (target_ref, x_ref, d1_ref, p1_ref, b1_ref, d2_ref, p2_ref, b2_ref)
    target_copy, x_copy, *weight_copies = fetch(sources, places, sems)
    target_copy.wait()
    for k in range(4):
        turned = target_ref[4 * k : 4 * k + 4].reshape(128, 128).T
        first_ref[48 + k : 49 + k, :] = turned[0:1]
        last_ref[48 + k : 49 + k, :] = turned[127:128]
    first_ref[52:56, :] = jnp.zeros((4, 128), f32)
    last_ref[52:56, :] = jnp.zeros((4, 128), f32)
    x_copy.wait()
    for c in range(64):
        rows_scr[lat_pitch * c : lat_pitch * c + 32, :] = x_ref[c].astype(f32)

    def body(p):
        here = jnp.concatenate(
            [rows_scr[pl.ds(p, 64, stride=lat_pitch), :], rows_scr[pl.ds(p + 16, 64, stride=lat_pitch), :]],
            axis=0,
        )
        turned = here.T
        xt_ref[p] = turned
        for j in range(3):
            first_ref[pl.ds(16 * j + p, 1), :] = turned[j : j + 1]
            last_ref[pl.ds(16 * j + p, 1), :] = turned[125 + j : 126 + j]

    each_slab(body)
    even = even_tile()
    first, last = first_ref[...], last_ref[...]
    outer_ref[...] = jnp.where(even, first, last)
    inner_ref[...] = jnp.where(even, last, first)
    for copy in weight_copies:
        copy.wait()


def main_kernel(
    d1_ref, p1_ref, b1_ref, d2_ref, p2_ref, b2_ref, xt_ref,
    taps_one_ref, one_ref, one_turned_ref, bias_one_ref, taps_two_ref, two_ref, bias_two_ref,
    first_ref, gate_ref, hidden_ref, second_ref,
    turn_ref, xs_ref, hs_ref,
):
    turn_ref[...] = jnp.zeros((128, 128), f32)
    for p in range(slabs):
        xs_ref[p + 1] = xt_ref[p]
    wrap_slabs(xs_ref)
    zero = jnp.zeros((7, 128), f32)
    taps_one_ref[...] = jnp.concatenate([both_halves(d1_ref[...]), zero], axis=0)
    taps_two_ref[...] = jnp.concatenate([both_halves(d2_ref[...]), zero], axis=0)
    bias_one_ref[...] = jnp.broadcast_to(both_halves(b1_ref[...]), (8, 128))
    turn_ref[0:1, 0:16] = b2_ref[...]
    column = jnp.broadcast_to(turn_ref[...].T[0:16, 0:1], (16, 128))
    bias_two_ref[0:16] = column
    bias_two_ref[16:32] = column
    turn_ref[0:1, :] = jnp.zeros((1, 128), f32)
    weight = p1_ref[...].astype(f32)
    turn_ref[0:64, 0:64] = weight
    turn_ref[64:128, 64:128] = weight
    one_ref[...] = turn_ref[...].astype(bf16)
    one_turned = turn_ref[...].T.astype(bf16)
    one_turned_ref[...] = one_turned
    weight = p2_ref[...].astype(f32)
    zero = jnp.zeros((16, 64), f32)
    two_ref[...] = jnp.concatenate(
        [jnp.concatenate([weight, zero], axis=1), jnp.concatenate([zero, weight], axis=1)], axis=0
    ).astype(bf16)

    def first_body(p):
        first = rounded(depthwise(taps_one_ref, xs_ref, p, 7, 112))
        first_ref[p] = first
        hidden, gate = activation(first, one_turned, bias_one_ref)
        hidden_ref[p] = hidden
        hs_ref[p + 1] = hidden
        gate_ref[p] = gate

    def second_body(p):
        second_ref[p] = depthwise(taps_two_ref, hs_ref, p, 7, 96).astype(bf16)

    in_turn(first_body, hs_ref, second_body)


def depthwise(taps_ref, ref, p, row, count):
    total = None
    for a in range(3):
        for b in range(3):
            tap = taps_ref[3 * a + b : 3 * a + b + 1, :]
            term = tap * ref[p + a, row + b : row + b + count, :]
            total = term if total is None else total + term
    return total


def activation(first, one_turned, bias_ref):
    pre = dot(first.astype(bf16), one_turned, 1, 0) + bias_ref[0:1]
    gate = 1.0 / (1.0 + jnp.exp(-pre))
    return rounded(pre * gate), gate * (1.0 + pre * (1.0 - gate))


def with_edges(main, edge):
    return jnp.concatenate([edge[0:8], main, edge[8:16]], axis=0)


def halo_kernel(
    xt_ref, outer_ref, inner_ref, hidden_ref, main_second_ref,
    taps_one_ref, one_turned_ref, bias_one_ref, taps_two_ref, two_ref, bias_ref,
    send_ref, xs_ref, first_ref, gate_ref, edge_hidden_ref, second_ref,
    hs_ref, y_ref, edge_ref, left_ref, right_ref,
):
    two = two_ref[...]
    even = even_tile()
    outer, inner = outer_ref[...], inner_ref[...]
    left_ref[...] = jnp.where(even, outer, inner)
    right_ref[...] = jnp.where(even, inner, outer)

    for k in range(slabs + 2):
        xs_ref[k, 0:16, :] = jnp.zeros((16, 128), f32)
        xs_ref[k, 144:160, :] = jnp.zeros((16, 128), f32)
    for p in range(slabs):
        xs_ref[p + 1, own : own + 128, :] = xt_ref[p]
        for j in range(3):
            xs_ref[p + 1, 13 + j : 14 + j, :] = left_ref[16 * j + p : 16 * j + p + 1, :]
            xs_ref[p + 1, 144 + j : 145 + j, :] = right_ref[16 * j + p : 16 * j + p + 1, :]
    wrap_slabs(xs_ref)

    one_turned = one_turned_ref[...]
    for k in range(0, slabs, 8):
        first = [
            depthwise(taps_one_ref, xs_ref, p, row, 16) for p in range(k, k + 8) for row in (7, 135)
        ]
        first = rounded(jnp.concatenate(first, axis=0))
        hidden, gate = activation(first, one_turned, bias_one_ref)
        for p in range(k, k + 8):
            at = 32 * (p - k)
            rows = slice(at + 8, at + 24)
            first_ref[p] = first[rows]
            gate_ref[p] = gate[rows]
            edge_hidden_ref[p] = hidden[rows]
            hs_ref[p + 1, 0:8, :] = jnp.zeros((8, 128), f32)
            hs_ref[p + 1, 8:24, :] = hidden[at : at + 16]
            hs_ref[p + 1, 24:40, :] = hidden_ref[p, 0:16, :]
            hs_ref[p + 1, 40:56, :] = hidden_ref[p, 96:112, :]
            hs_ref[p + 1, 56:72, :] = hidden[at + 16 : at + 32]
            hs_ref[p + 1, 72:80, :] = jnp.zeros((8, 128), f32)
    wrap_slabs(hs_ref)
    y_ref[...] = jnp.zeros(y_ref.shape, f32)
    edge_ref[...] = jnp.zeros(edge_ref.shape, f32)

    def second_body(p):
        before = depthwise(taps_two_ref, hs_ref, p, 7, 24)
        after = depthwise(taps_two_ref, hs_ref, p, 47, 24)
        edge_ref[pl.ds(p, 1), :] = before[7:8]
        edge_ref[pl.ds(16 + p, 1), :] = after[16:17]
        second = jnp.concatenate(
            [before[8:24].astype(bf16), main_second_ref[p], after[0:16].astype(bf16)], axis=0
        )
        second_ref[p] = second
        y = dot(two, second, 1, 1) + bias_ref[...]
        y_ref[pl.ds(p, 16, stride=chunk_pitch), :] = y[0:16]
        y_ref[pl.ds(16 + p, 16, stride=chunk_pitch), :] = y[16:32]

    each_slab(second_body)
    y = dot(two, edge_ref[...].astype(bf16), 1, 1) + bias_ref[...]
    lane = lanes_of((16, 128))
    y = jnp.where(lane < 32, y[0:16], jnp.where(lane < 64, pltpu.roll(y[16:32], 32, 1), 0.0))
    y_ref[pl.ds(32, 16, stride=chunk_pitch), :] = y
    for o in range(16):
        send_ref[o] = y_ref[chunk_pitch * o : chunk_pitch * o + chunk, :].astype(bf16)


def slope(diff):
    return diff * lax.rsqrt(diff * diff + smooth_width * smooth_width)


def crps_kernel(
    cells_all, x_ref, target_ref, outer_ref, inner_ref, send_ref, out_ref, forecast_hbm, sem
):
    forecast_copy = pltpu.make_async_copy(send_ref.at[:, 0:32], forecast_hbm.at[0], sem)
    forecast_copy.start()
    members = x_ref.shape[0]
    me = lax.axis_index("member")
    turn = lax.rem(4 - lax.rem(me, 4), 4) * 32
    even = even_tile()
    outer = outer_ref[pl.ds(48 + me // 4, 1), :]
    inner = inner_ref[pl.ds(48 + me // 4, 1), :]
    left = jnp.where(even, outer, inner)
    right = jnp.where(even, inner, outer)
    left = pltpu.roll(jnp.broadcast_to(left, (8, 128)), turn, 1)
    right = pltpu.roll(jnp.broadcast_to(right, (8, 128)), turn, 1)
    lane = lanes_of((8, 128))
    halo = jnp.where(
        lane < 16,
        left,
        jnp.where(
            lane < 32,
            pltpu.roll(right, 16, 1),
            jnp.where(lane < 48, pltpu.roll(left, 16, 1), pltpu.roll(right, 32, 1)),
        ),
    )
    for rows in (slice(0, 16), slice(16, 32), slice(32, 40)):
        x = [x_ref[i, rows, :].astype(f32) for i in range(members)]
        total = [None] * members
        for i in range(members):
            for j in range(i + 1, members):
                s = slope(x[i] - x[j])
                total[i] = s if total[i] is None else total[i] + s
                total[j] = -s if total[j] is None else total[j] - s
        aim = halo if rows.start == 32 else target_ref[me, rows, :]
        for i in range(members):
            value = slope(x[i] - aim) - pair_weight / (members - 1) * total[i]
            out_ref[i, rows, :] = (value / cells_all).astype(bf16)
    forecast_copy.wait()


def tap_sum(value):
    return jnp.sum(value.reshape(16, 8, 128), axis=0)


def backward_kernel(
    cot_ref, xs_ref, first_ref, gate_ref, hidden_ref, edge_first_ref, edge_gate_ref, edge_hidden_ref,
    second_ref, one_ref, two_ref, taps_two_ref,
    out_ref,
    cf_ref, bs_ref, sums_ref, cot_sum_ref, point_two_ref, point_one_ref, other_ref,
):
    for o in range(16):
        cf_ref[chunk_pitch * o : chunk_pitch * o + chunk, :] = cot_ref[o].astype(f32)
    two = two_ref[...]
    one = one_ref[...]
    sums_ref[...] = jnp.zeros(sums_ref.shape, f32)
    cot_sum_ref[...] = jnp.zeros(cot_sum_ref.shape, f32)
    point_two_ref[...] = jnp.zeros(point_two_ref.shape, f32)
    point_one_ref[...] = jnp.zeros(point_one_ref.shape, f32)
    other_ref[...] = jnp.zeros(other_ref.shape, f32)

    def cot_body(p):
        cot = jnp.concatenate(
            [cf_ref[pl.ds(p, 16, stride=chunk_pitch), :], cf_ref[pl.ds(16 + p, 16, stride=chunk_pitch), :]], axis=0
        )
        cot_sum_ref[0:32] += cot
        cot = cot.astype(bf16)
        bs_ref[p + 1, own : own + 128, :] = rounded(dot(cot, two, 0, 0))
        point_two_ref[...] += dot(cot, second_ref[p], 1, 0)

    each_slab(cot_body)
    halo = cf_ref[pl.ds(32, 16, stride=chunk_pitch), :]
    halo = jnp.concatenate([halo, pltpu.roll(halo, 96, 1)], axis=0).astype(bf16)
    halo = rounded(dot(halo, two, 0, 0))
    for p in range(slabs):
        bs_ref[p + 1, 15:16, :] = halo[p : p + 1]
        bs_ref[p + 1, 144:145, :] = halo[16 + p : 17 + p]
    wrap_slabs(bs_ref)

    def body(p):
        total = None
        hidden = with_edges(hidden_ref[p], edge_hidden_ref[p])
        for a in range(3):
            for b in range(3):
                t = 3 * a + b
                back = bs_ref[p + 2 - a, 17 - b : 145 - b, :]
                term = taps_two_ref[t : t + 1, :] * back
                total = term if total is None else total + term
                sums_ref[9 + t] += tap_sum(back * hidden)
        back_pre = (total * with_edges(gate_ref[p], edge_gate_ref[p])).astype(bf16)
        sums_ref[18] += tap_sum(back_pre.astype(f32))
        first = with_edges(first_ref[p], edge_first_ref[p]).astype(bf16)
        point_one_ref[...] += dot(back_pre, first, 0, 0)
        back_first = dot(back_pre, one, 1, 0)
        for a in range(3):
            for b in range(3):
                sums_ref[3 * a + b] += tap_sum(back_first * xs_ref[p + a, 15 + b : 143 + b, :])

    each_slab(body)
    for t in range(19):
        total = jnp.sum(sums_ref[t], axis=0, keepdims=True)
        other_ref[t : t + 1, :] = total + pltpu.roll(total, 64, 1)
    other_ref[24:40, :] = pltpu.roll(point_two_ref[0:16], 64, 1) + point_two_ref[16:32]
    bias_two = jnp.sum(cot_sum_ref[...].T, axis=0, keepdims=True)
    bias_two = bias_two + pltpu.roll(bias_two, 112, 1)
    other_ref[19:20, :] = pltpu.roll(bias_two, 64, 1)
    point_one = point_one_ref[0:64] + pltpu.roll(point_one_ref[64:128], 64, 1)
    packed = jnp.where(lanes_of((64, 128)) < 64, point_one, other_ref[...])
    out_ref[...] = packed.reshape(out_ref.shape)


def output_kernel(total_ref, depth_one_ref, point_one_ref, bias_one_ref, depth_two_ref, point_two_ref, bias_two_ref, rows_ref):
    rows_ref[...] = total_ref[...].reshape(64, 128)
    point_one_ref[...] = rows_ref[:, 0:64]
    depth_one_ref[...] = rows_ref[0:9, 64:128]
    depth_two_ref[...] = rows_ref[9:18, 64:128]
    bias_one_ref[...] = rows_ref[18:19, 64:128]
    bias_two_ref[...] = rows_ref[19:20, 64:80]
    point_two_ref[...] = rows_ref[24:40, 64:128]


def call(kernel, out_shape, scratch, flops, fetched=0, passed=0, **out):
    hbm = pl.BlockSpec(memory_space=pltpu.HBM)
    vmem = pl.BlockSpec(memory_space=pltpu.VMEM)
    return pl.pallas_call(
        kernel,
        out_shape=out_shape,
        in_specs=[hbm] * fetched + [vmem] * passed,
        scratch_shapes=scratch,
        **out,
        compiler_params=pltpu.CompilerParams(vmem_limit_bytes=24 * 1024 * 1024),
        cost_estimate=pl.CostEstimate(flops=flops, bytes_accessed=4 << 20, transcendentals=0),
    )


def in_hbm(*arrays):
    return [pltpu.with_memory_space_constraint(array, pltpu.HBM) for array in arrays]


def shape(dims, dtype):
    return jax.ShapeDtypeStruct(dims, dtype)


def local(predictor_inputs, target, depth_one, point_one, bias_one, depth_two, point_two, bias_two):
    members = lax.axis_size("member")
    tiles = lax.axis_size("tile")
    _, chans, rows, cols = predictor_inputs.shape
    slab = (slabs, cols, 128)
    xt, outer, inner, *weights = call(
        edge_kernel,
        (
            shape(slab, f32),
            shape((edge_rows, 128), f32),
            shape((edge_rows, 128), f32),
            shape((9, 64), f32),
            shape((64, 64), bf16),
            shape((1, 64), f32),
            shape((9, 64), f32),
            shape((16, 64), bf16),
            shape((1, 16), f32),
        ),
        [
            pltpu.VMEM((chans, rows, cols), bf16),
            pltpu.VMEM((16, rows, cols), f32),
            pltpu.VMEM((chans * lat_pitch + 32, 128), f32),
            pltpu.VMEM((edge_rows, 128), f32),
            pltpu.VMEM((edge_rows, 128), f32),
            pltpu.SemaphoreType.DMA((8,)),
        ],
        1 << 20,
        fetched=8,
    )(
        *in_hbm(
            predictor_inputs, target, depth_one.T, point_one, bias_one[None], depth_two.T, point_two,
            bias_two[None],
        )
    )
    outer = lax.ppermute(outer, "tile", [(i, (i + 2 * (i % 2) - 1) % tiles) for i in range(tiles)])
    inner = lax.ppermute(inner, "tile", [(i, i + 1 - 2 * (i % 2)) for i in range(tiles)])
    (
        taps_one, one, one_turned, bias_one, taps_two, two, bias_two,
        first, gate, hidden, main_second,
    ) = call(
        main_kernel,
        (
            shape((16, 128), f32),
            shape((128, 128), bf16),
            shape((128, 128), bf16),
            shape((8, 128), f32),
            shape((16, 128), f32),
            shape((32, 128), bf16),
            shape((32, 128), f32),
            shape((slabs, 112, 128), f32),
            shape((slabs, 112, 128), f32),
            shape((slabs, 112, 128), f32),
            shape((slabs, 96, 128), bf16),
        ),
        [
            pltpu.VMEM((128, 128), f32),
            pltpu.VMEM((slabs + 2, cols, 128), f32),
            pltpu.VMEM((slabs + 2, 112, 128), f32),
        ],
        1 << 28,
        passed=7,
    )(*weights, xt)
    edge = (slabs, 16, 128)
    send, xs, edge_first, edge_gate, edge_hidden, second = call(
        halo_kernel,
        (
            shape((16, chunk, 128), bf16),
            shape((slabs + 2, pitch, 128), f32),
            shape(edge, f32),
            shape(edge, f32),
            shape(edge, f32),
            shape(slab, bf16),
        ),
        [
            pltpu.VMEM((slabs + 2, 80, 128), f32),
            pltpu.VMEM((16 * chunk_pitch + 40, 128), f32),
            pltpu.VMEM((128, 128), f32),
            pltpu.VMEM((edge_rows, 128), f32),
            pltpu.VMEM((edge_rows, 128), f32),
        ],
        1 << 27,
        passed=11,
    )(
        xt, outer, inner, hidden, main_second, taps_one, one_turned, bias_one, taps_two, two, bias_two
    )
    seen = lax.all_to_all(send, "member", 0, 0, tiled=True)
    cot, out = call(
        functools.partial(crps_kernel, rows * cols * tiles),
        (shape((members, chunk, 128), bf16), shape((1, 16, rows, cols), bf16)),
        [pltpu.SemaphoreType.DMA],
        1 << 24,
        passed=5,
        out_specs=(pl.BlockSpec(memory_space=pltpu.VMEM), pl.BlockSpec(memory_space=pltpu.HBM)),
    )(seen, target, outer, inner, send)
    cot = lax.all_to_all(cot, "member", 0, 0, tiled=True)
    packed = call(
        backward_kernel,
        shape((16, 4, 128), f32),
        [
            pltpu.VMEM((16 * chunk_pitch + 40, 128), f32),
            pltpu.VMEM((slabs + 2, pitch, 128), f32),
            pltpu.VMEM((19, 8, 128), f32),
            pltpu.VMEM((128, 128), f32),
            pltpu.VMEM((32, 128), f32),
            pltpu.VMEM((128, 128), f32),
            pltpu.VMEM((64, 128), f32),
        ],
        1 << 28,
        passed=12,
    )(
        cot, xs, first, gate, hidden, edge_first, edge_gate, edge_hidden, second, one, two, taps_two
    )
    axes = ("member", "tile")
    near = [
        [32 * (2 * y + x_hi) + 2 * pair + core for y in range(8) for core in range(2)]
        for x_hi in range(2)
        for pair in range(16)
    ]
    far = [list(group) for group in zip(*near)]
    part = lax.all_to_all(packed, axes, 0, 0, tiled=True, axis_index_groups=near)
    part = jnp.sum(part, axis=0)
    part = jnp.broadcast_to(part[None], (len(near),) + part.shape)
    part = lax.all_to_all(part, axes, 0, 0, tiled=True, axis_index_groups=far)
    part = jnp.sum(part, axis=0)
    part = jnp.broadcast_to(part[None], (len(far),) + part.shape)
    total = lax.all_to_all(part, axes, 0, 0, tiled=True, axis_index_groups=near)
    g_depth_one, g_point_one, g_bias_one, g_depth_two, g_point_two, g_bias_two = call(
        output_kernel,
        (
            shape((9, 64), f32),
            shape((64, 64), f32),
            shape((1, 64), f32),
            shape((9, 64), f32),
            shape((16, 64), f32),
            shape((1, 16), f32),
        ),
        [pltpu.VMEM((64, 128), f32)],
        1 << 20,
        passed=1,
    )(total)
    return (
        out,
        g_depth_one.T,
        g_point_one,
        g_bias_one[0],
        g_depth_two.T,
        g_point_two,
        g_bias_two[0],
    )


def solution(mesh):
    return jax.shard_map(
        local,
        mesh=mesh,
        in_specs=(
            P("member", None, None, "tile"),
            P(None, None, "tile"),
            P(),
            P(),
            P(),
            P(),
            P(),
            P(),
        ),
        out_specs=(P("member", None, None, "tile"), P(), P(), P(), P(), P(), P()),
        check_vma=False,
    )
```

```python
import functools

import jax
import jax.numpy as jnp
from jax import lax
from jax.experimental import pallas as pl
from jax.experimental.pallas import tpu as pltpu
from jax.sharding import PartitionSpec as P

smooth_width = 0.25
pair_weight = 0.95

slabs = 16
pitch = 160
own = 16
chunk = 40
chunk_pitch = 50
lat_pitch = 34
edge_rows = 56

f32 = jnp.float32
bf16 = jnp.bfloat16


def lanes_of(shape):
    return lax.broadcasted_iota(jnp.int32, shape, len(shape) - 1)


def dot(left, right, left_dim, right_dim):
    return lax.dot_general(
        left, right, (((left_dim,), (right_dim,)), ((), ())), preferred_element_type=f32
    )


def rounded(value):
    return value.astype(bf16).astype(f32)


def wrap_slabs(ref):
    last = pltpu.roll(ref[slabs], 64, 1)
    ref[0] = jnp.where(lanes_of(last.shape) >= 64, last, 0.0)
    first = pltpu.roll(ref[1], 64, 1)
    ref[slabs + 1] = jnp.where(lanes_of(first.shape) < 64, first, 0.0)


def both_halves(row):
    return jnp.concatenate([row, row], axis=1)


def each_slab(body):
    for p in range(slabs):
        body(p)


def in_turn(make, ref, use):
    for p in (0, slabs - 1, 1):
        make(p)
    wrap_slabs(ref)
    for p in range(slabs):
        if p + 2 < slabs - 1:
            make(p + 2)
        use(p)


def fetch(sources, places, sems):
    copies = [
        pltpu.make_async_copy(source, place, sems.at[k])
        for k, (source, place) in enumerate(zip(sources, places))
    ]
    for copy in copies:
        copy.start()
    return copies


def even_tile():
    return lax.rem(lax.axis_index("tile"), 2) == 0


def edge_kernel(
    x_hbm, target_hbm, depth_one_hbm, point_one_hbm, bias_one_hbm, depth_two_hbm, point_two_hbm,
    bias_two_hbm,
    xt_ref, outer_ref, inner_ref, d1_ref, p1_ref, b1_ref, d2_ref, p2_ref, b2_ref,
    x_ref, target_ref, rows_scr, first_ref, last_ref, sems,
):
    sources = (
        target_hbm, x_hbm.at[0], depth_one_hbm, point_one_hbm, bias_one_hbm, depth_two_hbm,
        point_two_hbm, bias_two_hbm,
    )
    places = (target_ref, x_ref, d1_ref, p1_ref, b1_ref, d2_ref, p2_ref, b2_ref)
    target_copy, x_copy, *weight_copies = fetch(sources, places, sems)
    target_copy.wait()
    for k in range(4):
        turned = target_ref[4 * k : 4 * k + 4].reshape(128, 128).T
        first_ref[48 + k : 49 + k, :] = turned[0:1]
        last_ref[48 + k : 49 + k, :] = turned[127:128]
    first_ref[52:56, :] = jnp.zeros((4, 128), f32)
    last_ref[52:56, :] = jnp.zeros((4, 128), f32)
    x_copy.wait()
    for c in range(64):
        rows_scr[lat_pitch * c : lat_pitch * c + 32, :] = x_ref[c].astype(f32)

    def body(p):
        here = jnp.concatenate(
            [rows_scr[pl.ds(p, 64, stride=lat_pitch), :], rows_scr[pl.ds(p + 16, 64, stride=lat_pitch), :]],
            axis=0,
        )
        turned = here.T
        xt_ref[p] = turned
        for j in range(3):
            first_ref[pl.ds(16 * j + p, 1), :] = turned[j : j + 1]
            last_ref[pl.ds(16 * j + p, 1), :] = turned[125 + j : 126 + j]

    each_slab(body)
    even = even_tile()
    first, last = first_ref[...], last_ref[...]
    outer_ref[...] = jnp.where(even, first, last)
    inner_ref[...] = jnp.where(even, last, first)
    for copy in weight_copies:
        copy.wait()


def main_kernel(
    d1_ref, p1_ref, b1_ref, d2_ref, p2_ref, b2_ref, xt_ref,
    taps_one_ref, one_ref, one_turned_ref, bias_one_ref, taps_two_ref, two_ref, bias_two_ref,
    first_ref, gate_ref, hidden_ref, second_ref,
    turn_ref, xs_ref, hs_ref,
):
    turn_ref[...] = jnp.zeros((128, 128), f32)
    for p in range(slabs):
        xs_ref[p + 1] = xt_ref[p]
    wrap_slabs(xs_ref)
    zero = jnp.zeros((7, 128), f32)
    taps_one_ref[...] = jnp.concatenate([both_halves(d1_ref[...]), zero], axis=0)
    taps_two_ref[...] = jnp.concatenate([both_halves(d2_ref[...]), zero], axis=0)
    bias_one_ref[...] = jnp.broadcast_to(both_halves(b1_ref[...]), (8, 128))
    turn_ref[0:1, 0:16] = b2_ref[...]
    column = jnp.broadcast_to(turn_ref[...].T[0:16, 0:1], (16, 128))
    bias_two_ref[0:16] = column
    bias_two_ref[16:32] = column
    turn_ref[0:1, :] = jnp.zeros((1, 128), f32)
    weight = p1_ref[...].astype(f32)
    turn_ref[0:64, 0:64] = weight
    turn_ref[64:128, 64:128] = weight
    one_ref[...] = turn_ref[...].astype(bf16)
    one_turned = turn_ref[...].T.astype(bf16)
    one_turned_ref[...] = one_turned
    weight = p2_ref[...].astype(f32)
    zero = jnp.zeros((16, 64), f32)
    two_ref[...] = jnp.concatenate(
        [jnp.concatenate([weight, zero], axis=1), jnp.concatenate([zero, weight], axis=1)], axis=0
    ).astype(bf16)

    def first_body(p):
        first = rounded(depthwise(taps_one_ref, xs_ref, p, 7, 112))
        first_ref[p] = first
        hidden, gate = activation(first, one_turned, bias_one_ref)
        hidden_ref[p] = hidden
        hs_ref[p + 1] = hidden
        gate_ref[p] = gate

    def second_body(p):
        second_ref[p] = depthwise(taps_two_ref, hs_ref, p, 7, 96).astype(bf16)

    in_turn(first_body, hs_ref, second_body)


def depthwise(taps_ref, ref, p, row, count):
    total = None
    for a in range(3):
        for b in range(3):
            tap = taps_ref[3 * a + b : 3 * a + b + 1, :]
            term = tap * ref[p + a, row + b : row + b + count, :]
            total = term if total is None else total + term
    return total


def activation(first, one_turned, bias_ref):
    pre = dot(first.astype(bf16), one_turned, 1, 0) + bias_ref[0:1]
    gate = 1.0 / (1.0 + jnp.exp(-pre))
    return rounded(pre * gate), gate * (1.0 + pre * (1.0 - gate))


def with_edges(main, edge):
    return jnp.concatenate([edge[0:8], main, edge[8:16]], axis=0)


def halo_kernel(
    xt_ref, outer_ref, inner_ref, hidden_ref, main_second_ref,
    taps_one_ref, one_turned_ref, bias_one_ref, taps_two_ref, two_ref, bias_ref,
    send_ref, xs_ref, first_ref, gate_ref, edge_hidden_ref, second_ref,
    hs_ref, y_ref, edge_ref, left_ref, right_ref,
):
    two = two_ref[...]
    even = even_tile()
    outer, inner = outer_ref[...], inner_ref[...]
    left_ref[...] = jnp.where(even, outer, inner)
    right_ref[...] = jnp.where(even, inner, outer)

    for k in range(slabs + 2):
        xs_ref[k, 0:16, :] = jnp.zeros((16, 128), f32)
        xs_ref[k, 144:160, :] = jnp.zeros((16, 128), f32)
    for p in range(slabs):
        xs_ref[p + 1, own : own + 128, :] = xt_ref[p]
        for j in range(3):
            xs_ref[p + 1, 13 + j : 14 + j, :] = left_ref[16 * j + p : 16 * j + p + 1, :]
            xs_ref[p + 1, 144 + j : 145 + j, :] = right_ref[16 * j + p : 16 * j + p + 1, :]
    wrap_slabs(xs_ref)

    one_turned = one_turned_ref[...]
    for k in range(0, slabs, 8):
        first = [
            depthwise(taps_one_ref, xs_ref, p, row, 16) for p in range(k, k + 8) for row in (7, 135)
        ]
        first = rounded(jnp.concatenate(first, axis=0))
        hidden, gate = activation(first, one_turned, bias_one_ref)
        for p in range(k, k + 8):
            at = 32 * (p - k)
            rows = slice(at + 8, at + 24)
            first_ref[p] = first[rows]
            gate_ref[p] = gate[rows]
            edge_hidden_ref[p] = hidden[rows]
            hs_ref[p + 1, 0:8, :] = jnp.zeros((8, 128), f32)
            hs_ref[p + 1, 8:24, :] = hidden[at : at + 16]
            hs_ref[p + 1, 24:40, :] = hidden_ref[p, 0:16, :]
            hs_ref[p + 1, 40:56, :] = hidden_ref[p, 96:112, :]
            hs_ref[p + 1, 56:72, :] = hidden[at + 16 : at + 32]
            hs_ref[p + 1, 72:80, :] = jnp.zeros((8, 128), f32)
    wrap_slabs(hs_ref)
    y_ref[...] = jnp.zeros(y_ref.shape, f32)
    edge_ref[...] = jnp.zeros(edge_ref.shape, f32)

    def second_body(p):
        before = depthwise(taps_two_ref, hs_ref, p, 7, 24)
        after = depthwise(taps_two_ref, hs_ref, p, 47, 24)
        edge_ref[pl.ds(p, 1), :] = before[7:8]
        edge_ref[pl.ds(16 + p, 1), :] = after[16:17]
        second = jnp.concatenate(
            [before[8:24].astype(bf16), main_second_ref[p], after[0:16].astype(bf16)], axis=0
        )
        second_ref[p] = second
        y = dot(two, second, 1, 1) + bias_ref[...]
        y_ref[pl.ds(p, 16, stride=chunk_pitch), :] = y[0:16]
        y_ref[pl.ds(16 + p, 16, stride=chunk_pitch), :] = y[16:32]

    each_slab(second_body)
    y = dot(two, edge_ref[...].astype(bf16), 1, 1) + bias_ref[...]
    lane = lanes_of((16, 128))
    y = jnp.where(lane < 32, y[0:16], jnp.where(lane < 64, pltpu.roll(y[16:32], 32, 1), 0.0))
    y_ref[pl.ds(32, 16, stride=chunk_pitch), :] = y
    for o in range(16):
        send_ref[o] = y_ref[chunk_pitch * o : chunk_pitch * o + chunk, :].astype(bf16)


def slope(diff):
    return diff * lax.rsqrt(diff * diff + smooth_width * smooth_width)


def crps_kernel(
    cells_all, x_ref, target_ref, outer_ref, inner_ref, send_ref, out_ref, forecast_hbm,
    value_ref, sem,
):
    forecast_copy = pltpu.make_async_copy(send_ref.at[:, 0:32], forecast_hbm.at[0], sem)
    forecast_copy.start()
    members = x_ref.shape[0]
    me = lax.axis_index("member")
    turn = lax.rem(4 - lax.rem(me, 4), 4) * 32
    even = even_tile()
    outer = outer_ref[pl.ds(48 + me // 4, 1), :]
    inner = inner_ref[pl.ds(48 + me // 4, 1), :]
    left = jnp.where(even, outer, inner)
    right = jnp.where(even, inner, outer)
    left = pltpu.roll(jnp.broadcast_to(left, (8, 128)), turn, 1)
    right = pltpu.roll(jnp.broadcast_to(right, (8, 128)), turn, 1)
    lane = lanes_of((8, 128))
    halo = jnp.where(
        lane < 16,
        left,
        jnp.where(
            lane < 32,
            pltpu.roll(right, 16, 1),
            jnp.where(lane < 48, pltpu.roll(left, 16, 1), pltpu.roll(right, 32, 1)),
        ),
    )
    for rows in (slice(0, 16), slice(16, 32), slice(32, 40)):
        x = [x_ref[i].astype(f32)[rows] for i in range(members)]
        total = [None] * members
        for i in range(members):
            for j in range(i + 1, members):
                s = slope(x[i] - x[j])
                total[i] = s if total[i] is None else total[i] + s
                total[j] = -s if total[j] is None else total[j] - s
        aim = halo if rows.start == 32 else target_ref[me, rows, :]
        for i in range(members):
            value = slope(x[i] - aim) - pair_weight / (members - 1) * total[i]
            value_ref[i, rows, :] = value / cells_all
    for i in range(members):
        out_ref[i] = value_ref[i].astype(bf16)
    forecast_copy.wait()


def tap_sum(value):
    return jnp.sum(value.reshape(16, 8, 128), axis=0)


def backward_kernel(
    cot_ref, xs_ref, first_ref, gate_ref, hidden_ref, edge_first_ref, edge_gate_ref, edge_hidden_ref,
    second_ref, one_ref, two_ref, taps_two_ref,
    out_ref,
    cf_ref, bs_ref, sums_ref, cot_sum_ref, point_two_ref, point_one_ref, other_ref,
):
    for o in range(16):
        cf_ref[chunk_pitch * o : chunk_pitch * o + chunk, :] = cot_ref[o].astype(f32)
    two = two_ref[...]
    one = one_ref[...]
    sums_ref[...] = jnp.zeros(sums_ref.shape, f32)
    cot_sum_ref[...] = jnp.zeros(cot_sum_ref.shape, f32)
    point_two_ref[...] = jnp.zeros(point_two_ref.shape, f32)
    point_one_ref[...] = jnp.zeros(point_one_ref.shape, f32)
    other_ref[...] = jnp.zeros(other_ref.shape, f32)

    def cot_body(p):
        cot = jnp.concatenate(
            [cf_ref[pl.ds(p, 16, stride=chunk_pitch), :], cf_ref[pl.ds(16 + p, 16, stride=chunk_pitch), :]], axis=0
        )
        cot_sum_ref[0:32] += cot
        cot = cot.astype(bf16)
        bs_ref[p + 1, own : own + 128, :] = rounded(dot(cot, two, 0, 0))
        point_two_ref[...] += dot(cot, second_ref[p], 1, 0)

    each_slab(cot_body)
    halo = cf_ref[pl.ds(32, 16, stride=chunk_pitch), :]
    halo = jnp.concatenate([halo, pltpu.roll(halo, 96, 1)], axis=0).astype(bf16)
    halo = rounded(dot(halo, two, 0, 0))
    for p in range(slabs):
        bs_ref[p + 1, 15:16, :] = halo[p : p + 1]
        bs_ref[p + 1, 144:145, :] = halo[16 + p : 17 + p]
    wrap_slabs(bs_ref)

    def body(p):
        total = None
        hidden = with_edges(hidden_ref[p], edge_hidden_ref[p])
        for a in range(3):
            for b in range(3):
                t = 3 * a + b
                back = bs_ref[p + 2 - a, 17 - b : 145 - b, :]
                term = taps_two_ref[t : t + 1, :] * back
                total = term if total is None else total + term
                sums_ref[9 + t] += tap_sum(back * hidden)
        back_pre = (total * with_edges(gate_ref[p], edge_gate_ref[p])).astype(bf16)
        sums_ref[18] += tap_sum(back_pre.astype(f32))
        first = with_edges(first_ref[p], edge_first_ref[p]).astype(bf16)
        point_one_ref[...] += dot(back_pre, first, 0, 0)
        back_first = dot(back_pre, one, 1, 0)
        for a in range(3):
            for b in range(3):
                sums_ref[3 * a + b] += tap_sum(back_first * xs_ref[p + a, 15 + b : 143 + b, :])

    each_slab(body)
    for t in range(19):
        total = jnp.sum(sums_ref[t], axis=0, keepdims=True)
        other_ref[t : t + 1, :] = total + pltpu.roll(total, 64, 1)
    other_ref[24:40, :] = pltpu.roll(point_two_ref[0:16], 64, 1) + point_two_ref[16:32]
    bias_two = jnp.sum(cot_sum_ref[...].T, axis=0, keepdims=True)
    bias_two = bias_two + pltpu.roll(bias_two, 112, 1)
    other_ref[19:20, :] = pltpu.roll(bias_two, 64, 1)
    point_one = point_one_ref[0:64] + pltpu.roll(point_one_ref[64:128], 64, 1)
    packed = jnp.where(lanes_of((64, 128)) < 64, point_one, other_ref[...])
    out_ref[...] = packed.reshape(out_ref.shape)


def output_kernel(total_ref, depth_one_ref, point_one_ref, bias_one_ref, depth_two_ref, point_two_ref, bias_two_ref, rows_ref):
    rows_ref[...] = total_ref[...].reshape(64, 128)
    point_one_ref[...] = rows_ref[:, 0:64]
    depth_one_ref[...] = rows_ref[0:9, 64:128]
    depth_two_ref[...] = rows_ref[9:18, 64:128]
    bias_one_ref[...] = rows_ref[18:19, 64:128]
    bias_two_ref[...] = rows_ref[19:20, 64:80]
    point_two_ref[...] = rows_ref[24:40, 64:128]


def call(kernel, out_shape, scratch, flops, fetched=0, passed=0, **out):
    hbm = pl.BlockSpec(memory_space=pltpu.HBM)
    vmem = pl.BlockSpec(memory_space=pltpu.VMEM)
    return pl.pallas_call(
        kernel,
        out_shape=out_shape,
        in_specs=[hbm] * fetched + [vmem] * passed,
        scratch_shapes=scratch,
        **out,
        compiler_params=pltpu.CompilerParams(vmem_limit_bytes=24 * 1024 * 1024),
        cost_estimate=pl.CostEstimate(flops=flops, bytes_accessed=4 << 20, transcendentals=0),
    )


def in_hbm(*arrays):
    return [pltpu.with_memory_space_constraint(array, pltpu.HBM) for array in arrays]


def shape(dims, dtype):
    return jax.ShapeDtypeStruct(dims, dtype)


def local(predictor_inputs, target, depth_one, point_one, bias_one, depth_two, point_two, bias_two):
    members = lax.axis_size("member")
    tiles = lax.axis_size("tile")
    _, chans, rows, cols = predictor_inputs.shape
    slab = (slabs, cols, 128)
    xt, outer, inner, *weights = call(
        edge_kernel,
        (
            shape(slab, f32),
            shape((edge_rows, 128), f32),
            shape((edge_rows, 128), f32),
            shape((9, 64), f32),
            shape((64, 64), bf16),
            shape((1, 64), f32),
            shape((9, 64), f32),
            shape((16, 64), bf16),
            shape((1, 16), f32),
        ),
        [
            pltpu.VMEM((chans, rows, cols), bf16),
            pltpu.VMEM((16, rows, cols), f32),
            pltpu.VMEM((chans * lat_pitch + 32, 128), f32),
            pltpu.VMEM((edge_rows, 128), f32),
            pltpu.VMEM((edge_rows, 128), f32),
            pltpu.SemaphoreType.DMA((8,)),
        ],
        1 << 20,
        fetched=8,
    )(
        *in_hbm(
            predictor_inputs, target, depth_one.T, point_one, bias_one[None], depth_two.T, point_two,
            bias_two[None],
        )
    )
    outer = lax.ppermute(outer, "tile", [(i, (i + 2 * (i % 2) - 1) % tiles) for i in range(tiles)])
    inner = lax.ppermute(inner, "tile", [(i, i + 1 - 2 * (i % 2)) for i in range(tiles)])
    (
        taps_one, one, one_turned, bias_one, taps_two, two, bias_two,
        first, gate, hidden, main_second,
    ) = call(
        main_kernel,
        (
            shape((16, 128), f32),
            shape((128, 128), bf16),
            shape((128, 128), bf16),
            shape((8, 128), f32),
            shape((16, 128), f32),
            shape((32, 128), bf16),
            shape((32, 128), f32),
            shape((slabs, 112, 128), f32),
            shape((slabs, 112, 128), f32),
            shape((slabs, 112, 128), f32),
            shape((slabs, 96, 128), bf16),
        ),
        [
            pltpu.VMEM((128, 128), f32),
            pltpu.VMEM((slabs + 2, cols, 128), f32),
            pltpu.VMEM((slabs + 2, 112, 128), f32),
        ],
        1 << 28,
        passed=7,
    )(*weights, xt)
    edge = (slabs, 16, 128)
    send, xs, edge_first, edge_gate, edge_hidden, second = call(
        halo_kernel,
        (
            shape((16, chunk, 128), bf16),
            shape((slabs + 2, pitch, 128), f32),
            shape(edge, f32),
            shape(edge, f32),
            shape(edge, f32),
            shape(slab, bf16),
        ),
        [
            pltpu.VMEM((slabs + 2, 80, 128), f32),
            pltpu.VMEM((16 * chunk_pitch + 40, 128), f32),
            pltpu.VMEM((128, 128), f32),
            pltpu.VMEM((edge_rows, 128), f32),
            pltpu.VMEM((edge_rows, 128), f32),
        ],
        1 << 27,
        passed=11,
    )(
        xt, outer, inner, hidden, main_second, taps_one, one_turned, bias_one, taps_two, two, bias_two
    )
    seen = lax.all_to_all(send, "member", 0, 0, tiled=True)
    cot, out = call(
        functools.partial(crps_kernel, rows * cols * tiles),
        (shape((members, chunk, 128), bf16), shape((1, 16, rows, cols), bf16)),
        [pltpu.VMEM((members, chunk, 128), f32), pltpu.SemaphoreType.DMA],
        1 << 24,
        passed=5,
        out_specs=(pl.BlockSpec(memory_space=pltpu.VMEM), pl.BlockSpec(memory_space=pltpu.HBM)),
    )(seen, target, outer, inner, send)
    cot = lax.all_to_all(cot, "member", 0, 0, tiled=True)
    packed = call(
        backward_kernel,
        shape((16, 4, 128), f32),
        [
            pltpu.VMEM((16 * chunk_pitch + 40, 128), f32),
            pltpu.VMEM((slabs + 2, pitch, 128), f32),
            pltpu.VMEM((19, 8, 128), f32),
            pltpu.VMEM((128, 128), f32),
            pltpu.VMEM((32, 128), f32),
            pltpu.VMEM((128, 128), f32),
            pltpu.VMEM((64, 128), f32),
        ],
        1 << 28,
        passed=12,
    )(
        cot, xs, first, gate, hidden, edge_first, edge_gate, edge_hidden, second, one, two, taps_two
    )
    axes = ("member", "tile")
    near = [[16 * g + k for k in range(16)] for g in range(members * tiles // 16)]
    far = [list(group) for group in zip(*near)]
    part = lax.all_to_all(packed, axes, 0, 0, tiled=True, axis_index_groups=near)
    part = jnp.sum(part, axis=0)
    part = jnp.broadcast_to(part[None], (len(near),) + part.shape)
    part = lax.all_to_all(part, axes, 0, 0, tiled=True, axis_index_groups=far)
    part = jnp.sum(part, axis=0)
    part = jnp.broadcast_to(part[None], (len(far),) + part.shape)
    total = lax.all_to_all(part, axes, 0, 0, tiled=True, axis_index_groups=near)
    g_depth_one, g_point_one, g_bias_one, g_depth_two, g_point_two, g_bias_two = call(
        output_kernel,
        (
            shape((9, 64), f32),
            shape((64, 64), f32),
            shape((1, 64), f32),
            shape((9, 64), f32),
            shape((16, 64), f32),
            shape((1, 16), f32),
        ),
        [pltpu.VMEM((64, 128), f32)],
        1 << 20,
        passed=1,
    )(total)
    return (
        out,
        g_depth_one.T,
        g_point_one,
        g_bias_one[0],
        g_depth_two.T,
        g_point_two,
        g_bias_two[0],
    )


def solution(mesh):
    return jax.shard_map(
        local,
        mesh=mesh,
        in_specs=(
            P("member", None, None, "tile"),
            P(None, None, "tile"),
            P(),
            P(),
            P(),
            P(),
            P(),
            P(),
        ),
        out_specs=(P("member", None, None, "tile"), P(), P(), P(), P(), P(), P()),
        check_vma=False,
    )
```

```python
import functools

import jax
import jax.numpy as jnp
from jax import lax
from jax.experimental import pallas as pl
from jax.experimental.pallas import tpu as pltpu
from jax.sharding import PartitionSpec as P

smooth_width = 0.25
pair_weight = 0.95

slabs = 16
pitch = 160
own = 16
chunk = 40
chunk_pitch = 50
lat_pitch = 34
edge_rows = 56

f32 = jnp.float32
bf16 = jnp.bfloat16


def lanes_of(shape):
    return lax.broadcasted_iota(jnp.int32, shape, len(shape) - 1)


def dot(left, right, left_dim, right_dim):
    return lax.dot_general(
        left, right, (((left_dim,), (right_dim,)), ((), ())), preferred_element_type=f32
    )


def rounded(value):
    return value.astype(bf16).astype(f32)


def wrap_slabs(ref):
    last = pltpu.roll(ref[slabs], 64, 1)
    ref[0] = jnp.where(lanes_of(last.shape) >= 64, last, 0.0)
    first = pltpu.roll(ref[1], 64, 1)
    ref[slabs + 1] = jnp.where(lanes_of(first.shape) < 64, first, 0.0)


def both_halves(row):
    return jnp.concatenate([row, row], axis=1)


def each_slab(body):
    for p in range(slabs):
        body(p)


def in_turn(make, ref, use):
    for p in (0, slabs - 1, 1):
        make(p)
    wrap_slabs(ref)
    for p in range(slabs):
        if p + 2 < slabs - 1:
            make(p + 2)
        use(p)


def fetch(sources, places, sems):
    copies = [
        pltpu.make_async_copy(source, place, sems.at[k])
        for k, (source, place) in enumerate(zip(sources, places))
    ]
    for copy in copies:
        copy.start()
    return copies


def even_tile():
    return lax.rem(lax.axis_index("tile"), 2) == 0


def edge_kernel(
    x_hbm, target_hbm, depth_one_hbm, point_one_hbm, bias_one_hbm, depth_two_hbm, point_two_hbm,
    bias_two_hbm,
    xt_ref, outer_ref, inner_ref, d1_ref, p1_ref, b1_ref, d2_ref, p2_ref, b2_ref,
    x_ref, target_ref, rows_scr, first_ref, last_ref, sems,
):
    sources = (
        target_hbm, x_hbm.at[0], depth_one_hbm, point_one_hbm, bias_one_hbm, depth_two_hbm,
        point_two_hbm, bias_two_hbm,
    )
    places = (target_ref, x_ref, d1_ref, p1_ref, b1_ref, d2_ref, p2_ref, b2_ref)
    target_copy, x_copy, *weight_copies = fetch(sources, places, sems)
    target_copy.wait()
    for k in range(4):
        turned = target_ref[4 * k : 4 * k + 4].reshape(128, 128).T
        first_ref[48 + k : 49 + k, :] = turned[0:1]
        last_ref[48 + k : 49 + k, :] = turned[127:128]
    first_ref[52:56, :] = jnp.zeros((4, 128), f32)
    last_ref[52:56, :] = jnp.zeros((4, 128), f32)
    x_copy.wait()
    for c in range(64):
        rows_scr[lat_pitch * c : lat_pitch * c + 32, :] = x_ref[c].astype(f32)

    def body(p):
        here = jnp.concatenate(
            [rows_scr[pl.ds(p, 64, stride=lat_pitch), :], rows_scr[pl.ds(p + 16, 64, stride=lat_pitch), :]],
            axis=0,
        )
        turned = here.T
        xt_ref[p] = turned
        for j in range(3):
            first_ref[pl.ds(16 * j + p, 1), :] = turned[j : j + 1]
            last_ref[pl.ds(16 * j + p, 1), :] = turned[125 + j : 126 + j]

    each_slab(body)
    even = even_tile()
    first, last = first_ref[...], last_ref[...]
    outer_ref[...] = jnp.where(even, first, last)
    inner_ref[...] = jnp.where(even, last, first)
    for copy in weight_copies:
        copy.wait()


def main_kernel(
    d1_ref, p1_ref, b1_ref, d2_ref, p2_ref, b2_ref, xt_ref,
    taps_one_ref, one_ref, one_turned_ref, bias_one_ref, taps_two_ref, two_ref, bias_two_ref,
    first_ref, gate_ref, hidden_ref, second_ref,
    turn_ref, xs_ref, hs_ref,
):
    turn_ref[...] = jnp.zeros((128, 128), f32)
    for p in range(slabs):
        xs_ref[p + 1] = xt_ref[p]
    wrap_slabs(xs_ref)
    zero = jnp.zeros((7, 128), f32)
    taps_one_ref[...] = jnp.concatenate([both_halves(d1_ref[...]), zero], axis=0)
    taps_two_ref[...] = jnp.concatenate([both_halves(d2_ref[...]), zero], axis=0)
    bias_one_ref[...] = jnp.broadcast_to(both_halves(b1_ref[...]), (8, 128))
    turn_ref[0:1, 0:16] = b2_ref[...]
    column = jnp.broadcast_to(turn_ref[...].T[0:16, 0:1], (16, 128))
    bias_two_ref[0:16] = column
    bias_two_ref[16:32] = column
    turn_ref[0:1, :] = jnp.zeros((1, 128), f32)
    weight = p1_ref[...].astype(f32)
    turn_ref[0:64, 0:64] = weight
    turn_ref[64:128, 64:128] = weight
    one_ref[...] = turn_ref[...].astype(bf16)
    one_turned = turn_ref[...].T.astype(bf16)
    one_turned_ref[...] = one_turned
    weight = p2_ref[...].astype(f32)
    zero = jnp.zeros((16, 64), f32)
    two_ref[...] = jnp.concatenate(
        [jnp.concatenate([weight, zero], axis=1), jnp.concatenate([zero, weight], axis=1)], axis=0
    ).astype(bf16)

    def first_body(p):
        first = rounded(depthwise(taps_one_ref, xs_ref, p, 7, 112))
        first_ref[p] = first
        hidden, gate = activation(first, one_turned, bias_one_ref)
        hidden_ref[p] = hidden
        hs_ref[p + 1] = hidden
        gate_ref[p] = gate

    def second_body(p):
        second_ref[p] = depthwise(taps_two_ref, hs_ref, p, 7, 96).astype(bf16)

    in_turn(first_body, hs_ref, second_body)


def depthwise(taps_ref, ref, p, row, count):
    total = None
    for a in range(3):
        for b in range(3):
            tap = taps_ref[3 * a + b : 3 * a + b + 1, :]
            term = tap * ref[p + a, row + b : row + b + count, :]
            total = term if total is None else total + term
    return total


def activation(first, one_turned, bias_ref):
    pre = dot(first.astype(bf16), one_turned, 1, 0) + bias_ref[0:1]
    gate = 1.0 / (1.0 + jnp.exp(-pre))
    return rounded(pre * gate), gate * (1.0 + pre * (1.0 - gate))


def with_edges(main, edge):
    return jnp.concatenate([edge[0:8], main, edge[8:16]], axis=0)


def halo_kernel(
    xt_ref, outer_ref, inner_ref, hidden_ref, main_second_ref,
    taps_one_ref, one_turned_ref, bias_one_ref, taps_two_ref, two_ref, bias_ref,
    send_ref, xs_ref, first_ref, gate_ref, edge_hidden_ref, second_ref,
    hs_ref, y_ref, edge_ref, left_ref, right_ref,
):
    two = two_ref[...]
    even = even_tile()
    outer, inner = outer_ref[...], inner_ref[...]
    left_ref[...] = jnp.where(even, outer, inner)
    right_ref[...] = jnp.where(even, inner, outer)

    for k in range(slabs + 2):
        xs_ref[k, 0:16, :] = jnp.zeros((16, 128), f32)
        xs_ref[k, 144:160, :] = jnp.zeros((16, 128), f32)
    for p in range(slabs):
        xs_ref[p + 1, own : own + 128, :] = xt_ref[p]
        for j in range(3):
            xs_ref[p + 1, 13 + j : 14 + j, :] = left_ref[16 * j + p : 16 * j + p + 1, :]
            xs_ref[p + 1, 144 + j : 145 + j, :] = right_ref[16 * j + p : 16 * j + p + 1, :]
    wrap_slabs(xs_ref)

    one_turned = one_turned_ref[...]
    for k in range(0, slabs, 8):
        first = [
            depthwise(taps_one_ref, xs_ref, p, row, 16) for p in range(k, k + 8) for row in (7, 135)
        ]
        first = rounded(jnp.concatenate(first, axis=0))
        hidden, gate = activation(first, one_turned, bias_one_ref)
        for p in range(k, k + 8):
            at = 32 * (p - k)
            rows = slice(at + 8, at + 24)
            first_ref[p] = first[rows]
            gate_ref[p] = gate[rows]
            edge_hidden_ref[p] = hidden[rows]
            hs_ref[p + 1, 0:8, :] = jnp.zeros((8, 128), f32)
            hs_ref[p + 1, 8:24, :] = hidden[at : at + 16]
            hs_ref[p + 1, 24:40, :] = hidden_ref[p, 0:16, :]
            hs_ref[p + 1, 40:56, :] = hidden_ref[p, 96:112, :]
            hs_ref[p + 1, 56:72, :] = hidden[at + 16 : at + 32]
            hs_ref[p + 1, 72:80, :] = jnp.zeros((8, 128), f32)
    wrap_slabs(hs_ref)
    y_ref[...] = jnp.zeros(y_ref.shape, f32)
    edge_ref[...] = jnp.zeros(edge_ref.shape, f32)

    def second_body(p):
        before = depthwise(taps_two_ref, hs_ref, p, 7, 24)
        after = depthwise(taps_two_ref, hs_ref, p, 47, 24)
        edge_ref[pl.ds(p, 1), :] = before[7:8]
        edge_ref[pl.ds(16 + p, 1), :] = after[16:17]
        second = jnp.concatenate(
            [before[8:24].astype(bf16), main_second_ref[p], after[0:16].astype(bf16)], axis=0
        )
        second_ref[p] = second
        y = dot(two, second, 1, 1) + bias_ref[...]
        y_ref[pl.ds(p, 16, stride=chunk_pitch), :] = y[0:16]
        y_ref[pl.ds(16 + p, 16, stride=chunk_pitch), :] = y[16:32]

    each_slab(second_body)
    y = dot(two, edge_ref[...].astype(bf16), 1, 1) + bias_ref[...]
    lane = lanes_of((16, 128))
    y = jnp.where(lane < 32, y[0:16], jnp.where(lane < 64, pltpu.roll(y[16:32], 32, 1), 0.0))
    y_ref[pl.ds(32, 16, stride=chunk_pitch), :] = y
    for o in range(16):
        send_ref[o] = y_ref[chunk_pitch * o : chunk_pitch * o + chunk, :].astype(bf16)


def slope(diff):
    return diff * lax.rsqrt(diff * diff + smooth_width * smooth_width)


def crps_kernel(
    cells_all, x_ref, target_ref, outer_ref, inner_ref, send_ref, out_ref, forecast_hbm,
    value_ref, sem,
):
    forecast_copy = pltpu.make_async_copy(send_ref.at[:, 0:32], forecast_hbm.at[0], sem)
    forecast_copy.start()
    members = x_ref.shape[0]
    me = lax.axis_index("member")
    turn = lax.rem(4 - lax.rem(me, 4), 4) * 32
    even = even_tile()
    outer = outer_ref[pl.ds(48 + me // 4, 1), :]
    inner = inner_ref[pl.ds(48 + me // 4, 1), :]
    left = jnp.where(even, outer, inner)
    right = jnp.where(even, inner, outer)
    left = pltpu.roll(jnp.broadcast_to(left, (8, 128)), turn, 1)
    right = pltpu.roll(jnp.broadcast_to(right, (8, 128)), turn, 1)
    lane = lanes_of((8, 128))
    halo = jnp.where(
        lane < 16,
        left,
        jnp.where(
            lane < 32,
            pltpu.roll(right, 16, 1),
            jnp.where(lane < 48, pltpu.roll(left, 16, 1), pltpu.roll(right, 32, 1)),
        ),
    )
    for rows in (slice(0, 16), slice(16, 32), slice(32, 40)):
        x = [x_ref[i].astype(f32)[rows] for i in range(members)]
        total = [None] * members
        for i in range(members):
            for j in range(i + 1, members):
                s = slope(x[i] - x[j])
                total[i] = s if total[i] is None else total[i] + s
                total[j] = -s if total[j] is None else total[j] - s
        aim = halo if rows.start == 32 else target_ref[me, rows, :]
        for i in range(members):
            value = slope(x[i] - aim) - pair_weight / (members - 1) * total[i]
            value_ref[i, rows, :] = value / cells_all
    for i in range(members):
        out_ref[i] = value_ref[i].astype(bf16)
    forecast_copy.wait()


def tap_sum(value):
    return jnp.sum(value.reshape(16, 8, 128), axis=0)


def backward_kernel(
    cot_ref, xs_ref, first_ref, gate_ref, hidden_ref, edge_first_ref, edge_gate_ref, edge_hidden_ref,
    second_ref, one_ref, two_ref, taps_two_ref,
    out_ref,
    cf_ref, bs_ref, sums_ref, cot_sum_ref, point_two_ref, point_one_ref, other_ref,
):
    for o in range(16):
        cf_ref[chunk_pitch * o : chunk_pitch * o + chunk, :] = cot_ref[o].astype(f32)
    two = two_ref[...]
    one = one_ref[...]
    sums_ref[...] = jnp.zeros(sums_ref.shape, f32)
    cot_sum_ref[...] = jnp.zeros(cot_sum_ref.shape, f32)
    point_two_ref[...] = jnp.zeros(point_two_ref.shape, f32)
    point_one_ref[...] = jnp.zeros(point_one_ref.shape, f32)
    other_ref[...] = jnp.zeros(other_ref.shape, f32)

    parts = []
    for p in range(slabs):
        cot = jnp.concatenate(
            [
                cf_ref[pl.ds(p, 16, stride=chunk_pitch), :],
                cf_ref[pl.ds(16 + p, 16, stride=chunk_pitch), :],
            ],
            axis=0,
        )
        cot_sum_ref[0:32] += cot
        parts.append(cot.astype(bf16))
    for p in range(slabs):
        bs_ref[p + 1, own : own + 128, :] = rounded(dot(parts[p], two, 0, 0))
    cot = jnp.concatenate(parts, axis=1)
    point_two_ref[...] = dot(cot, second_ref[...].reshape(128 * slabs, 128), 1, 0)
    halo = cf_ref[pl.ds(32, 16, stride=chunk_pitch), :]
    halo = jnp.concatenate([halo, pltpu.roll(halo, 96, 1)], axis=0).astype(bf16)
    halo = rounded(dot(halo, two, 0, 0))
    for p in range(slabs):
        bs_ref[p + 1, 15:16, :] = halo[p : p + 1]
        bs_ref[p + 1, 144:145, :] = halo[16 + p : 17 + p]
    wrap_slabs(bs_ref)

    def body(p):
        total = None
        hidden = with_edges(hidden_ref[p], edge_hidden_ref[p])
        for a in range(3):
            for b in range(3):
                t = 3 * a + b
                back = bs_ref[p + 2 - a, 17 - b : 145 - b, :]
                term = taps_two_ref[t : t + 1, :] * back
                total = term if total is None else total + term
                sums_ref[9 + t] += tap_sum(back * hidden)
        back_pre = (total * with_edges(gate_ref[p], edge_gate_ref[p])).astype(bf16)
        sums_ref[18] += tap_sum(back_pre.astype(f32))
        first = with_edges(first_ref[p], edge_first_ref[p]).astype(bf16)
        point_one_ref[...] += dot(back_pre, first, 0, 0)
        back_first = dot(back_pre, one, 1, 0)
        for a in range(3):
            for b in range(3):
                sums_ref[3 * a + b] += tap_sum(back_first * xs_ref[p + a, 15 + b : 143 + b, :])

    each_slab(body)
    for t in range(19):
        total = jnp.sum(sums_ref[t], axis=0, keepdims=True)
        other_ref[t : t + 1, :] = total + pltpu.roll(total, 64, 1)
    other_ref[24:40, :] = pltpu.roll(point_two_ref[0:16], 64, 1) + point_two_ref[16:32]
    bias_two = jnp.sum(cot_sum_ref[...].T, axis=0, keepdims=True)
    bias_two = bias_two + pltpu.roll(bias_two, 112, 1)
    other_ref[19:20, :] = pltpu.roll(bias_two, 64, 1)
    point_one = point_one_ref[0:64] + pltpu.roll(point_one_ref[64:128], 64, 1)
    packed = jnp.where(lanes_of((64, 128)) < 64, point_one, other_ref[...])
    out_ref[...] = packed.reshape(out_ref.shape)


def output_kernel(total_ref, depth_one_ref, point_one_ref, bias_one_ref, depth_two_ref, point_two_ref, bias_two_ref, rows_ref):
    rows_ref[...] = total_ref[...].reshape(64, 128)
    point_one_ref[...] = rows_ref[:, 0:64]
    depth_one_ref[...] = rows_ref[0:9, 64:128]
    depth_two_ref[...] = rows_ref[9:18, 64:128]
    bias_one_ref[...] = rows_ref[18:19, 64:128]
    bias_two_ref[...] = rows_ref[19:20, 64:80]
    point_two_ref[...] = rows_ref[24:40, 64:128]


def call(kernel, out_shape, scratch, flops, fetched=0, passed=0, **out):
    hbm = pl.BlockSpec(memory_space=pltpu.HBM)
    vmem = pl.BlockSpec(memory_space=pltpu.VMEM)
    return pl.pallas_call(
        kernel,
        out_shape=out_shape,
        in_specs=[hbm] * fetched + [vmem] * passed,
        scratch_shapes=scratch,
        **out,
        compiler_params=pltpu.CompilerParams(vmem_limit_bytes=24 * 1024 * 1024),
        cost_estimate=pl.CostEstimate(flops=flops, bytes_accessed=4 << 20, transcendentals=0),
    )


def in_hbm(*arrays):
    return [pltpu.with_memory_space_constraint(array, pltpu.HBM) for array in arrays]


def shape(dims, dtype):
    return jax.ShapeDtypeStruct(dims, dtype)


def local(predictor_inputs, target, depth_one, point_one, bias_one, depth_two, point_two, bias_two):
    members = lax.axis_size("member")
    tiles = lax.axis_size("tile")
    _, chans, rows, cols = predictor_inputs.shape
    slab = (slabs, cols, 128)
    xt, outer, inner, *weights = call(
        edge_kernel,
        (
            shape(slab, f32),
            shape((edge_rows, 128), f32),
            shape((edge_rows, 128), f32),
            shape((9, 64), f32),
            shape((64, 64), bf16),
            shape((1, 64), f32),
            shape((9, 64), f32),
            shape((16, 64), bf16),
            shape((1, 16), f32),
        ),
        [
            pltpu.VMEM((chans, rows, cols), bf16),
            pltpu.VMEM((16, rows, cols), f32),
            pltpu.VMEM((chans * lat_pitch + 32, 128), f32),
            pltpu.VMEM((edge_rows, 128), f32),
            pltpu.VMEM((edge_rows, 128), f32),
            pltpu.SemaphoreType.DMA((8,)),
        ],
        1 << 20,
        fetched=8,
    )(
        *in_hbm(
            predictor_inputs, target, depth_one.T, point_one, bias_one[None], depth_two.T, point_two,
            bias_two[None],
        )
    )
    outer = lax.ppermute(outer, "tile", [(i, (i + 2 * (i % 2) - 1) % tiles) for i in range(tiles)])
    inner = lax.ppermute(inner, "tile", [(i, i + 1 - 2 * (i % 2)) for i in range(tiles)])
    (
        taps_one, one, one_turned, bias_one, taps_two, two, bias_two,
        first, gate, hidden, main_second,
    ) = call(
        main_kernel,
        (
            shape((16, 128), f32),
            shape((128, 128), bf16),
            shape((128, 128), bf16),
            shape((8, 128), f32),
            shape((16, 128), f32),
            shape((32, 128), bf16),
            shape((32, 128), f32),
            shape((slabs, 112, 128), f32),
            shape((slabs, 112, 128), f32),
            shape((slabs, 112, 128), f32),
            shape((slabs, 96, 128), bf16),
        ),
        [
            pltpu.VMEM((128, 128), f32),
            pltpu.VMEM((slabs + 2, cols, 128), f32),
            pltpu.VMEM((slabs + 2, 112, 128), f32),
        ],
        1 << 28,
        passed=7,
    )(*weights, xt)
    edge = (slabs, 16, 128)
    send, xs, edge_first, edge_gate, edge_hidden, second = call(
        halo_kernel,
        (
            shape((16, chunk, 128), bf16),
            shape((slabs + 2, pitch, 128), f32),
            shape(edge, f32),
            shape(edge, f32),
            shape(edge, f32),
            shape(slab, bf16),
        ),
        [
            pltpu.VMEM((slabs + 2, 80, 128), f32),
            pltpu.VMEM((16 * chunk_pitch + 40, 128), f32),
            pltpu.VMEM((128, 128), f32),
            pltpu.VMEM((edge_rows, 128), f32),
            pltpu.VMEM((edge_rows, 128), f32),
        ],
        1 << 27,
        passed=11,
    )(
        xt, outer, inner, hidden, main_second, taps_one, one_turned, bias_one, taps_two, two, bias_two
    )
    seen = lax.all_to_all(send, "member", 0, 0, tiled=True)
    cot, out = call(
        functools.partial(crps_kernel, rows * cols * tiles),
        (shape((members, chunk, 128), bf16), shape((1, 16, rows, cols), bf16)),
        [pltpu.VMEM((members, chunk, 128), f32), pltpu.SemaphoreType.DMA],
        1 << 24,
        passed=5,
        out_specs=(pl.BlockSpec(memory_space=pltpu.VMEM), pl.BlockSpec(memory_space=pltpu.HBM)),
    )(seen, target, outer, inner, send)
    cot = lax.all_to_all(cot, "member", 0, 0, tiled=True)
    packed = call(
        backward_kernel,
        shape((16, 4, 128), f32),
        [
            pltpu.VMEM((16 * chunk_pitch + 40, 128), f32),
            pltpu.VMEM((slabs + 2, pitch, 128), f32),
            pltpu.VMEM((19, 8, 128), f32),
            pltpu.VMEM((128, 128), f32),
            pltpu.VMEM((32, 128), f32),
            pltpu.VMEM((128, 128), f32),
            pltpu.VMEM((64, 128), f32),
        ],
        1 << 28,
        passed=12,
    )(
        cot, xs, first, gate, hidden, edge_first, edge_gate, edge_hidden, second, one, two, taps_two
    )
    axes = ("member", "tile")
    near = [
        [16 * (2 * (2 * y + x_hi) + x_lo) + 2 * z + core for core in range(2) for z in range(8)]
        for x_hi in range(2)
        for x_lo in range(2)
        for y in range(8)
    ]
    far = [list(group) for group in zip(*near)]
    part = lax.all_to_all(packed, axes, 0, 0, tiled=True, axis_index_groups=near)
    part = jnp.sum(part, axis=0)
    part = jnp.broadcast_to(part[None], (len(near),) + part.shape)
    part = lax.all_to_all(part, axes, 0, 0, tiled=True, axis_index_groups=far)
    part = jnp.sum(part, axis=0)
    part = jnp.broadcast_to(part[None], (len(far),) + part.shape)
    total = lax.all_to_all(part, axes, 0, 0, tiled=True, axis_index_groups=near)
    g_depth_one, g_point_one, g_bias_one, g_depth_two, g_point_two, g_bias_two = call(
        output_kernel,
        (
            shape((9, 64), f32),
            shape((64, 64), f32),
            shape((1, 64), f32),
            shape((9, 64), f32),
            shape((16, 64), f32),
            shape((1, 16), f32),
        ),
        [pltpu.VMEM((64, 128), f32)],
        1 << 20,
        passed=1,
    )(total)
    return (
        out,
        g_depth_one.T,
        g_point_one,
        g_bias_one[0],
        g_depth_two.T,
        g_point_two,
        g_bias_two[0],
    )


def solution(mesh):
    return jax.shard_map(
        local,
        mesh=mesh,
        in_specs=(
            P("member", None, None, "tile"),
            P(None, None, "tile"),
            P(),
            P(),
            P(),
            P(),
            P(),
            P(),
        ),
        out_specs=(P("member", None, None, "tile"), P(), P(), P(), P(), P(), P()),
        check_vma=False,
    )
```

```python
import functools

import jax
import jax.numpy as jnp
from jax import lax
from jax.experimental import pallas as pl
from jax.experimental.pallas import tpu as pltpu
from jax.sharding import PartitionSpec as P

smooth_width = 0.25
pair_weight = 0.95

slabs = 16
pitch = 160
own = 16
chunk = 40
chunk_pitch = 50
lat_pitch = 34
edge_rows = 56

f32 = jnp.float32
bf16 = jnp.bfloat16


def lanes_of(shape):
    return lax.broadcasted_iota(jnp.int32, shape, len(shape) - 1)


def dot(left, right, left_dim, right_dim):
    return lax.dot_general(
        left, right, (((left_dim,), (right_dim,)), ((), ())), preferred_element_type=f32
    )


def rounded(value):
    return value.astype(bf16).astype(f32)


def wrap_slabs(ref):
    last = pltpu.roll(ref[slabs], 64, 1)
    ref[0] = jnp.where(lanes_of(last.shape) >= 64, last, 0.0)
    first = pltpu.roll(ref[1], 64, 1)
    ref[slabs + 1] = jnp.where(lanes_of(first.shape) < 64, first, 0.0)


def both_halves(row):
    return jnp.concatenate([row, row], axis=1)


def each_slab(body):
    for p in range(slabs):
        body(p)


def in_turn(make, ref, use):
    for p in (0, slabs - 1, 1):
        make(p)
    wrap_slabs(ref)
    for p in range(slabs):
        if p + 2 < slabs - 1:
            make(p + 2)
        use(p)


def fetch(sources, places, sems):
    copies = [
        pltpu.make_async_copy(source, place, sems.at[k])
        for k, (source, place) in enumerate(zip(sources, places))
    ]
    for copy in copies:
        copy.start()
    return copies


def even_tile():
    return lax.rem(lax.axis_index("tile"), 2) == 0


def edge_kernel(
    x_hbm, target_hbm, depth_one_hbm, point_one_hbm, bias_one_hbm, depth_two_hbm, point_two_hbm,
    bias_two_hbm,
    xt_ref, outer_ref, inner_ref, d1_ref, p1_ref, b1_ref, d2_ref, p2_ref, b2_ref,
    x_ref, target_ref, rows_scr, first_ref, last_ref, sems,
):
    sources = (
        target_hbm, x_hbm.at[0], depth_one_hbm, point_one_hbm, bias_one_hbm, depth_two_hbm,
        point_two_hbm, bias_two_hbm,
    )
    places = (target_ref, x_ref, d1_ref, p1_ref, b1_ref, d2_ref, p2_ref, b2_ref)
    target_copy, x_copy, *weight_copies = fetch(sources, places, sems)
    target_copy.wait()
    for k in range(4):
        turned = target_ref[4 * k : 4 * k + 4].reshape(128, 128).T
        first_ref[48 + k : 49 + k, :] = turned[0:1]
        last_ref[48 + k : 49 + k, :] = turned[127:128]
    first_ref[52:56, :] = jnp.zeros((4, 128), f32)
    last_ref[52:56, :] = jnp.zeros((4, 128), f32)
    x_copy.wait()
    for c in range(64):
        rows_scr[lat_pitch * c : lat_pitch * c + 32, :] = x_ref[c].astype(f32)

    def body(p):
        here = jnp.concatenate(
            [rows_scr[pl.ds(p, 64, stride=lat_pitch), :], rows_scr[pl.ds(p + 16, 64, stride=lat_pitch), :]],
            axis=0,
        )
        turned = here.T
        xt_ref[p] = turned
        for j in range(3):
            first_ref[pl.ds(16 * j + p, 1), :] = turned[j : j + 1]
            last_ref[pl.ds(16 * j + p, 1), :] = turned[125 + j : 126 + j]

    each_slab(body)
    even = even_tile()
    first, last = first_ref[...], last_ref[...]
    outer_ref[...] = jnp.where(even, first, last)
    inner_ref[...] = jnp.where(even, last, first)
    for copy in weight_copies:
        copy.wait()


def main_kernel(
    d1_ref, p1_ref, b1_ref, d2_ref, p2_ref, b2_ref, xt_ref,
    taps_one_ref, one_ref, one_turned_ref, bias_one_ref, taps_two_ref, two_ref, bias_two_ref,
    first_ref, gate_ref, hidden_ref, second_ref,
    turn_ref, xs_ref, hs_ref,
):
    turn_ref[...] = jnp.zeros((128, 128), f32)
    for p in range(slabs):
        xs_ref[p + 1] = xt_ref[p]
    wrap_slabs(xs_ref)
    zero = jnp.zeros((7, 128), f32)
    taps_one_ref[...] = jnp.concatenate([both_halves(d1_ref[...]), zero], axis=0)
    taps_two_ref[...] = jnp.concatenate([both_halves(d2_ref[...]), zero], axis=0)
    bias_one_ref[...] = jnp.broadcast_to(both_halves(b1_ref[...]), (8, 128))
    turn_ref[0:1, 0:16] = b2_ref[...]
    column = jnp.broadcast_to(turn_ref[...].T[0:16, 0:1], (16, 128))
    bias_two_ref[0:16] = column
    bias_two_ref[16:32] = column
    turn_ref[0:1, :] = jnp.zeros((1, 128), f32)
    weight = p1_ref[...].astype(f32)
    turn_ref[0:64, 0:64] = weight
    turn_ref[64:128, 64:128] = weight
    one_ref[...] = turn_ref[...].astype(bf16)
    one_turned = turn_ref[...].T.astype(bf16)
    one_turned_ref[...] = one_turned
    weight = p2_ref[...].astype(f32)
    zero = jnp.zeros((16, 64), f32)
    two_ref[...] = jnp.concatenate(
        [jnp.concatenate([weight, zero], axis=1), jnp.concatenate([zero, weight], axis=1)], axis=0
    ).astype(bf16)

    def first_body(p):
        first = rounded(depthwise(taps_one_ref, xs_ref, p, 7, 112))
        first_ref[p] = first
        hidden, gate = activation(first, one_turned, bias_one_ref)
        hidden_ref[p] = hidden
        hs_ref[p + 1] = hidden
        gate_ref[p] = gate

    def second_body(p):
        second_ref[p] = depthwise(taps_two_ref, hs_ref, p, 7, 96).astype(bf16)

    in_turn(first_body, hs_ref, second_body)


def depthwise(taps_ref, ref, p, row, count):
    total = None
    for a in range(3):
        for b in range(3):
            tap = taps_ref[3 * a + b : 3 * a + b + 1, :]
            term = tap * ref[p + a, row + b : row + b + count, :]
            total = term if total is None else total + term
    return total


def activation(first, one_turned, bias_ref):
    pre = dot(first.astype(bf16), one_turned, 1, 0) + bias_ref[0:1]
    gate = 1.0 / (1.0 + jnp.exp(-pre))
    return rounded(pre * gate), gate * (1.0 + pre * (1.0 - gate))


def with_edges(main, edge):
    return jnp.concatenate([edge[0:8], main, edge[8:16]], axis=0)


def halo_kernel(
    xt_ref, outer_ref, inner_ref, hidden_ref, main_second_ref,
    taps_one_ref, one_turned_ref, bias_one_ref, taps_two_ref, two_ref, bias_ref,
    send_ref, xs_ref, first_ref, gate_ref, edge_hidden_ref, second_ref,
    hs_ref, y_ref, edge_ref, left_ref, right_ref,
):
    two = two_ref[...]
    even = even_tile()
    outer, inner = outer_ref[...], inner_ref[...]
    left_ref[...] = jnp.where(even, outer, inner)
    right_ref[...] = jnp.where(even, inner, outer)

    for k in range(slabs + 2):
        xs_ref[k, 0:16, :] = jnp.zeros((16, 128), f32)
        xs_ref[k, 144:160, :] = jnp.zeros((16, 128), f32)
    for p in range(slabs):
        xs_ref[p + 1, own : own + 128, :] = xt_ref[p]
        for j in range(3):
            xs_ref[p + 1, 13 + j : 14 + j, :] = left_ref[16 * j + p : 16 * j + p + 1, :]
            xs_ref[p + 1, 144 + j : 145 + j, :] = right_ref[16 * j + p : 16 * j + p + 1, :]
    wrap_slabs(xs_ref)

    one_turned = one_turned_ref[...]
    for k in range(0, slabs, 8):
        first = [
            depthwise(taps_one_ref, xs_ref, p, row, 16) for p in range(k, k + 8) for row in (7, 135)
        ]
        first = rounded(jnp.concatenate(first, axis=0))
        hidden, gate = activation(first, one_turned, bias_one_ref)
        for p in range(k, k + 8):
            at = 32 * (p - k)
            rows = slice(at + 8, at + 24)
            first_ref[p] = first[rows]
            gate_ref[p] = gate[rows]
            edge_hidden_ref[p] = hidden[rows]
            hs_ref[p + 1, 0:8, :] = jnp.zeros((8, 128), f32)
            hs_ref[p + 1, 8:24, :] = hidden[at : at + 16]
            hs_ref[p + 1, 24:40, :] = hidden_ref[p, 0:16, :]
            hs_ref[p + 1, 40:56, :] = hidden_ref[p, 96:112, :]
            hs_ref[p + 1, 56:72, :] = hidden[at + 16 : at + 32]
            hs_ref[p + 1, 72:80, :] = jnp.zeros((8, 128), f32)
    wrap_slabs(hs_ref)
    y_ref[...] = jnp.zeros(y_ref.shape, f32)
    edge_ref[...] = jnp.zeros(edge_ref.shape, f32)

    def second_body(p):
        before = depthwise(taps_two_ref, hs_ref, p, 7, 24)
        after = depthwise(taps_two_ref, hs_ref, p, 47, 24)
        edge_ref[pl.ds(p, 1), :] = before[7:8]
        edge_ref[pl.ds(16 + p, 1), :] = after[16:17]
        second = jnp.concatenate(
            [before[8:24].astype(bf16), main_second_ref[p], after[0:16].astype(bf16)], axis=0
        )
        second_ref[p] = second
        y = dot(two, second, 1, 1) + bias_ref[...]
        y_ref[pl.ds(p, 16, stride=chunk_pitch), :] = y[0:16]
        y_ref[pl.ds(16 + p, 16, stride=chunk_pitch), :] = y[16:32]

    each_slab(second_body)
    y = dot(two, edge_ref[...].astype(bf16), 1, 1) + bias_ref[...]
    lane = lanes_of((16, 128))
    y = jnp.where(lane < 32, y[0:16], jnp.where(lane < 64, pltpu.roll(y[16:32], 32, 1), 0.0))
    y_ref[pl.ds(32, 16, stride=chunk_pitch), :] = y
    for o in range(16):
        send_ref[o] = y_ref[chunk_pitch * o : chunk_pitch * o + chunk, :].astype(bf16)


def slope(diff):
    return diff * lax.rsqrt(diff * diff + smooth_width * smooth_width)


def crps_kernel(
    cells_all, x_ref, target_ref, outer_ref, inner_ref, send_ref, out_ref, forecast_hbm,
    value_ref, sem,
):
    forecast_copy = pltpu.make_async_copy(send_ref.at[:, 0:32], forecast_hbm.at[0], sem)
    forecast_copy.start()
    members = x_ref.shape[0]
    me = lax.axis_index("member")
    me = lax.rem(me, 2) * (members // 2) + me // 2
    turn = lax.rem(4 - lax.rem(me, 4), 4) * 32
    even = even_tile()
    outer = outer_ref[pl.ds(48 + me // 4, 1), :]
    inner = inner_ref[pl.ds(48 + me // 4, 1), :]
    left = jnp.where(even, outer, inner)
    right = jnp.where(even, inner, outer)
    left = pltpu.roll(jnp.broadcast_to(left, (8, 128)), turn, 1)
    right = pltpu.roll(jnp.broadcast_to(right, (8, 128)), turn, 1)
    lane = lanes_of((8, 128))
    halo = jnp.where(
        lane < 16,
        left,
        jnp.where(
            lane < 32,
            pltpu.roll(right, 16, 1),
            jnp.where(lane < 48, pltpu.roll(left, 16, 1), pltpu.roll(right, 32, 1)),
        ),
    )
    for rows in (slice(0, 16), slice(16, 32), slice(32, 40)):
        x = [x_ref[i].astype(f32)[rows] for i in range(members)]
        total = [None] * members
        for i in range(members):
            for j in range(i + 1, members):
                s = slope(x[i] - x[j])
                total[i] = s if total[i] is None else total[i] + s
                total[j] = -s if total[j] is None else total[j] - s
        aim = halo if rows.start == 32 else target_ref[me, rows, :]
        for i in range(members):
            value = slope(x[i] - aim) - pair_weight / (members - 1) * total[i]
            value_ref[i, rows, :] = value / cells_all
    for i in range(members):
        out_ref[i] = value_ref[i].astype(bf16)
    forecast_copy.wait()


def tap_sum(value):
    return jnp.sum(value.reshape(16, 8, 128), axis=0)


def backward_kernel(
    cot_ref, xs_ref, first_ref, gate_ref, hidden_ref, edge_first_ref, edge_gate_ref, edge_hidden_ref,
    second_ref, one_ref, two_ref, taps_two_ref,
    out_ref,
    cf_ref, bs_ref, sums_ref, cot_sum_ref, point_two_ref, point_one_ref, other_ref,
):
    for o in range(16):
        cf_ref[chunk_pitch * o : chunk_pitch * o + chunk, :] = cot_ref[o].astype(f32)
    two = two_ref[...]
    one = one_ref[...]
    sums_ref[...] = jnp.zeros(sums_ref.shape, f32)
    cot_sum_ref[...] = jnp.zeros(cot_sum_ref.shape, f32)
    point_two_ref[...] = jnp.zeros(point_two_ref.shape, f32)
    point_one_ref[...] = jnp.zeros(point_one_ref.shape, f32)
    other_ref[...] = jnp.zeros(other_ref.shape, f32)

    parts = []
    for p in range(slabs):
        cot = jnp.concatenate(
            [
                cf_ref[pl.ds(p, 16, stride=chunk_pitch), :],
                cf_ref[pl.ds(16 + p, 16, stride=chunk_pitch), :],
            ],
            axis=0,
        )
        cot_sum_ref[0:32] += cot
        parts.append(cot.astype(bf16))
    for p in range(slabs):
        bs_ref[p + 1, own : own + 128, :] = rounded(dot(parts[p], two, 0, 0))
    cot = jnp.concatenate(parts, axis=1)
    point_two_ref[...] = dot(cot, second_ref[...].reshape(128 * slabs, 128), 1, 0)
    halo = cf_ref[pl.ds(32, 16, stride=chunk_pitch), :]
    halo = jnp.concatenate([halo, pltpu.roll(halo, 96, 1)], axis=0).astype(bf16)
    halo = rounded(dot(halo, two, 0, 0))
    for p in range(slabs):
        bs_ref[p + 1, 15:16, :] = halo[p : p + 1]
        bs_ref[p + 1, 144:145, :] = halo[16 + p : 17 + p]
    wrap_slabs(bs_ref)

    def body(p):
        total = None
        hidden = with_edges(hidden_ref[p], edge_hidden_ref[p])
        for a in range(3):
            for b in range(3):
                t = 3 * a + b
                back = bs_ref[p + 2 - a, 17 - b : 145 - b, :]
                term = taps_two_ref[t : t + 1, :] * back
                total = term if total is None else total + term
                sums_ref[9 + t] += tap_sum(back * hidden)
        back_pre = (total * with_edges(gate_ref[p], edge_gate_ref[p])).astype(bf16)
        sums_ref[18] += tap_sum(back_pre.astype(f32))
        first = with_edges(first_ref[p], edge_first_ref[p]).astype(bf16)
        point_one_ref[...] += dot(back_pre, first, 0, 0)
        back_first = dot(back_pre, one, 1, 0)
        for a in range(3):
            for b in range(3):
                sums_ref[3 * a + b] += tap_sum(back_first * xs_ref[p + a, 15 + b : 143 + b, :])

    each_slab(body)
    for t in range(19):
        total = jnp.sum(sums_ref[t], axis=0, keepdims=True)
        other_ref[t : t + 1, :] = total + pltpu.roll(total, 64, 1)
    other_ref[24:40, :] = pltpu.roll(point_two_ref[0:16], 64, 1) + point_two_ref[16:32]
    bias_two = jnp.sum(cot_sum_ref[...].T, axis=0, keepdims=True)
    bias_two = bias_two + pltpu.roll(bias_two, 112, 1)
    other_ref[19:20, :] = pltpu.roll(bias_two, 64, 1)
    point_one = point_one_ref[0:64] + pltpu.roll(point_one_ref[64:128], 64, 1)
    packed = jnp.where(lanes_of((64, 128)) < 64, point_one, other_ref[...])
    out_ref[...] = packed.reshape(out_ref.shape)


def output_kernel(total_ref, depth_one_ref, point_one_ref, bias_one_ref, depth_two_ref, point_two_ref, bias_two_ref, rows_ref):
    rows_ref[...] = total_ref[...].reshape(64, 128)
    point_one_ref[...] = rows_ref[:, 0:64]
    depth_one_ref[...] = rows_ref[0:9, 64:128]
    depth_two_ref[...] = rows_ref[9:18, 64:128]
    bias_one_ref[...] = rows_ref[18:19, 64:128]
    bias_two_ref[...] = rows_ref[19:20, 64:80]
    point_two_ref[...] = rows_ref[24:40, 64:128]


def call(kernel, out_shape, scratch, flops, fetched=0, passed=0, **out):
    hbm = pl.BlockSpec(memory_space=pltpu.HBM)
    vmem = pl.BlockSpec(memory_space=pltpu.VMEM)
    return pl.pallas_call(
        kernel,
        out_shape=out_shape,
        in_specs=[hbm] * fetched + [vmem] * passed,
        scratch_shapes=scratch,
        **out,
        compiler_params=pltpu.CompilerParams(vmem_limit_bytes=24 * 1024 * 1024),
        cost_estimate=pl.CostEstimate(flops=flops, bytes_accessed=4 << 20, transcendentals=0),
    )


def in_hbm(*arrays):
    return [pltpu.with_memory_space_constraint(array, pltpu.HBM) for array in arrays]


def shape(dims, dtype):
    return jax.ShapeDtypeStruct(dims, dtype)


def local(predictor_inputs, target, depth_one, point_one, bias_one, depth_two, point_two, bias_two):
    members = lax.axis_size("member")
    tiles = lax.axis_size("tile")
    _, chans, rows, cols = predictor_inputs.shape
    slab = (slabs, cols, 128)
    xt, outer, inner, *weights = call(
        edge_kernel,
        (
            shape(slab, f32),
            shape((edge_rows, 128), f32),
            shape((edge_rows, 128), f32),
            shape((9, 64), f32),
            shape((64, 64), bf16),
            shape((1, 64), f32),
            shape((9, 64), f32),
            shape((16, 64), bf16),
            shape((1, 16), f32),
        ),
        [
            pltpu.VMEM((chans, rows, cols), bf16),
            pltpu.VMEM((16, rows, cols), f32),
            pltpu.VMEM((chans * lat_pitch + 32, 128), f32),
            pltpu.VMEM((edge_rows, 128), f32),
            pltpu.VMEM((edge_rows, 128), f32),
            pltpu.SemaphoreType.DMA((8,)),
        ],
        1 << 20,
        fetched=8,
    )(
        *in_hbm(
            predictor_inputs, target, depth_one.T, point_one, bias_one[None], depth_two.T, point_two,
            bias_two[None],
        )
    )
    outer = lax.ppermute(outer, "tile", [(i, (i + 2 * (i % 2) - 1) % tiles) for i in range(tiles)])
    inner = lax.ppermute(inner, "tile", [(i, i + 1 - 2 * (i % 2)) for i in range(tiles)])
    (
        taps_one, one, one_turned, bias_one, taps_two, two, bias_two,
        first, gate, hidden, main_second,
    ) = call(
        main_kernel,
        (
            shape((16, 128), f32),
            shape((128, 128), bf16),
            shape((128, 128), bf16),
            shape((8, 128), f32),
            shape((16, 128), f32),
            shape((32, 128), bf16),
            shape((32, 128), f32),
            shape((slabs, 112, 128), f32),
            shape((slabs, 112, 128), f32),
            shape((slabs, 112, 128), f32),
            shape((slabs, 96, 128), bf16),
        ),
        [
            pltpu.VMEM((128, 128), f32),
            pltpu.VMEM((slabs + 2, cols, 128), f32),
            pltpu.VMEM((slabs + 2, 112, 128), f32),
        ],
        1 << 28,
        passed=7,
    )(*weights, xt)
    edge = (slabs, 16, 128)
    send, xs, edge_first, edge_gate, edge_hidden, second = call(
        halo_kernel,
        (
            shape((16, chunk, 128), bf16),
            shape((slabs + 2, pitch, 128), f32),
            shape(edge, f32),
            shape(edge, f32),
            shape(edge, f32),
            shape(slab, bf16),
        ),
        [
            pltpu.VMEM((slabs + 2, 80, 128), f32),
            pltpu.VMEM((16 * chunk_pitch + 40, 128), f32),
            pltpu.VMEM((128, 128), f32),
            pltpu.VMEM((edge_rows, 128), f32),
            pltpu.VMEM((edge_rows, 128), f32),
        ],
        1 << 27,
        passed=11,
    )(
        xt, outer, inner, hidden, main_second, taps_one, one_turned, bias_one, taps_two, two, bias_two
    )
    axes = ("member", "tile")
    ring = [
        [tiles * (2 * y + x_hi) + t for x_hi in range(2) for y in range(members // 2)]
        for t in range(tiles)
    ]
    seen = lax.all_to_all(send, axes, 0, 0, tiled=True, axis_index_groups=ring)
    cot, out = call(
        functools.partial(crps_kernel, rows * cols * tiles),
        (shape((members, chunk, 128), bf16), shape((1, 16, rows, cols), bf16)),
        [pltpu.VMEM((members, chunk, 128), f32), pltpu.SemaphoreType.DMA],
        1 << 24,
        passed=5,
        out_specs=(pl.BlockSpec(memory_space=pltpu.VMEM), pl.BlockSpec(memory_space=pltpu.HBM)),
    )(seen, target, outer, inner, send)
    cot = lax.all_to_all(cot, axes, 0, 0, tiled=True, axis_index_groups=ring)
    packed = call(
        backward_kernel,
        shape((16, 4, 128), f32),
        [
            pltpu.VMEM((16 * chunk_pitch + 40, 128), f32),
            pltpu.VMEM((slabs + 2, pitch, 128), f32),
            pltpu.VMEM((19, 8, 128), f32),
            pltpu.VMEM((128, 128), f32),
            pltpu.VMEM((32, 128), f32),
            pltpu.VMEM((128, 128), f32),
            pltpu.VMEM((64, 128), f32),
        ],
        1 << 28,
        passed=12,
    )(
        cot, xs, first, gate, hidden, edge_first, edge_gate, edge_hidden, second, one, two, taps_two
    )
    near = [
        [16 * (2 * (2 * y + x_hi) + x_lo) + 2 * z + core for core in range(2) for z in range(8)]
        for x_hi in range(2)
        for x_lo in range(2)
        for y in range(8)
    ]
    far = [list(group) for group in zip(*near)]
    part = lax.all_to_all(packed, axes, 0, 0, tiled=True, axis_index_groups=near)
    part = jnp.sum(part, axis=0)
    part = jnp.broadcast_to(part[None], (len(near),) + part.shape)
    part = lax.all_to_all(part, axes, 0, 0, tiled=True, axis_index_groups=far)
    part = jnp.sum(part, axis=0)
    part = jnp.broadcast_to(part[None], (len(far),) + part.shape)
    total = lax.all_to_all(part, axes, 0, 0, tiled=True, axis_index_groups=near)
    g_depth_one, g_point_one, g_bias_one, g_depth_two, g_point_two, g_bias_two = call(
        output_kernel,
        (
            shape((9, 64), f32),
            shape((64, 64), f32),
            shape((1, 64), f32),
            shape((9, 64), f32),
            shape((16, 64), f32),
            shape((1, 16), f32),
        ),
        [pltpu.VMEM((64, 128), f32)],
        1 << 20,
        passed=1,
    )(total)
    return (
        out,
        g_depth_one.T,
        g_point_one,
        g_bias_one[0],
        g_depth_two.T,
        g_point_two,
        g_bias_two[0],
    )


def solution(mesh):
    return jax.shard_map(
        local,
        mesh=mesh,
        in_specs=(
            P("member", None, None, "tile"),
            P(None, None, "tile"),
            P(),
            P(),
            P(),
            P(),
            P(),
            P(),
        ),
        out_specs=(P("member", None, None, "tile"), P(), P(), P(), P(), P(), P()),
        check_vma=False,
    )
```
